128 devices in a mesh: dp: 2 (over core), wide: 16 (over x, y), narrow: 4 (over z).
Axes of the slice: x: 4, y: 4, z: 4, core: 2. Of those that a mesh axis runs over, the one named last changes fastest.
Arguments:
- hidden_in: bfloat16 [6, 2048, 768], P('dp', 'wide'), may hold values from -6 to 6
- segments: int32 [6, 2048], P('dp', 'wide'), may hold values from 0 to 4, as said below
- weight_query: bfloat16 [768, 768], P(None, 'narrow'), may hold values from -0.21875 to 0.21875
- bias_query: float32 [768], P('narrow'), may hold values from -3 to 3
- weight_key: bfloat16 [768, 768], P(None, 'narrow'), may hold values from -0.21875 to 0.21875
- bias_key: float32 [768], P('narrow'), may hold values from -3 to 3
- weight_value: bfloat16 [768, 768], P(None, 'narrow'), may hold values from -0.21875 to 0.21875
- bias_value: float32 [768], P('narrow'), may hold values from -1.2 to 1.2
- weight_out: bfloat16 [768, 768], P('narrow'), may hold values from -1 to 1
- bias_out: float32 [768], replicated, may hold values from -3 to 3
- gain_one: float32 [768], replicated, may hold values from 0.5 to 1.5
- shift_one: float32 [768], replicated, may hold values from -3 to 3
- weight_up: bfloat16 [768, 3072], P('wide', 'narrow'), may hold values from -0.21875 to 0.21875
- bias_up: float32 [3072], P('narrow'), may hold values from -3 to 3
- weight_down: bfloat16 [3072, 768], P('narrow', 'wide'), may hold values from -0.109375 to 0.109375
- bias_down: float32 [768], replicated, may hold values from -3 to 3
- gain_two: float32 [768], replicated, may hold values from 0.5 to 1.5
- shift_two: float32 [768], replicated, may hold values from -3 to 3
- cotangent: bfloat16 [6, 2048, 768], P('dp', 'wide'), may hold values from -6 to 6
Outputs:
- layer_out: float32 [6, 2048, 768], P('dp', 'wide')
- grad_input: float32 [6, 2048, 768], P('dp', 'wide')
- grad_weight_query: float32 [768, 768], P(('dp', 'wide'), 'narrow')
- grad_bias_query: float32 [768], P('narrow')
- grad_weight_key: float32 [768, 768], P(('dp', 'wide'), 'narrow')
- grad_bias_key: float32 [768], P('narrow')
- grad_weight_value: float32 [768, 768], P(('dp', 'wide'), 'narrow')
- grad_bias_value: float32 [768], P('narrow')
- grad_weight_out: float32 [768, 768], P('narrow', ('dp', 'wide'))
- grad_bias_out: float32 [768], replicated
- grad_gain_one: float32 [768], replicated
- grad_shift_one: float32 [768], replicated
- grad_weight_up: float32 [768, 3072], P(('dp', 'wide'), 'narrow')
- grad_bias_up: float32 [3072], P('narrow')
- grad_weight_down: float32 [3072, 768], P('narrow', ('dp', 'wide'))
- grad_bias_down: float32 [768], replicated
- grad_gain_two: float32 [768], replicated
- grad_shift_two: float32 [768], replicated
The draws below stay inside these ranges and needn't reach their ends.
Inputs may be any that keep to these rules, and one draw needn't show every extreme that they name: `segments`: along each row the ids start at 0, never fall and rise by at most 1 from one token to the next; a document is a run of equal ids, and every row holds exactly five documents.
All inputs are finite; a program needn't handle non-finite values.
Results may differ from the reference program's by a relative error of at most 0.023.
Values may be sent and summed in bfloat16 or wider, within the bound.
No kernel may reach another device: no remote copies, remote signals or barrier semaphores. Data moves between devices by JAX's collectives and lax.ppermute only.
A program may use at most 128 MiB of HBM per device.

```python
import jax
import jax.numpy as jnp
import numpy as np
from jax import lax

D = 768
HEADS = 12
HD = 64
FF = 3072
ROWS = 3
LW = 128
ROWS_ALL = 6
LROW = 2048


def draw_segments(key, part):
    key = jax.random.fold_in(key, 11)
    key_one, key_two, key_three, key_four, key_pick, key_spread = jax.random.split(key, 6)
    half_width = LW // 2
    cut_one = jax.random.randint(key_one, (ROWS_ALL, 1), 1, half_width)
    cut_two = jax.random.randint(key_two, (ROWS_ALL, 1), half_width, LW)
    cut_three = jax.random.randint(key_three, (ROWS_ALL, 1), LROW - LW, LROW - half_width)
    cut_four = jax.random.randint(key_four, (ROWS_ALL, 1), LROW - half_width, LROW)
    places = jnp.arange(LROW, dtype=jnp.int32)[None, :]
    span_cuts = (places == cut_one) | (places == cut_two) | (places == cut_three) | (places == cut_four)
    row_keys = jax.random.split(key_spread, ROWS_ALL)
    picks = jax.vmap(lambda row_key: jax.random.permutation(row_key, LROW - 1)[:4] + 1)(row_keys)
    free_cuts = jnp.any(places[:, :, None] == picks.astype(jnp.int32)[:, None, :], axis=2)
    group_count = ROWS_ALL // ROWS
    chosen = jax.random.randint(key_pick, (group_count, 1), 0, ROWS)
    row_place = jnp.arange(ROWS, dtype=jnp.int32)[None, :]
    spanning = (row_place == chosen).reshape(ROWS_ALL, 1)
    cuts = jnp.where(spanning, span_cuts, free_cuts)
    return jnp.cumsum(cuts.astype(jnp.int32), axis=1).astype(jnp.int32)


def steps_of(rng, shape, cuts, least, high):
    def one(position, shards_of):
        draws = jax.random.uniform(jax.random.fold_in(jax.random.fold_in(rng, 6), position), (shards_of,), jnp.float32, least / len(cuts), high / len(cuts))
        return jnp.repeat(jnp.exp(draws), shape[position] // shards_of).reshape((-1,) + (1,) * (len(shape) - position - 1))

    level = one(*cuts[0])
    for cut in cuts[1:]:
        level = level * one(*cut)
    return level


def centred(key, extent, width, reach, cuts=(), held_as=jnp.bfloat16):
    level = steps_of(key, extent, cuts, -0.22, 0.18) if cuts else 1.0
    values = jax.random.normal(key, extent, jnp.float32) * width * level
    return jnp.minimum(jnp.maximum(values, -reach), reach).astype(held_as)


def setup_inputs(seed: int = 0) -> dict:
    arg_keys = jax.random.split(jax.random.key(seed), 20)
    hidden_in = centred(arg_keys[0], (ROWS_ALL, LROW, D), 1.0, 6.0, ((0, 2), (1, 16)))
    segments = draw_segments(jax.random.fold_in(arg_keys[19], 71), 0)
    weight_query = centred(arg_keys[2], (D, D), D ** -0.5, 0.21875, ((1, 4),))
    bias_query = centred(arg_keys[3], (D,), 0.5, 3.0, ((0, 4),), jnp.float32)
    weight_key = centred(arg_keys[4], (D, D), D ** -0.5, 0.21875, ((1, 4),))
    bias_key = centred(arg_keys[5], (D,), 0.5, 3.0, ((0, 4),), jnp.float32)
    weight_value = centred(arg_keys[6], (D, D), D ** -0.5, 0.21875, ((1, 4),))
    bias_value = centred(arg_keys[7], (D,), 0.2, 1.2, ((0, 4),), jnp.float32)
    weight_out = centred(arg_keys[8], (D, D), (max(32, 16 * D // LROW)) ** -0.5, 1.0, ((0, 4),))
    bias_out = centred(arg_keys[9], (D,), 0.5, 3.0, (), jnp.float32)
    gain_one = jnp.clip(1.0 + 0.1 * jax.random.normal(arg_keys[10], (D,), jnp.float32), 0.5, 1.5)
    shift_one = centred(arg_keys[11], (D,), 0.5, 3.0, (), jnp.float32)
    weight_up = centred(arg_keys[12], (D, FF), D ** -0.5, 0.21875, ((0, 16), (1, 4)))
    bias_up = centred(arg_keys[13], (FF,), 0.5, 3.0, ((0, 4),), jnp.float32)
    weight_down = centred(arg_keys[14], (FF, D), FF ** -0.5, 0.109375, ((0, 4), (1, 16)))
    bias_down = centred(arg_keys[15], (D,), 0.5, 3.0, (), jnp.float32)
    gain_two = jnp.clip(1.0 + 0.1 * jax.random.normal(arg_keys[16], (D,), jnp.float32), 0.5, 1.5)
    shift_two = centred(arg_keys[17], (D,), 0.5, 3.0, (), jnp.float32)
    cotangent = centred(arg_keys[18], (ROWS_ALL, LROW, D), 1.0, 6.0, ((0, 2), (1, 16)))
    return {"hidden_in": hidden_in, "segments": segments, "weight_query": weight_query, "bias_query": bias_query, "weight_key": weight_key, "bias_key": bias_key, "weight_value": weight_value, "bias_value": bias_value, "weight_out": weight_out, "bias_out": bias_out, "gain_one": gain_one, "shift_one": shift_one, "weight_up": weight_up, "bias_up": bias_up, "weight_down": weight_down, "bias_down": bias_down, "gain_two": gain_two, "shift_two": shift_two, "cotangent": cotangent}


EPSILON = 1e-12
NEG_LARGE = -1e+30

@jax.custom_vjp
def low(v):
    return lax.optimization_barrier(v.astype(jnp.bfloat16)).astype(jnp.float32)

@jax.custom_vjp
def low_back(v):
    return v

def low_keep(v):
    return (low(v), None)

def low_pass(kept, grad):
    return (grad,)

def back_keep(v):
    return (v, None)

def back_low(kept, grad):
    return (low(grad),)
low.defvjp(low_keep, low_pass)
low_back.defvjp(back_keep, back_low)

def layer_norm(residual, gain_vec, shift_vec):
    center = residual - lax.optimization_barrier(jnp.mean(residual, axis=-1, keepdims=True))
    spread = lax.optimization_barrier(jnp.mean(center * center, axis=-1, keepdims=True))
    return center * lax.rsqrt(spread + EPSILON) * gain_vec + shift_vec

def rotary_tables(positions):
    inverse = jnp.asarray(np.power(10000.0, -np.arange(0, HD, 2) / HD), dtype=jnp.float32)
    angles = positions[..., None] * jnp.repeat(inverse, 2)
    return (jnp.cos(angles), jnp.sin(angles))

def pair_swap(tensor):
    paired = tensor.reshape(tensor.shape[:-1] + (tensor.shape[-1] // 2, 2))
    return jnp.stack([-paired[..., 1], paired[..., 0]], axis=-1).reshape(tensor.shape)

def widen(freq_table, tensor):
    repeats = tensor.shape[-1] // freq_table.shape[-1]
    return jnp.tile(freq_table, (1,) * (freq_table.ndim - 1) + (repeats,))

def rotate(tensor, cosine_tab, sine_tab):
    return tensor * widen(cosine_tab, tensor) + pair_swap(tensor) * widen(sine_tab, tensor)

def matmul(left, right):
    return jnp.dot(left, right, precision=lax.Precision.HIGHEST)

def split_heads(tensor):
    return tensor.reshape(ROWS_ALL, LROW, HEADS, HD).transpose(0, 2, 1, 3).reshape(ROWS_ALL * HEADS, LROW, HD)

def merge_heads(tensor):
    return tensor.reshape(ROWS_ALL, HEADS, LROW, HD).transpose(0, 2, 1, 3).reshape(ROWS_ALL, LROW, D)

def head_attention(packed):
    query_head, key_head, value_head, seg_head = packed
    scores = low_back(jnp.dot(query_head, key_head.T, precision=lax.Precision.HIGHEST))
    allowed = seg_head[:, None] == seg_head[None, :]
    prob_full = jax.nn.softmax(jnp.where(allowed, scores, NEG_LARGE), axis=-1)
    return jnp.dot(low(prob_full), value_head, precision=lax.Precision.HIGHEST)

def reference(hidden_in, segments, weight_query, bias_query, weight_key, bias_key, weight_value, bias_value, weight_out, bias_out, gain_one, shift_one, weight_up, bias_up, weight_down, bias_down, gain_two, shift_two, cotangent):
    places = jnp.arange(LROW, dtype=jnp.int32)[None, :]
    opening = jnp.concatenate([jnp.ones((ROWS_ALL, 1), jnp.bool_), segments[:, 1:] != segments[:, :-1]], axis=1)
    positions = (places - lax.cummax(jnp.where(opening, places, 0), axis=1)).astype(jnp.float32)
    cosine_tab, sine_tab = rotary_tables(positions)
    seg_heads = jnp.repeat(segments, HEADS, axis=0)
    score_scale = HD ** (-0.5)

    def forward(hidden, w_query, b_query, w_key, b_key, w_value, b_value, w_out, b_out, g_one, s_one, w_up, b_up, w_down, b_down, g_two, s_two):
        query_pre = low_back(matmul(hidden, w_query) + b_query)
        key_pre = low_back(matmul(hidden, w_key) + b_key)
        value_low = low(low_back(matmul(hidden, w_value) + b_value))
        query_rot = low(rotate(query_pre, cosine_tab, sine_tab) * score_scale)
        key_rot = low(rotate(key_pre, cosine_tab, sine_tab))
        attended = lax.map(jax.checkpoint(head_attention), (split_heads(query_rot), split_heads(key_rot), split_heads(value_low), seg_heads))
        attn_low = low(low_back(merge_heads(attended)))
        attn_out = low_back(matmul(attn_low, w_out) + b_out)
        normed_one = layer_norm(hidden + attn_out, g_one, s_one)
        pre_act = low_back(matmul(low(normed_one), w_up) + b_up)
        hidden_low = low(jax.nn.gelu(pre_act, approximate=False))
        ffn_out = low_back(matmul(hidden_low, w_down) + b_down)
        return layer_norm(normed_one + ffn_out, g_two, s_two)
    params = (hidden_in.astype(jnp.float32), weight_query.astype(jnp.float32), bias_query, weight_key.astype(jnp.float32), bias_key, weight_value.astype(jnp.float32), bias_value, weight_out.astype(jnp.float32), bias_out, gain_one, shift_one, weight_up.astype(jnp.float32), bias_up, weight_down.astype(jnp.float32), bias_down, gain_two, shift_two)
    layer_out, pullback = jax.vjp(forward, *params)
    grads = pullback(cotangent.astype(jnp.float32))
    return (layer_out, grads[0], grads[1], grads[2], grads[3], grads[4], grads[5], grads[6], grads[7], grads[8], grads[9], grads[10], grads[11], grads[12], grads[13], grads[14], grads[15], grads[16])
```

```python
import functools
import math

import jax
import jax.numpy as jnp
import numpy as np
from jax import lax
from jax.experimental import pallas as pl
from jax.experimental.pallas import tpu as pltpu
from jax.sharding import PartitionSpec as P

D = 768
HD = 64
R = 3
T = 128
NH = 3
E = NH * HD
F = 768
NW = 16
NN = 4
TOK = R * T
L = NW * T
C = T // NN
CH = R * C
PAIRS = R * NH
G = D // (2 * NW)
SLOT = 3 * HD + 16
AUG = HD + 16
NWG = 1792
EPSILON = 1e-12
BIG = 1e30
LOG2E = math.log2(math.e)
LN2 = math.log(2.0)
f32, bf16 = jnp.float32, jnp.bfloat16


def dot(a, b, dims):
    return lax.dot_general(a, b, (dims, ((), ())), preferred_element_type=f32)


NORMAL, BOTH_LAST, BOTH_FIRST = ((1,), (0,)), ((1,), (1,)), ((0,), (0,))


def call(name, kernel, outs, args, scratch=(), flops=0, any_space=()):
    return pl.pallas_call(
        kernel,
        out_shape=[jax.ShapeDtypeStruct(s, t) for s, t in outs],
        in_specs=[pl.BlockSpec(memory_space=pltpu.VMEM) for _ in args],
        out_specs=[pl.BlockSpec(memory_space=pltpu.VMEM) for _ in outs],
        scratch_shapes=list(scratch),
        compiler_params=pltpu.CompilerParams(vmem_limit_bytes=48 * 1024 * 1024),
        cost_estimate=pl.CostEstimate(flops=flops, bytes_accessed=4 * 1024 * 1024, transcendentals=0),
        name=name,
    )(*args)


def row_of(ref):
    return ref[...].reshape(1, ref.shape[-1])


def split3(v):
    hi = v.astype(bf16).astype(f32)
    rest = v - hi
    mid = rest.astype(bf16).astype(f32)
    return hi, mid, rest - mid


def sine_cosine(angle):
    turns = jnp.floor(angle * (2.0 / math.pi) + 0.5)
    r = ((angle - turns * 1.5703125) - turns * 4.837512969970703125e-4) - turns * 7.54978995489188e-8
    z = r * r
    sine = r + r * z * (-1.6666654611e-1 + z * (8.3321608736e-3 + z * -1.9515295891e-4))
    cosine = 1.0 - 0.5 * z + z * z * (4.166664568298827e-2 + z * (-1.388731625493765e-3 + z * 2.443315711809948e-5))
    quarter = turns - 4.0 * jnp.floor(turns * 0.25)
    odd = (quarter == 1.0) | (quarter == 3.0)
    sin_abs = jnp.where(odd, cosine, sine)
    cos_abs = jnp.where(odd, sine, cosine)
    return jnp.where(quarter >= 2.0, -sin_abs, sin_abs), jnp.where((quarter == 1.0) | (quarter == 2.0), -cos_abs, cos_abs)


def swap_pairs(t):
    rows = lax.broadcasted_iota(jnp.int32, t.shape, 0)
    return jnp.where(rows % 2 == 0, pltpu.roll(t, HD - 1, 0), pltpu.roll(t, 1, 0))


def project_kernel(x, seg, wq, bq, wk, bk, wv, bv, slots):
    flat = x[...].reshape(TOK, D)
    for j, (w, b) in enumerate(((wq, bq), (wk, bk), (wv, bv))):
        y = dot(flat, w[...], NORMAL) + row_of(b)
        yt = y.T.astype(bf16)
        for r in range(R):
            for h in range(NH):
                slots[r * NH + h, j * HD : (j + 1) * HD, :] = yt[h * HD : (h + 1) * HD, r * T : (r + 1) * T]
    for r in range(R):
        ids = jnp.broadcast_to(seg[r : r + 1, :].astype(f32), (16, T)).astype(bf16)
        for h in range(NH):
            slots[r * NH + h, 3 * HD :, :] = ids


def attend_kernel(got, freq, out, q_t, k_t, v_t, o_t, cos_t, sin_t, k_nat):
    @pl.when(lax.axis_index("wide") < PAIRS)
    def _():
        ids = [got[w, 3 * HD :, :].astype(f32)[0:1, :] for w in range(NW)]
        starts = []
        for d in range(1, 5):
            below = jnp.zeros((1, T), f32)
            for w in range(NW):
                below = below + jnp.where(ids[w] < d, 1.0, 0.0)
            starts.append(jnp.sum(below, axis=1, keepdims=True))
        odd = lax.broadcasted_iota(jnp.int32, (HD, T), 0) % 2 == 1
        ext = lax.broadcasted_iota(jnp.int32, (16, T), 0)
        lane = lax.broadcasted_iota(jnp.int32, (1, T), 1).astype(f32)
        for w in range(NW):
            at = slice(w * T, (w + 1) * T)
            start = jnp.zeros((1, T), f32)
            for d in range(1, 5):
                start = jnp.where(ids[w] == d, starts[d - 1], start)
            sine, cosine = sine_cosine(freq[...] * (lane + (w * T) - start))
            sine = jnp.where(odd, sine, -sine)
            cos_t[:, at] = cosine
            sin_t[:, at] = sine
            query = got[w, 0:HD, :].astype(f32)
            key = got[w, HD : 2 * HD, :].astype(f32)
            query = (query * cosine + swap_pairs(query) * sine) * (HD**-0.5 * LOG2E)
            key = key * cosine + swap_pairs(key) * sine
            same = ids[w] == ext.astype(f32)
            doc = ext < 5
            key_ext = jnp.where(doc, jnp.where(same, 1.0, 0.0), jnp.where(ext < 8, 1.0, 0.0))
            q_t[0:HD, at] = query.astype(bf16)
            q_t[HD:AUG, at] = jnp.where(doc, jnp.where(same, 0.0, -BIG), 0.0).astype(bf16)
            k_t[0:HD, at] = key.astype(bf16)
            k_t[HD:AUG, at] = key_ext.astype(bf16)
            k_nat[at, :] = jnp.concatenate([key, key_ext], axis=0).T.astype(bf16)
            v_t[0:HD, at] = got[w, 2 * HD : 3 * HD, :]
            v_t[HD:AUG, at] = jnp.where(ext < 3, 1.0, 0.0).astype(bf16)

        def tile(i, carry):
            at = pl.ds(pl.multiple_of(i * 256, 256), 256)
            s = dot(k_nat[...], q_t[:, at], NORMAL)
            top = jnp.max(s, axis=0, keepdims=True)
            p = jnp.exp2(s - top).astype(bf16)
            o = dot(v_t[...], p, NORMAL)
            total = o[HD : HD + 1, :]
            o = o[0:HD, :] / total
            o_t[:, at] = o
            low = o.astype(bf16)
            out[2 * i] = low[:, 0:T]
            out[2 * i + 1] = low[:, T:]
            hi, mid, lo = split3(-(top + jnp.log(total) * LOG2E))
            rows = lax.broadcasted_iota(jnp.int32, (16, 256), 0)
            more = jnp.where(rows == 5, hi, jnp.where(rows == 6, mid, jnp.where(rows == 7, lo, 0.0)))
            q_t[HD:AUG, at] = (q_t[HD:AUG, at].astype(f32) + more).astype(bf16)
            return carry

        lax.fori_loop(0, L // 256, tile, 0)


def attend_back_kernel(got, q_t, k_t, v_t, o_t, cos_t, sin_t, out, do_t, do_nat, q_nat, k_nat, v_nat, dq_t):
    @pl.when(lax.axis_index("wide") < PAIRS)
    def _():
        ext = lax.broadcasted_iota(jnp.int32, (16, T), 0)
        for w in range(NW):
            at = slice(w * T, (w + 1) * T)
            low = got[w]
            grad = low.astype(f32)
            delta = -jnp.sum(grad * o_t[:, at], axis=0, keepdims=True)
            hi, mid, lo = split3(delta)
            do_t[0:HD, at] = low
            do_t[HD:AUG, at] = jnp.where(
                ext == 0, hi, jnp.where(ext == 1, mid, jnp.where(ext == 2, lo, 0.0))
            ).astype(bf16)
            do_nat[at, :] = grad.T.astype(bf16)
            q_nat[at, :] = q_t[0:HD, at].astype(f32).T.astype(bf16)
            k_nat[at, :] = k_t[:, at].astype(f32).T.astype(bf16)
            v_nat[at, :] = v_t[:, at].astype(f32).T.astype(bf16)
        dq_t[...] = jnp.zeros((HD, L), f32)

        def folded(t):
            total = t[:, 0:T]
            for k in range(1, t.shape[1] // T):
                total = total + t[:, k * T : (k + 1) * T]
            return total

        def tile(j, carry):
            sum_key, sum_value = carry
            at = pl.ds(pl.multiple_of(j * 256, 256), 256)
            p = jnp.exp2(dot(k_nat[at, :], q_t[...], NORMAL))
            dp = dot(v_nat[at, :], do_t[...], NORMAL)
            ds = (p * dp).astype(bf16)
            dv = dot(p.astype(bf16), do_nat[...], NORMAL).T.astype(bf16)
            dk = dot(ds, q_nat[...], NORMAL).T * LN2
            dk = (dk * cos_t[:, at] - swap_pairs(dk) * sin_t[:, at]).astype(bf16)
            dq_t[...] += dot(k_t[0:HD, at], ds, NORMAL)
            for k in range(2):
                out[2 * j + k, HD : 2 * HD, :] = dk[:, k * T : (k + 1) * T]
                out[2 * j + k, 2 * HD : 3 * HD, :] = dv[:, k * T : (k + 1) * T]
            return sum_key + folded(dk.astype(f32)), sum_value + folded(dv.astype(f32))

        zero = jnp.zeros((HD, T), f32)
        sum_key, sum_value = lax.fori_loop(0, L // 256, tile, (zero, zero))
        sum_query = zero
        for w in range(NW):
            at = slice(w * T, (w + 1) * T)
            dq = dq_t[:, at] * (HD**-0.5)
            dq = (dq * cos_t[:, at] - swap_pairs(dq) * sin_t[:, at]).astype(bf16)
            out[w, 0:HD, :] = dq
            sum_query = sum_query + dq.astype(f32)
        rows = [jnp.sum(t.T, axis=0, keepdims=True) for t in (sum_query, sum_key, sum_value)]
        first = jnp.concatenate([rows[0], rows[1]], axis=1)
        second = jnp.concatenate([rows[2], rows[2]], axis=1)
        first_hi, second_hi = first.astype(bf16).astype(f32), second.astype(bf16).astype(f32)
        block = jnp.where(
            ext == 0,
            first_hi,
            jnp.where(ext == 1, second_hi, jnp.where(ext == 2, first - first_hi, second - second_hi)),
        )
        block = jnp.where(ext < 4, block, 0.0).astype(bf16)
        for w in range(NW):
            out[w, 3 * HD :, :] = block


def chunk_rows(c, r):
    return pl.ds(pl.multiple_of(r * T + c * C, C), C)


def forward_kernel(
    o0, o1, o2, o3, w0, w1, w2, w3, x, b_out, g_one, s_one, up_down, b_up,
    normed_low, hidden_low, slope, xhat_own, rstd_own, part0, part1, part2, part3,
    resid, xhat, rstd, wide_part,
):
    n = lax.axis_index("narrow")
    for r in range(R):
        at = slice(r * T, (r + 1) * T)
        heads = jnp.concatenate([o[r * NH : (r + 1) * NH].reshape(E, T) for o in (o0, o1, o2, o3)], axis=0)
        weight = jnp.concatenate([w[...] for w in (w0, w1, w2, w3)], axis=0)
        resid[at, :] = x[r].astype(f32) + (dot(heads, weight, BOTH_FIRST) + row_of(b_out))
    residual = resid[...]
    center = residual - jnp.mean(residual, axis=-1, keepdims=True)
    inverse = lax.rsqrt(jnp.mean(center * center, axis=-1, keepdims=True) + EPSILON)
    unit = center * inverse
    xhat[...] = unit
    rstd[...] = jnp.broadcast_to(inverse, (TOK, T))
    low = (unit * row_of(g_one) + row_of(s_one)).astype(bf16)
    normed_low[...] = low
    up = up_down[:, 0 : D // NW, :].reshape(D, F)
    down = up_down[:, D // NW :, :].reshape(D, F)
    pre = dot(low, up, NORMAL) + row_of(b_up)
    half = 0.5 * (1.0 + lax.erf(pre * (2.0**-0.5)))
    slope[...] = half + pre * jnp.exp(-0.5 * pre * pre) * (1.0 / math.sqrt(2.0 * math.pi))
    hidden = (pre * half).astype(bf16)
    hidden_low[...] = hidden
    wide_part[...] = dot(hidden, down, BOTH_LAST)
    for r in range(R):
        to = slice(r * C, (r + 1) * C)
        xhat_own[to, :] = xhat[chunk_rows(n, r), :]
        rstd_own[to, :] = rstd[chunk_rows(n, r), :]
        part0[to, :] = wide_part[chunk_rows(n, r), :]
        for s, part in ((1, part1), (2, part2), (3, part3)):
            part[to, :] = wide_part[chunk_rows((n + s) % NN, r), :].astype(bf16)


def norm_two_kernel(
    part0, part1, part2, part3, xhat_own, cot, g_one, s_one, b_down, g_two, s_two,
    layer_low, grad_ffn, grad_two, sums,
):
    n = lax.axis_index("narrow")
    total = part0[...] + part1[...].astype(f32) + part2[...].astype(f32) + part3[...].astype(f32)
    normed = xhat_own[...] * row_of(g_one) + row_of(s_one)
    residual = normed + (total + row_of(b_down))
    center = residual - jnp.mean(residual, axis=-1, keepdims=True)
    inverse = lax.rsqrt(jnp.mean(center * center, axis=-1, keepdims=True) + EPSILON)
    unit = center * inverse
    layer_low[...] = (unit * row_of(g_two) + row_of(s_two)).astype(bf16)
    ct = jnp.concatenate([cot[r, pl.ds(pl.multiple_of(n * C, C), C), :] for r in range(R)], axis=0).astype(f32)
    scaled = ct * row_of(g_two)
    grad = inverse * (
        scaled
        - jnp.mean(scaled, axis=-1, keepdims=True)
        - unit * jnp.mean(scaled * unit, axis=-1, keepdims=True)
    )
    grad_two[...] = grad
    low = grad.astype(bf16)
    grad_ffn[...] = low
    sums[...] = jnp.concatenate(
        [
            jnp.sum(ct * unit, axis=0, keepdims=True),
            jnp.sum(ct, axis=0, keepdims=True),
            jnp.sum(low.astype(f32), axis=0, keepdims=True),
            jnp.zeros((5, D), f32),
        ],
        axis=0,
    )


def assemble(n, parts, whole):
    for s, part in enumerate(parts):
        c = (n + NN - s) % NN
        for r in range(R):
            whole[chunk_rows(c, r), :] = part[r * C : (r + 1) * C, :].astype(whole.dtype)


def ffn_back_kernel(g0, g1, g2, g3, up_down, slope, grad_all, grad_pre, part0, part1, part2, part3, wide_part):
    n = lax.axis_index("narrow")
    assemble(n, (g0, g1, g2, g3), grad_all)
    up = up_down[:, 0 : D // NW, :].reshape(D, F)
    down = up_down[:, D // NW :, :].reshape(D, F)
    low = (slope[...] * dot(grad_all[...], down, NORMAL)).astype(bf16)
    grad_pre[...] = low
    wide_part[...] = dot(low, up, BOTH_LAST)
    for r in range(R):
        to = slice(r * C, (r + 1) * C)
        part0[to, :] = wide_part[chunk_rows(n, r), :]
        for s, part in ((1, part1), (2, part2), (3, part3)):
            part[to, :] = wide_part[chunk_rows((n + s) % NN, r), :].astype(bf16)


def norm_one_back_kernel(
    part0, part1, part2, part3, grad_two, xhat_own, rstd_own, g_one, sums_two, grad_one, grad_low, sums
):
    total = part0[...] + part1[...].astype(f32) + part2[...].astype(f32) + part3[...].astype(f32)
    grad = grad_two[...] + total
    unit = xhat_own[...]
    scaled = grad * row_of(g_one)
    one = rstd_own[:, 0:1] * (
        scaled
        - jnp.mean(scaled, axis=-1, keepdims=True)
        - unit * jnp.mean(scaled * unit, axis=-1, keepdims=True)
    )
    grad_one[...] = one
    low = one.astype(bf16)
    grad_low[...] = low
    sums[...] = jnp.concatenate(
        [
            sums_two[0:3, :],
            jnp.sum(grad * unit, axis=0, keepdims=True),
            jnp.sum(grad, axis=0, keepdims=True),
            jnp.sum(low.astype(f32), axis=0, keepdims=True),
            jnp.zeros((2, D), f32),
        ],
        axis=0,
    )


def grad_attn_kernel(g0, g1, g2, g3, w_out, grad_all, slots):
    n = lax.axis_index("narrow")
    assemble(n, (g0, g1, g2, g3), grad_all)
    grad = dot(w_out[...], grad_all[...], BOTH_LAST).astype(bf16)
    for r in range(R):
        for h in range(NH):
            slots[r * NH + h] = grad[h * HD : (h + 1) * HD, r * T : (r + 1) * T]


def weights_kernel(
    normed_low, grad_pre, grad_ffn, hidden_low, grad_out, attn, v0, v1, v2, v3, send, keep, sums, whole, vectors
):
    n, c = lax.axis_index("narrow"), lax.axis_index("dp")
    whole[:, 0:F] = dot(normed_low[...], grad_pre[...], BOTH_FIRST)
    whole[:, F : 2 * F] = dot(grad_ffn[...], hidden_low[...], BOTH_FIRST)
    heads = jnp.concatenate([attn[r * NH : (r + 1) * NH].reshape(E, T) for r in range(R)], axis=1)
    whole[:, 2 * F : 2 * F + E] = dot(grad_out[...], heads, ((0,), (1,)))
    half = D // 2
    send[:, 0 : 2 * F + E] = whole[pl.ds(pl.multiple_of((1 - c) * half, half), half), :].astype(bf16)
    keep[:, 0 : 2 * F + E] = whole[pl.ds(pl.multiple_of(c * half, half), half), :]
    for s, v in enumerate((v0, v1, v2, v3)):
        vectors[(n + NN - s) % NN] = v[...]
    total = vectors[0] + vectors[1] + vectors[2] + vectors[3]
    bias = jnp.sum(grad_pre[...].astype(f32), axis=0, keepdims=True)
    row = lax.broadcasted_iota(jnp.int32, (8, D), 0)
    sums[...] = jnp.where(row == 6, bias, total)


def weights_add_kernel(keep, got, sums, sums_got, slots):
    both = (keep[...] + got[...].astype(f32)).astype(bf16)
    total = sums[...] + sums_got[...]
    vec = jnp.concatenate([total[:, 256 * k : 256 * (k + 1)] for k in range(3)], axis=0).astype(bf16)
    for w in range(NW):
        slots[w, :, 0:NWG] = both[w * G : (w + 1) * G, :]
        slots[w, :, NWG:] = vec


def weights_sum_kernel(got, up, down, out, g_two, s_two, b_down, g_one, s_one, b_out, b_up):
    total = got[0].astype(f32)
    for w in range(1, NW):
        total = total + got[w].astype(f32)
    up[...] = total[:, 0:F]
    down[...] = total[:, F : 2 * F].T
    out[...] = total[:, 2 * F : 2 * F + E].T
    vec = jnp.concatenate([total[8 * k : 8 * (k + 1), NWG:] for k in range(3)], axis=1)
    for k, ref in enumerate((g_two, s_two, b_down, g_one, s_one, b_out, b_up)):
        ref[...] = vec[k : k + 1, :].reshape(D)


def input_back_kernel(got, x, wq, wk, wv, part0, part1, part2, part3, send, keep, sums, whole, wide_part):
    n, c = lax.axis_index("narrow"), lax.axis_index("dp")
    flat = x[...].reshape(TOK, D)
    total = None
    for j, w in enumerate((wq, wk, wv)):
        grad_t = jnp.concatenate(
            [
                jnp.concatenate([got[r * NH + h, j * HD : (j + 1) * HD, :] for h in range(NH)], axis=0)
                for r in range(R)
            ],
            axis=1,
        )
        grad = grad_t.astype(f32).T.astype(bf16)
        term = dot(grad, w[...], BOTH_LAST)
        total = term if total is None else total + term
        whole[:, j * E : (j + 1) * E] = dot(flat, grad, BOTH_FIRST)
    wide_part[...] = total
    for r in range(R):
        to = slice(r * C, (r + 1) * C)
        part0[to, :] = wide_part[chunk_rows(n, r), :]
        for s, part in ((1, part1), (2, part2), (3, part3)):
            part[to, :] = wide_part[chunk_rows((n + s) % NN, r), :].astype(bf16)
    half = D // 2
    send[...] = whole[pl.ds(pl.multiple_of((1 - c) * half, half), half), :].astype(bf16)
    keep[...] = whole[pl.ds(pl.multiple_of(c * half, half), half), :]
    heads = []
    for h in range(NH):
        block = got[h, 3 * HD :, :].astype(f32)
        for r in range(1, R):
            block = block + got[r * NH + h, 3 * HD :, :].astype(f32)
        heads.append(block)
    first = jnp.concatenate([b[0:1, 0:HD] + b[2:3, 0:HD] for b in heads], axis=1)
    second = jnp.concatenate([b[0:1, HD:] + b[2:3, HD:] for b in heads], axis=1)
    third = jnp.concatenate([b[1:2, 0:HD] + b[3:4, 0:HD] for b in heads], axis=1)
    sums[...] = jnp.concatenate([first, second, third, jnp.zeros((5, E), f32)], axis=0)


def input_add_kernel(keep, got, sums, sums_got, slots, b_q, b_k, b_v):
    both = (keep[...] + got[...].astype(f32)).astype(bf16)
    for w in range(NW):
        slots[w] = both[w * G : (w + 1) * G, :]
    total = sums[...] + sums_got[...]
    for k, ref in enumerate((b_q, b_k, b_v)):
        ref[...] = total[k : k + 1, :].reshape(E)


def input_sum_kernel(got, g_q, g_k, g_v):
    total = got[0].astype(f32)
    for w in range(1, NW):
        total = total + got[w].astype(f32)
    for k, ref in enumerate((g_q, g_k, g_v)):
        ref[...] = total[:, k * E : (k + 1) * E]


def input_chunk_kernel(part0, part1, part2, part3, grad_one, low):
    total = part0[...] + part1[...].astype(f32) + part2[...].astype(f32) + part3[...].astype(f32)
    low[...] = (grad_one[...] + total).astype(bf16)


def spread_kernel(g0, g1, g2, g3, out):
    n = lax.axis_index("narrow")
    for s, part in enumerate((g0, g1, g2, g3)):
        at = pl.ds(pl.multiple_of((n + NN - s) % NN * C, C), C)
        for r in range(R):
            out[r, at, :] = part[r * C : (r + 1) * C, :].astype(f32)


def shifted(x, s):
    return lax.ppermute(x, "narrow", [(i, (i + s) % NN) for i in range(NN)])


def gather_narrow(x):
    return (x, shifted(x, 1), shifted(x, 2), shifted(x, 3))


def scatter_narrow(parts):
    return (parts[0], shifted(parts[1], 1), shifted(parts[2], 2), shifted(parts[3], 3))


def other_core(x):
    return lax.ppermute(x, "dp", [(0, 1), (1, 0)])


def exchange(slots):
    return lax.all_to_all(slots, "wide", 0, 0, tiled=True)


def body(
    hidden_in, segments, weight_query, bias_query, weight_key, bias_key, weight_value, bias_value,
    weight_out, bias_out, gain_one, shift_one, weight_up, bias_up, weight_down, bias_down,
    gain_two, shift_two, cotangent,
):
    frequency = np.repeat(np.power(10000.0, -np.arange(0, HD, 2) / HD), 2).astype(np.float32)
    frequency = jnp.asarray(np.broadcast_to(frequency[:, None], (HD, T)))
    up_down = jnp.concatenate([weight_up, weight_down.T], axis=0)
    up_down = lax.all_gather(up_down, "wide", axis=0, tiled=False)
    weights_out = gather_narrow(weight_out)

    (slots,) = call(
        "project",
        project_kernel,
        [((NW, SLOT, T), bf16)],
        (hidden_in, segments, weight_query, bias_query, weight_key, bias_key, weight_value, bias_value),
        flops=2 * TOK * D * 3 * E,
    )
    got = exchange(slots)
    out_slots, q_t, k_t, v_t, o_t, cos_t, sin_t = call(
        "attend",
        attend_kernel,
        [
            ((NW, HD, T), bf16),
            ((AUG, L), bf16),
            ((AUG, L), bf16),
            ((AUG, L), bf16),
            ((HD, L), f32),
            ((HD, L), f32),
            ((HD, L), f32),
        ],
        (got, frequency),
        scratch=[pltpu.VMEM((L, AUG), bf16)],
        flops=16 * L * L * HD,
    )
    attn = exchange(out_slots)[0:PAIRS]
    heads = gather_narrow(attn)
    chunk_f32, chunk_low = ((CH, D), f32), ((CH, D), bf16)
    tok_low = ((TOK, D), bf16)
    parts4 = [chunk_f32, chunk_low, chunk_low, chunk_low]
    normed_low, hidden_low, slope, xhat_own, rstd_own, *parts = call(
        "forward",
        forward_kernel,
        [tok_low, tok_low, ((TOK, F), f32), chunk_f32, ((CH, T), f32), *parts4],
        (*heads, *weights_out, hidden_in, bias_out, gain_one, shift_one, up_down, bias_up),
        scratch=[
            pltpu.VMEM((TOK, D), f32),
            pltpu.VMEM((TOK, D), f32),
            pltpu.VMEM((TOK, T), f32),
            pltpu.VMEM((TOK, D), f32),
        ],
        flops=3 * 2 * TOK * D * F,
    )
    parts = scatter_narrow(parts)
    layer_low, grad_ffn, grad_two, sums_two = call(
        "norm_two",
        norm_two_kernel,
        [chunk_low, chunk_low, chunk_f32, ((8, D), f32)],
        (*parts, xhat_own, cotangent, gain_one, shift_one, bias_down, gain_two, shift_two),
    )
    grads = gather_narrow(grad_ffn)
    grad_ffn_all, grad_pre, *parts = call(
        "ffn_back",
        ffn_back_kernel,
        [tok_low, ((TOK, F), bf16), *parts4],
        (*grads, up_down, slope),
        scratch=[pltpu.VMEM((TOK, D), f32)],
        flops=2 * 2 * TOK * D * F,
    )
    parts = scatter_narrow(parts)
    grad_one, grad_low, sums_one = call(
        "norm_one_back",
        norm_one_back_kernel,
        [chunk_f32, chunk_low, ((8, D), f32)],
        (*parts, grad_two, xhat_own, rstd_own, gain_one, sums_two),
    )
    grads = gather_narrow(grad_low)
    grad_out_all, slots = call(
        "grad_attn",
        grad_attn_kernel,
        [tok_low, ((NW, HD, T), bf16)],
        (*grads, weight_out),
        flops=2 * TOK * D * E,
    )
    got = exchange(slots)
    (slots,) = call(
        "attend_back",
        attend_back_kernel,
        [((NW, SLOT, T), bf16)],
        (got, q_t, k_t, v_t, o_t, cos_t, sin_t),
        scratch=[
            pltpu.VMEM((AUG, L), bf16),
            pltpu.VMEM((L, HD), bf16),
            pltpu.VMEM((L, HD), bf16),
            pltpu.VMEM((L, AUG), bf16),
            pltpu.VMEM((L, AUG), bf16),
            pltpu.VMEM((HD, L), f32),
        ],
        flops=40 * L * L * HD,
    )
    vectors = gather_narrow(sums_one)
    send, keep, sums = call(
        "weights",
        weights_kernel,
        [((D // 2, NWG), bf16), ((D // 2, NWG), f32), ((8, D), f32)],
        (normed_low, grad_pre, grad_ffn_all, hidden_low, grad_out_all, attn, *vectors),
        scratch=[pltpu.VMEM((D, 2 * F + E), f32), pltpu.VMEM((NN, 8, D), f32)],
        flops=2 * TOK * D * (2 * F + E),
    )
    (weight_slots,) = call(
        "weights_add",
        weights_add_kernel,
        [((NW, G, NWG + 256), bf16)],
        (keep, other_core(send), sums, other_core(sums)),
    )
    vec = ((D,), f32)
    grad_up, grad_down, grad_out, g_two, s_two, b_down, g_one, s_one, b_out, b_up = call(
        "weights_sum",
        weights_sum_kernel,
        [((G, F), f32), ((F, G), f32), ((E, G), f32), vec, vec, vec, vec, vec, vec, vec],
        (exchange(weight_slots),),
    )
    whole_out = ((R, T, D), f32)
    (layer_out,) = call("layer_out", spread_kernel, [whole_out], gather_narrow(layer_low))

    got = exchange(slots)
    *parts, send, keep, sums = call(
        "input_back",
        input_back_kernel,
        [*parts4, ((D // 2, 3 * E), bf16), ((D // 2, 3 * E), f32), ((8, E), f32)],
        (got, hidden_in, weight_query, weight_key, weight_value),
        scratch=[pltpu.VMEM((D, 3 * E), f32), pltpu.VMEM((TOK, D), f32)],
        flops=2 * 2 * TOK * D * 3 * E,
    )
    parts = scatter_narrow(parts)
    slots, b_query, b_key, b_value = call(
        "input_add",
        input_add_kernel,
        [((NW, G, 3 * E), bf16), ((E,), f32), ((E,), f32), ((E,), f32)],
        (keep, other_core(send), sums, other_core(sums)),
    )
    (input_low,) = call("input_chunk", input_chunk_kernel, [chunk_low], (*parts, grad_one))
    (grad_input,) = call("grad_input", spread_kernel, [whole_out], gather_narrow(input_low))
    g_query, g_key, g_value = call(
        "input_sum", input_sum_kernel, [((G, E), f32)] * 3, (exchange(slots),)
    )
    return (
        layer_out, grad_input, g_query, b_query, g_key, b_key, g_value, b_value, grad_out, b_out,
        g_one, s_one, grad_up, b_up, grad_down, b_down, g_two, s_two,
    )


def solution(mesh):
    tokens, whole = P("dp", "wide", None), P()
    column, vector = P(None, "narrow"), P("narrow")
    rows_split, columns_split = P(("dp", "wide"), "narrow"), P("narrow", ("dp", "wide"))
    in_specs = (
        tokens, P("dp", "wide"), column, vector, column, vector, column, vector, P("narrow", None), whole,
        whole, whole, P("wide", "narrow"), vector, P("narrow", "wide"), whole, whole, whole, tokens,
    )
    out_specs = (
        tokens, tokens, rows_split, vector, rows_split, vector, rows_split, vector, columns_split, whole,
        whole, whole, rows_split, vector, columns_split, whole, whole, whole,
    )
    return jax.shard_map(body, mesh=mesh, in_specs=in_specs, out_specs=out_specs, check_vma=False)
```

```python
import functools
import math

import jax
import jax.numpy as jnp
import numpy as np
from jax import lax
from jax.experimental import pallas as pl
from jax.experimental.pallas import tpu as pltpu
from jax.sharding import PartitionSpec as P

D = 768
HD = 64
R = 3
T = 128
NH = 3
E = NH * HD
F = 768
NW = 16
NN = 4
TOK = R * T
L = NW * T
C = T // NN
CH = R * C
PAIRS = R * NH
G = D // (2 * NW)
SLOT = 3 * HD + 16
AUG = HD + 16
EPSILON = 1e-12
BIG = 1e30
LOG2E = math.log2(math.e)
LN2 = math.log(2.0)
COST = 10**11
f32, bf16 = jnp.float32, jnp.bfloat16


def dot(a, b, dims):
    return lax.dot_general(a, b, (dims, ((), ())), preferred_element_type=f32)


NORMAL, BOTH_LAST, BOTH_FIRST = ((1,), (0,)), ((1,), (1,)), ((0,), (0,))


def call(
    name, kernel, outs, args, scratch=(), cost=1024, mib=16, after=(), far_in=(), any_in=(), near=(), far=(), aliases={},
    token=False,
):
    if token:
        outs = [*outs, ((8, 128), f32)]

    def run(*refs):
        end = len(args) + len(after)
        if token:
            at = end + len(outs) - 1
            refs[at][...] = jnp.zeros((8, 128), f32)
            refs = refs[:at] + refs[at + 1 :]
        kernel(*refs[: len(args)], *refs[end:])

    def shape(k, s, t):
        return pltpu.VMEM(s, t) if k in near else pltpu.HBM(s, t) if k in far else jax.ShapeDtypeStruct(s, t)

    args = [pltpu.with_memory_space_constraint(a, pltpu.HBM) if k in far_in else a for k, a in enumerate(args)]
    return pl.pallas_call(
        run,
        out_shape=[shape(k, s, t) for k, (s, t) in enumerate(outs)],
        in_specs=[
            pl.BlockSpec(memory_space=pltpu.HBM if k in far_in else pl.ANY if k in any_in else pltpu.VMEM)
            for k in range(len(args))
        ]
        + [pl.BlockSpec(memory_space=pl.ANY) for _ in after],
        out_specs=[pl.BlockSpec(memory_space=pltpu.HBM if k in far else pltpu.VMEM) for k in range(len(outs))],
        scratch_shapes=list(scratch),
        input_output_aliases=aliases,
        compiler_params=pltpu.CompilerParams(vmem_limit_bytes=mib * 1024 * 1024),
        cost_estimate=pl.CostEstimate(flops=cost, bytes_accessed=1024, transcendentals=0),
        name=name,
    )(*args, *after)


def later(x, *after):
    return pl.pallas_call(
        lambda *refs: None,
        out_shape=jax.ShapeDtypeStruct(x.shape, x.dtype),
        in_specs=[pl.BlockSpec(memory_space=pltpu.HBM)] + [pl.BlockSpec(memory_space=pl.ANY) for _ in after],
        out_specs=pl.BlockSpec(memory_space=pltpu.HBM),
        input_output_aliases={0: 0},
        cost_estimate=pl.CostEstimate(flops=1024, bytes_accessed=1024, transcendentals=0),
        name="later",
    )(x, *after)


def copies(pairs, sems):
    made = [pltpu.make_async_copy(a, b, sems.at[k]) for k, (a, b) in enumerate(pairs)]
    for copy in made:
        copy.start()
    return made


def row_of(ref):
    return ref[...].reshape(1, ref.shape[-1])


def split3(v):
    hi = v.astype(bf16).astype(f32)
    rest = v - hi
    mid = rest.astype(bf16).astype(f32)
    return hi, mid, (rest - mid).astype(bf16).astype(f32)


def sine_cosine(angle):
    turns = jnp.floor(angle * (2.0 / math.pi) + 0.5)
    r = ((angle - turns * 1.5703125) - turns * 4.837512969970703125e-4) - turns * 7.54978995489188e-8
    z = r * r
    sine = r + r * z * (-1.6666654611e-1 + z * (8.3321608736e-3 + z * -1.9515295891e-4))
    cosine = 1.0 - 0.5 * z + z * z * (4.166664568298827e-2 + z * (-1.388731625493765e-3 + z * 2.443315711809948e-5))
    quarter = turns - 4.0 * jnp.floor(turns * 0.25)
    odd = (quarter == 1.0) | (quarter == 3.0)
    sin_abs = jnp.where(odd, cosine, sine)
    cos_abs = jnp.where(odd, sine, cosine)
    return jnp.where(quarter >= 2.0, -sin_abs, sin_abs), jnp.where((quarter == 1.0) | (quarter == 2.0), -cos_abs, cos_abs)


def swap_pairs(t):
    rows = lax.broadcasted_iota(jnp.int32, t.shape, 0)
    return jnp.where(rows % 2 == 0, pltpu.roll(t, HD - 1, 0), pltpu.roll(t, 1, 0))


def project_kernel(x_far, seg, wq, bq, wk, bk, wv, bv, slots, x, near, bias0, bias1, bias2, ids, sems):
    pairs = [(x_far, x), (wq, near.at[0]), (bq, bias0), (wk, near.at[1]), (bk, bias1)]
    pairs += [(wv, near.at[2]), (bv, bias2), (seg, ids)]
    loads = copies(pairs, sems)
    for load in loads:
        load.wait()
    flat = x[...].reshape(TOK, D)
    for j, b in enumerate((bias0, bias1, bias2)):
        w = near.at[j]
        bias = jnp.broadcast_to(row_of(b), (T, E)).T
        yt = (dot(w[...], flat, BOTH_LAST) + jnp.concatenate([bias] * R, axis=1)).astype(bf16)
        for r in range(R):
            for h in range(NH):
                slots[r * NH + h, j * HD : (j + 1) * HD, :] = yt[h * HD : (h + 1) * HD, r * T : (r + 1) * T]
    for r in range(R):
        block = jnp.broadcast_to(ids[r : r + 1, :].astype(f32), (16, T)).astype(bf16)
        for h in range(NH):
            slots[r * NH + h, 3 * HD :, :] = block


def stack_kernel(a, b, c, d, out, sems):
    for copy in copies([(part, out.at[s]) for s, part in enumerate((a, b, c, d))], sems):
        copy.wait()


def attend_kernel(
    got, freq, out_far, q_far, k_far, v_far, o_far, cos_far, sin_far,
    out, q_t, k_t, v_t, o_t, cos_t, sin_t, k_nat, sems,
):
    @pl.when(lax.axis_index("wide") < PAIRS)
    def _():
        ids = [got[w, 3 * HD :, :].astype(f32)[0:1, :] for w in range(NW)]
        starts = []
        for d in range(1, 5):
            below = jnp.zeros((1, T), f32)
            for w in range(NW):
                below = below + jnp.where(ids[w] < d, 1.0, 0.0)
            starts.append(jnp.sum(below, axis=1, keepdims=True))
        odd = lax.broadcasted_iota(jnp.int32, (HD, T), 0) % 2 == 1
        ext = lax.broadcasted_iota(jnp.int32, (16, T), 0)
        lane = lax.broadcasted_iota(jnp.int32, (1, T), 1).astype(f32)
        for w in range(NW):
            at = slice(w * T, (w + 1) * T)
            start = jnp.zeros((1, T), f32)
            for d in range(1, 5):
                start = jnp.where(ids[w] == d, starts[d - 1], start)
            sine, cosine = sine_cosine(freq[...] * (lane + (w * T) - start))
            sine = jnp.where(odd, sine, -sine)
            cos_t[:, at] = cosine
            sin_t[:, at] = sine
            query = got[w, 0:HD, :].astype(f32)
            key = got[w, HD : 2 * HD, :].astype(f32)
            query = (query * cosine + swap_pairs(query) * sine) * (HD**-0.5 * LOG2E)
            key = key * cosine + swap_pairs(key) * sine
            same = ids[w] == ext.astype(f32)
            doc = ext < 5
            key_ext = jnp.where(doc, jnp.where(same, 1.0, 0.0), jnp.where(ext < 8, 1.0, 0.0))
            q_t[0:HD, at] = query.astype(bf16)
            q_t[HD:AUG, at] = jnp.where(doc, jnp.where(same, 0.0, -BIG), 0.0).astype(bf16)
            k_t[0:HD, at] = key.astype(bf16)
            k_t[HD:AUG, at] = key_ext.astype(bf16)
            k_nat[at, :] = jnp.concatenate([key, key_ext], axis=0).T.astype(bf16)
            v_t[0:HD, at] = got[w, 2 * HD : 3 * HD, :]
            v_t[HD:AUG, at] = jnp.where(ext < 3, 1.0, 0.0).astype(bf16)

        stores = copies([(k_t, k_far), (v_t, v_far), (cos_t, cos_far), (sin_t, sin_far)], sems)

        def tile(i, carry):
            at = pl.ds(pl.multiple_of(i * 256, 256), 256)
            s = dot(k_nat[...], q_t[:, at], NORMAL)
            top = jnp.max(s, axis=0, keepdims=True)
            p = jnp.exp2(s - top).astype(bf16)
            o = dot(v_t[...], p, NORMAL)
            total = o[HD : HD + 1, :]
            o = o[0:HD, :] / total
            o_t[:, at] = o
            natural = o.T
            for j in range(2 * NN):
                block = natural[j * C : (j + 1) * C, :]
                out[2 * NN * i + j] = jnp.concatenate([block[0 : C // 2], block[C // 2 :]], axis=1).astype(bf16)
            hi, mid, lo = split3(-(top + jnp.log(total) * LOG2E))
            rows = lax.broadcasted_iota(jnp.int32, (16, 256), 0)
            more = jnp.where(rows == 5, hi, jnp.where(rows == 6, mid, jnp.where(rows == 7, lo, 0.0)))
            q_t[HD:AUG, at] = (q_t[HD:AUG, at].astype(f32) + more).astype(bf16)
            return carry

        lax.fori_loop(0, L // 256, tile, 0)
        last = [(out, out_far, 4), (q_t, q_far, 5), (o_t, o_far, 6)]
        last = [pltpu.make_async_copy(a, b, sems.at[k]) for a, b, k in last]
        for store in last:
            store.start()
        for store in stores + last:
            store.wait()


def attend_back_kernel(
    got_far, o_far, q_far, k_far, v_far, cos_far, sin_far, out_far,
    out, got, o_t, q_t, k_t, v_t, cos_t, sin_t, do_t, do_nat, q_nat, k_nat, v_nat, dq_t, sems,
):
    @pl.when(lax.axis_index("wide") < PAIRS)
    def _():
        pairs = [(q_far, q_t), (k_far, k_t), (v_far, v_t), (got_far, got), (o_far, o_t), (cos_far, cos_t), (sin_far, sin_t)]
        loads = copies(pairs, sems)
        for load in loads[:3]:
            load.wait()
        ext = lax.broadcasted_iota(jnp.int32, (16, T), 0)
        for w in range(NW):
            at = slice(w * T, (w + 1) * T)
            q_nat[at, :] = q_t[0:HD, at].astype(f32).T.astype(bf16)
            k_nat[at, :] = k_t[:, at].astype(f32).T.astype(bf16)
            v_nat[at, :] = v_t[:, at].astype(f32).T.astype(bf16)
        for load in loads[3:]:
            load.wait()
        for w in range(NW):
            at = slice(w * T, (w + 1) * T)
            pieces = []
            for n in range(NN):
                piece = got[w * NN + n].astype(f32)
                pieces += [piece[:, 0:HD], piece[:, HD:]]
            natural = jnp.concatenate(pieces, axis=0)
            do_nat[at, :] = natural.astype(bf16)
            grad = natural.T
            delta = -jnp.sum(grad * o_t[:, at], axis=0, keepdims=True)
            hi, mid, lo = split3(delta)
            do_t[0:HD, at] = grad.astype(bf16)
            do_t[HD:AUG, at] = jnp.where(
                ext == 0, hi, jnp.where(ext == 1, mid, jnp.where(ext == 2, lo, 0.0))
            ).astype(bf16)
        dq_t[...] = jnp.zeros((HD, L), f32)

        def folded(t):
            total = t[:, 0:T]
            for k in range(1, t.shape[1] // T):
                total = total + t[:, k * T : (k + 1) * T]
            return total

        def tile(j, carry):
            sum_key, sum_value = carry
            at = pl.ds(pl.multiple_of(j * 256, 256), 256)
            p = jnp.exp2(dot(k_nat[at, :], q_t[...], NORMAL))
            dp = dot(v_nat[at, :], do_t[...], NORMAL)
            ds = (p * dp).astype(bf16)
            dv = dot(p.astype(bf16), do_nat[...], NORMAL).T.astype(bf16)
            dk = dot(ds, q_nat[...], NORMAL).T * LN2
            dk = (dk * cos_t[:, at] - swap_pairs(dk) * sin_t[:, at]).astype(bf16)
            dq_t[...] += dot(k_t[0:HD, at], ds, NORMAL)
            for k in range(2):
                out[2 * j + k, HD : 2 * HD, :] = dk[:, k * T : (k + 1) * T]
                out[2 * j + k, 2 * HD : 3 * HD, :] = dv[:, k * T : (k + 1) * T]
            return sum_key + folded(dk.astype(f32)), sum_value + folded(dv.astype(f32))

        zero = jnp.zeros((HD, T), f32)
        sum_key, sum_value = lax.fori_loop(0, L // 256, tile, (zero, zero))
        sum_query = zero
        stores = []
        for w in range(NW):
            at = slice(w * T, (w + 1) * T)
            dq = dq_t[:, at] * (HD**-0.5)
            dq = (dq * cos_t[:, at] - swap_pairs(dq) * sin_t[:, at]).astype(bf16)
            out[w, 0:HD, :] = dq
            stores += copies([(out.at[w, 0 : 3 * HD, :], out_far.at[w, 0 : 3 * HD, :])], sems.at[w:])
            sum_query = sum_query + dq.astype(f32)
        rows = [jnp.sum(t.T, axis=0, keepdims=True) for t in (sum_query, sum_key, sum_value)]
        first = jnp.concatenate([rows[0], rows[1]], axis=1)
        second = jnp.concatenate([rows[2], rows[2]], axis=1)
        first_hi, second_hi = first.astype(bf16).astype(f32), second.astype(bf16).astype(f32)
        block = jnp.where(
            ext == 0,
            first_hi,
            jnp.where(ext == 1, second_hi, jnp.where(ext == 2, first - first_hi, second - second_hi)),
        )
        block = jnp.where(ext < 4, block, 0.0).astype(bf16)
        for w in range(NW):
            out[w, 3 * HD :, :] = block
        for store in stores:
            store.wait()
        stores = copies([(out.at[:, 3 * HD :, :], out_far.at[:, 3 * HD :, :])], sems)
        stores[0].wait()


def chunk_rows(c, r):
    return pl.ds(pl.multiple_of(r * T + c * C, C), C)


def row_mean(t):
    return jnp.mean(t, axis=-1, keepdims=True)


def column_sum(t):
    return jnp.sum(t, axis=0, keepdims=True)


def gelu_and_slope(pre):
    half = 0.5 * (1.0 + lax.erf(pre * (2.0**-0.5)))
    return (pre * half).astype(bf16), half + pre * jnp.exp(-0.5 * pre * pre) * (1.0 / math.sqrt(2.0 * math.pi))


ATTN, NORMED, FIRST = 0, 32, 128
FFN, OUT, SUMS, LAST = 0, 96, 192, 208


def first_kernel(
    w0, m1, m2, m3, u1, u2, u3, x, attn, b_out, g_one, s_one, w_out_far, state_far, pack0, pack1, pack2, pack3,
    w_out, state, heads, packs, sems,
):
    n, c = lax.axis_index("narrow"), lax.axis_index("dp")
    pairs = [(w0, w_out.at[0:E, :])]
    for s, (mine, other) in enumerate(((m1, u1), (m2, u2), (m3, u3)), 1):
        for source, core in ((mine, c), (other, 1 - c)):
            pairs.append((source, w_out.at[pl.ds(pl.multiple_of(s * E + core * (E // 2), E // 2), E // 2), :]))
    loads = copies(pairs, sems)
    for s in range(NN):
        for r in range(R):
            for h in range(NH):
                block = attn[(r * NH + h) * NN + (n + NN - s) % NN]
                at = s * E + h * HD
                heads[r * C : r * C + C // 2, at : at + HD] = block[:, 0:HD]
                heads[r * C + C // 2 : (r + 1) * C, at : at + HD] = block[:, HD:]
    mine = pl.ds(pl.multiple_of(n * C, C), C)
    tokens = jnp.concatenate([x[r, mine, :] for r in range(R)], axis=0).astype(f32)
    for load in loads:
        load.wait()
    stores = copies([(w_out, w_out_far)], sems.at[5:])
    residual = tokens + (dot(heads[...], w_out[...], NORMAL) + row_of(b_out))
    center = residual - row_mean(residual)
    rstd = lax.rsqrt(row_mean(center * center) + EPSILON)
    unit = center * rstd
    state[:, 0:D] = unit
    state[:, D:] = jnp.broadcast_to(rstd, (CH, T))
    stores += copies([(state, state_far)], sems.at[4:])
    low = (unit * row_of(g_one) + row_of(s_one)).astype(bf16)
    for s, pack in enumerate((pack0, pack1, pack2, pack3)):
        packs[s, NORMED:FIRST, :] = low
        for r in range(R):
            packs[s, ATTN:NORMED, 256 * r : 256 * r + E] = heads[r * C : (r + 1) * C, s * E : (s + 1) * E]
        stores.append(pltpu.make_async_copy(packs.at[s], pack, sems.at[s]))
        stores[-1].start()
    for store in stores:
        store.wait()


def middle_kernel(
    every_far, state_far, cot_far, w_out_far, g_one, s_one, b0, b1, b2, b3, b_down, g_two, s_two,
    slots_far, one_far, pack_far, layer_far,
    state, cot, w_out, weights, slope, grad_one, slots, pack, layer, sems,
):
    n = lax.axis_index("narrow")
    first = copies([(state_far, state), (cot_far, cot), (w_out_far, w_out)], sems.at[8:])
    pairs = [(every_far.at[which, :, s], weights.at[which, s]) for which in range(2) for s in range(NN)]
    loads = copies(pairs, sems)
    for load in first:
        load.wait()
    mine = pl.ds(pl.multiple_of(n * C, C), C)
    ct = jnp.concatenate([cot[r, mine, :] for r in range(R)], axis=0).astype(f32)
    unit, rstd = state[:, 0:D], state[:, D : D + 1]
    normed = unit * row_of(g_one) + row_of(s_one)
    low = normed.astype(bf16)

    def weight(which, s):
        return weights[which, s].reshape(D, F)

    total = None
    for s, b in enumerate((b0, b1, b2, b3)):
        loads[s].wait()
        hidden, slope[s] = gelu_and_slope(dot(low, weight(0, s), NORMAL) + row_of(b))
        loads[NN + s].wait()
        term = dot(hidden, weight(1, s), BOTH_LAST)
        total = term if s == 0 else total + term
    residual = normed + (total + row_of(b_down))
    center = residual - row_mean(residual)
    rstd_two = lax.rsqrt(row_mean(center * center) + EPSILON)
    unit_two = center * rstd_two
    layer[...] = (unit_two * row_of(g_two) + row_of(s_two)).astype(bf16)
    scaled = ct * row_of(g_two)
    grad_two = rstd_two * (scaled - row_mean(scaled) - unit_two * row_mean(scaled * unit_two))
    low_two = grad_two.astype(bf16)
    pack[FFN:OUT, :] = low_two
    total = None
    for s in range(NN):
        pre = (slope[s] * dot(low_two, weight(1, s), NORMAL)).astype(bf16)
        term = dot(pre, weight(0, s), BOTH_LAST)
        total = term if s == 0 else total + term
    grad = grad_two + total
    scaled = grad * row_of(g_one)
    one = rstd * (scaled - row_mean(scaled) - unit * row_mean(scaled * unit))
    grad_one[...] = one
    low_one = one.astype(bf16)
    every = dot(low_one, w_out[...], BOTH_LAST)
    for s in range(NN):
        for r in range(R):
            for h in range(NH):
                block = every[r * C : (r + 1) * C, s * E + h * HD : s * E + (h + 1) * HD]
                slot = jnp.concatenate([block[0 : C // 2], block[C // 2 :]], axis=1).astype(bf16)
                slots[(r * NH + h) * NN + (n + NN - s) % NN] = slot
    stores = copies([(slots, slots_far), (grad_one, one_far), (layer, layer_far)], sems)
    pack[OUT:SUMS, :] = low_one
    sums = [ct * unit_two, ct, low_two.astype(f32), grad * unit, grad, low_one.astype(f32)]
    pack[SUMS:LAST, :] = jnp.concatenate([column_sum(t) for t in sums] + [jnp.zeros((10, D), f32)], axis=0).astype(bf16)
    stores += copies([(pack, pack_far)], sems.at[3:])
    for store in stores:
        store.wait()


def halves(whole, send, send_far, keep_far, sems):
    c = lax.axis_index("dp")
    half = D // 2
    send[0:half, :] = whole[pl.ds(pl.multiple_of((1 - c) * half, half), half), :].astype(bf16)
    return copies([(send, send_far), (whole.at[pl.ds(pl.multiple_of(c * half, half), half), :], keep_far)], sems)


def hidden_kernel(a0, a1, a2, a3, every_far, b_up, hidden_far, slope_far, firsts, weights, hidden, slope, sems):
    pairs = [(p, firsts.at[s]) for s, p in enumerate((a0, a1, a2, a3))] + [(every_far.at[0, :, 0], weights)]
    for load in copies(pairs, sems):
        load.wait()
    normed = firsts[:, NORMED:FIRST, :].reshape(TOK, D)
    act, slant = gelu_and_slope(dot(normed, weights[...].reshape(D, F), NORMAL) + row_of(b_up))
    hidden[...] = act
    slope[...] = slant
    for store in copies([(hidden, hidden_far), (slope, slope_far)], sems):
        store.wait()


def weights_kernel(
    a0, a1, a2, a3, p0, p1, p2, p3, every_far, hidden_far, slope_far,
    send0_far, send1_far, send2_far, send3_far, keep_far, out_whole, sums,
    firsts, packs, weights, hidden, slope, whole, send, vectors, sems,
):
    n, c = lax.axis_index("narrow"), lax.axis_index("dp")
    pairs = [(every_far.at[1, :, 0], weights), (slope_far, slope)]
    pairs += [(p, packs.at[s]) for s, p in enumerate((p0, p1, p2, p3))]
    pairs += [(p, firsts.at[s]) for s, p in enumerate((a0, a1, a2, a3))] + [(hidden_far, hidden)]
    loads = copies(pairs, sems)
    for load in loads[:6]:
        load.wait()
    grad_ffn = packs[:, FFN:OUT, :].reshape(TOK, D)
    pre = (slope[...] * dot(grad_ffn, weights[...].reshape(D, F), NORMAL)).astype(bf16)
    for load in loads[6:]:
        load.wait()
    whole[:, 0:F] = dot(firsts[:, NORMED:FIRST, :].reshape(TOK, D), pre, BOTH_FIRST)
    whole[:, F:] = dot(grad_ffn, hidden[...], BOTH_FIRST)
    half = D // 2
    send[...] = whole[pl.ds(pl.multiple_of((1 - c) * half, half), half), :].astype(bf16)
    pairs = [(send.at[96 * k : 96 * (k + 1), :], far) for k, far in enumerate((send0_far, send1_far, send2_far, send3_far))]
    stores = copies([*pairs, (whole.at[pl.ds(pl.multiple_of(c * half, half), half), :], keep_far)], sems)
    heads = [firsts[s, ATTN:NORMED, 256 * r : 256 * r + E] for s in range(NN) for r in range(R)]
    out_whole[...] = dot(packs[:, OUT:SUMS, :].reshape(TOK, D), jnp.concatenate(heads, axis=0), BOTH_FIRST)
    for s in range(NN):
        vectors[(n + NN - s) % NN] = packs[s, SUMS:LAST, :].astype(f32)[0:8, :]
    total = vectors[0] + vectors[1] + vectors[2] + vectors[3]
    row = lax.broadcasted_iota(jnp.int32, (8, D), 0)
    sums[...] = jnp.where(row == 6, column_sum(pre.astype(f32)), total)
    for store in stores:
        store.wait()


def weights_add_kernel(keep_far, got0, got1, got2, got3, slots_far, keep, got, slots, sems):
    pairs = [(far, got.at[96 * k : 96 * (k + 1), :]) for k, far in enumerate((got0, got1, got2, got3))]
    for load in copies([(keep_far, keep), *pairs], sems):
        load.wait()
    both = (keep[...] + got[...].astype(f32)).astype(bf16)
    stores = []
    for w in range(NW):
        slots[w] = both[w * G : (w + 1) * G, :]
        stores.append(pltpu.make_async_copy(slots.at[w], slots_far.at[w, :, 0 : 2 * F], sems.at[w]))
        stores[w].start()
    for store in stores:
        store.wait()


def input_back_kernel(
    x_far, wq, wk, wv, got, out_whole, vec, part0_far, part1_far, part2_far, part3_far, send_far, keep_far, sums,
    part0, part1, part2, part3, whole, send, wide_part, x, near, sems,
):
    n = lax.axis_index("narrow")
    loads = copies([(x_far, x), (wq, near.at[0]), (wk, near.at[1]), (wv, near.at[2])], sems)
    grads = []
    for j in range(3):
        grad_t = jnp.concatenate(
            [
                jnp.concatenate([got[r * NH + h, j * HD : (j + 1) * HD, :] for h in range(NH)], axis=0)
                for r in range(R)
            ],
            axis=1,
        )
        grads.append(grad_t.astype(f32).T.astype(bf16))
    grad = jnp.concatenate(grads, axis=1)
    whole[:, 3 * E :] = out_whole[...]
    loads[0].wait()
    whole[:, 0 : 3 * E] = dot(x[...].reshape(TOK, D), grad, BOTH_FIRST)
    for load in loads[1:]:
        load.wait()
    wide_part[...] = dot(grad, near[...].reshape(3 * E, D), NORMAL)
    for r in range(R):
        to = slice(r * C, (r + 1) * C)
        part0[to, :] = wide_part[chunk_rows(n, r), :]
        for s, part in ((1, part1), (2, part2), (3, part3)):
            part[to, :] = wide_part[chunk_rows((n + s) % NN, r), :].astype(bf16)
    pairs = [(part0, part0_far), (part1, part1_far), (part2, part2_far), (part3, part3_far)]
    stores = copies(pairs, sems)
    heads = []
    for h in range(NH):
        block = got[h, 3 * HD :, :].astype(f32)
        for r in range(1, R):
            block = block + got[r * NH + h, 3 * HD :, :].astype(f32)
        heads.append(block)
    first = jnp.concatenate([b[0:1, 0:HD] + b[2:3, 0:HD] for b in heads], axis=1)
    second = jnp.concatenate([b[0:1, HD:] + b[2:3, HD:] for b in heads], axis=1)
    third = jnp.concatenate([b[1:2, 0:HD] + b[3:4, 0:HD] for b in heads], axis=1)
    row = jnp.concatenate([first, second, third], axis=1)
    sums[...] = row
    hi, mid, lo = split3(jnp.concatenate([row, jnp.zeros((1, E), f32)], axis=1))
    send[D // 2 :, :] = jnp.concatenate([vec[...], hi, mid, lo, jnp.zeros((5, D), f32)], axis=0).astype(bf16)
    for store in stores + halves(whole, send, send_far, keep_far, sems.at[4:]):
        store.wait()


def input_add_kernel(keep_far, got_far, slots_in, sums, vec, slots_far, b_q, b_k, b_v, keep, got, slots, sems):
    for load in copies([(keep_far, keep), (got_far, got)], sems):
        load.wait()
    both = (keep[...] + got[0 : D // 2, :].astype(f32)).astype(bf16)
    more = got[D // 2 :, :].astype(f32)
    rows = vec[...].astype(bf16).astype(f32) + more[0:8, :]
    lanes = D // 3
    rows = jnp.concatenate([rows[:, lanes * k : lanes * (k + 1)] for k in range(3)], axis=0).astype(bf16)
    stores = []
    for w in range(NW):
        slots[w] = jnp.concatenate([both[w * G : (w + 1) * G, :], rows], axis=1)
        stores.append(pltpu.make_async_copy(slots.at[w], slots_far.at[w, :, 2 * F :], sems.at[w]))
        stores[w].start()
    hi, mid, lo = split3(sums[...])
    bias = more[:, 0 : 3 * E]
    total = (hi + bias[8:9, :]) + ((mid + bias[9:10, :]) + (lo + bias[10:11, :]))
    for k, ref in enumerate((b_q, b_k, b_v)):
        ref[...] = total[:, k * E : (k + 1) * E].reshape(E)
    for store in stores:
        store.wait()


def input_sum_kernel(got, g_up, g_down, g_q, g_k, g_v, g_out, g_two, s_two, b_down, g_one, s_one, b_out, b_up):
    total = got[0].astype(f32)
    for w in range(1, NW):
        total = total + got[w].astype(f32)
    g_up[...] = total[:, 0:F]
    g_down[...] = total[:, F : 2 * F]
    for k, ref in enumerate((g_q, g_k, g_v, g_out)):
        ref[...] = total[:, 2 * F + k * E : 2 * F + (k + 1) * E]
    vec = jnp.concatenate([total[8 * k : 8 * (k + 1), 2 * F + D :] for k in range(3)], axis=1)
    for k, ref in enumerate((g_two, s_two, b_down, g_one, s_one, b_out, b_up)):
        ref[...] = vec[k : k + 1, :].reshape(D)


def input_chunk_kernel(part_far, one_far, part1, part2, part3, low, part0, grad_one, sems):
    for load in copies([(part_far, part0), (one_far, grad_one)], sems):
        load.wait()
    total = part0[...] + part1[...].astype(f32) + part2[...].astype(f32) + part3[...].astype(f32)
    low[...] = (grad_one[...] + total).astype(bf16)


def spread_kernel(g0, g1, g2, g3, out):
    n = lax.axis_index("narrow")
    for s, part in enumerate((g0, g1, g2, g3)):
        at = pl.ds(pl.multiple_of((n + NN - s) % NN * C, C), C)
        for r in range(R):
            out[r, at, :] = part[r * C : (r + 1) * C, :].astype(f32)


def shifted(x, s):
    return lax.ppermute(x, "narrow", [(i, (i + s) % NN) for i in range(NN)])


def gather_narrow(x):
    return (x, shifted(x, 1), shifted(x, 2), shifted(x, 3))


def scatter_narrow(parts):
    return (parts[0], shifted(parts[1], 1), shifted(parts[2], 2), shifted(parts[3], 3))


def other_core(x):
    return lax.ppermute(x, "dp", [(0, 1), (1, 0)])


def exchange(slots):
    return lax.all_to_all(slots, "wide", 0, 0, tiled=True)


def exchange_all(slots):
    return lax.all_to_all(slots, ("wide", "narrow"), 0, 0, tiled=True)


def body(
    hidden_in, segments, weight_query, bias_query, weight_key, bias_key, weight_value, bias_value,
    weight_out, bias_out, gain_one, shift_one, weight_up, bias_up, weight_down, bias_down,
    gain_two, shift_two, cotangent,
):
    frequency = np.repeat(np.power(10000.0, -np.arange(0, HD, 2) / HD), 2).astype(np.float32)
    frequency = jnp.asarray(np.broadcast_to(frequency[:, None], (HD, T)))
    shard = jnp.where(lax.axis_index("dp") == 0, weight_up, weight_down.T)
    shards = gather_narrow(shard)
    mine = lax.dynamic_slice_in_dim(weight_out, lax.axis_index("dp") * (E // 2), E // 2, 0)
    weights_got = gather_narrow(mine)[1:]
    weights_out = (weight_out, *weights_got, *(other_core(w) for w in weights_got))
    biases_up = gather_narrow(bias_up)
    query_t, key_t, value_t = weight_query.T, weight_key.T, weight_value.T

    slots, token = call(
        "project",
        project_kernel,
        [((NW, SLOT, T), bf16)],
        (hidden_in, segments, query_t, bias_query, key_t, bias_key, value_t, bias_value),
        scratch=[
            pltpu.VMEM((R, T, D), bf16),
            pltpu.VMEM((3, E, D), bf16),
            pltpu.VMEM((E,), f32),
            pltpu.VMEM((E,), f32),
            pltpu.VMEM((E,), f32),
            pltpu.VMEM((R, T), jnp.int32),
            pltpu.SemaphoreType.DMA((8,)),
        ],
        far_in=range(8),
        token=True,
    )
    (shards,) = call(
        "stack",
        stack_kernel,
        [((NN, D // NW, F), bf16)],
        shards,
        scratch=[pltpu.SemaphoreType.DMA((NN,))],
        any_in=range(NN),
        far=(0,),
        after=(token,),
    )
    every = lax.all_gather(shards, ("dp", "wide")).reshape(2, NW, NN, D // NW, F)
    got = exchange(slots)
    out_slots, q_t, k_t, v_t, o_t, cos_t, sin_t = call(
        "attend",
        attend_kernel,
        [
            ((NW * NN, C // 2, 2 * HD), bf16),
            ((AUG, L), bf16),
            ((AUG, L), bf16),
            ((AUG, L), bf16),
            ((HD, L), f32),
            ((HD, L), f32),
            ((HD, L), f32),
        ],
        (got, frequency),
        scratch=[
            pltpu.VMEM((NW * NN, C // 2, 2 * HD), bf16),
            pltpu.VMEM((AUG, L), bf16),
            pltpu.VMEM((AUG, L), bf16),
            pltpu.VMEM((AUG, L), bf16),
            pltpu.VMEM((HD, L), f32),
            pltpu.VMEM((HD, L), f32),
            pltpu.VMEM((HD, L), f32),
            pltpu.VMEM((L, AUG), bf16),
            pltpu.SemaphoreType.DMA((7,)),
        ],
        after=weights_got,
        far=range(7),
    )
    attn = exchange_all(out_slots)
    chunk_f32, chunk_low = ((CH, D), f32), ((CH, D), bf16)
    parts4 = [chunk_f32, chunk_low, chunk_low, chunk_low]
    slot_shape = (NW * NN, C // 2, 2 * HD)
    w_out, state, *firsts, token = call(
        "first",
        first_kernel,
        [((D, D), bf16), ((CH, D + T), f32)] + [((FIRST, D), bf16)] * NN,
        (*weights_out, hidden_in, attn, bias_out, gain_one, shift_one),
        scratch=[
            pltpu.VMEM((D, D), bf16),
            pltpu.VMEM((CH, D + T), f32),
            pltpu.VMEM((CH, D), bf16),
            pltpu.VMEM((NN, FIRST, D), bf16),
            pltpu.SemaphoreType.DMA((7,)),
        ],
        far_in=range(7),
        far=range(6),
        token=True,
        after=biases_up[1:],
    )
    firsts = (firsts[0], *(shifted(firsts[s], NN - s) for s in range(1, NN)))
    every = later(every, token)
    slots, grad_one, pack, layer = call(
        "middle",
        middle_kernel,
        [(slot_shape, bf16), chunk_f32, ((LAST, D), bf16), chunk_low],
        (every, state, cotangent, w_out, gain_one, shift_one, *biases_up, bias_down, gain_two, shift_two),
        scratch=[
            pltpu.VMEM((CH, D + T), f32),
            pltpu.VMEM((R, T, D), bf16),
            pltpu.VMEM((D, D), bf16),
            pltpu.VMEM((2, NN, NW, D // NW, F), bf16),
            pltpu.VMEM((NN, CH, F), f32),
            pltpu.VMEM((CH, D), f32),
            pltpu.VMEM(slot_shape, bf16),
            pltpu.VMEM((LAST, D), bf16),
            pltpu.VMEM((CH, D), bf16),
            pltpu.SemaphoreType.DMA((11,)),
        ],
        mib=32,
        far_in=range(4),
        far=range(4),
    )
    got = exchange_all(later(slots, *firsts[1:]))
    packs = gather_narrow(pack)
    firsts = (firsts[0], firsts[3], firsts[2], firsts[1])
    hidden, slope, token = call(
        "hidden",
        hidden_kernel,
        [((TOK, F), bf16), ((TOK, F), f32)],
        (*firsts, every, bias_up),
        scratch=[
            pltpu.VMEM((NN, FIRST, D), bf16),
            pltpu.VMEM((NW, D // NW, F), bf16),
            pltpu.VMEM((TOK, F), bf16),
            pltpu.VMEM((TOK, F), f32),
            pltpu.SemaphoreType.DMA((5,)),
        ],
        far_in=range(5),
        far=(0, 1),
        token=True,
    )
    slots, token = call(
        "attend_back",
        attend_back_kernel,
        [((NW, SLOT, T), bf16)],
        (got, o_t, q_t, k_t, v_t, cos_t, sin_t),
        scratch=[
            pltpu.VMEM((NW, SLOT, T), bf16),
            pltpu.VMEM((NW * NN, C // 2, 2 * HD), bf16),
            pltpu.VMEM((HD, L), f32),
            pltpu.VMEM((AUG, L), bf16),
            pltpu.VMEM((AUG, L), bf16),
            pltpu.VMEM((AUG, L), bf16),
            pltpu.VMEM((HD, L), f32),
            pltpu.VMEM((HD, L), f32),
            pltpu.VMEM((AUG, L), bf16),
            pltpu.VMEM((L, HD), bf16),
            pltpu.VMEM((L, HD), bf16),
            pltpu.VMEM((L, AUG), bf16),
            pltpu.VMEM((L, AUG), bf16),
            pltpu.VMEM((HD, L), f32),
            pltpu.SemaphoreType.DMA((NW,)),
        ],
        far_in=range(7),
        far=(0,),
        after=(token, *packs[1:]),
        token=True,
    )
    layers = gather_narrow(later(layer, token))
    whole_out = ((R, T, D), f32)
    *sends, up_keep, out_whole, vec = call(
        "weights",
        weights_kernel,
        [((96, 2 * F), bf16)] * 4 + [((D // 2, 2 * F), f32), ((D, E), f32), ((8, D), f32)],
        (*firsts, *packs, every, hidden, slope),
        scratch=[
            pltpu.VMEM((NN, FIRST, D), bf16),
            pltpu.VMEM((NN, LAST, D), bf16),
            pltpu.VMEM((NW, D // NW, F), bf16),
            pltpu.VMEM((TOK, F), bf16),
            pltpu.VMEM((TOK, F), f32),
            pltpu.VMEM((D, 2 * F), f32),
            pltpu.VMEM((D // 2, 2 * F), bf16),
            pltpu.VMEM((NN, 8, D), f32),
            pltpu.SemaphoreType.DMA((11,)),
        ],
        mib=32,
        far_in=range(11),
        far=range(5),
        after=(token,),
    )
    slots_shape = ((NW, G, 2 * F + D + D // 3), bf16)
    last_slots, added = call(
        "weights_add",
        weights_add_kernel,
        [slots_shape],
        (up_keep, *(other_core(send) for send in sends)),
        scratch=[
            pltpu.VMEM((D // 2, 2 * F), f32),
            pltpu.VMEM((D // 2, 2 * F), bf16),
            pltpu.VMEM((NW, G, 2 * F), bf16),
            pltpu.SemaphoreType.DMA((NW,)),
        ],
        far_in=range(5),
        far=(0,),
        token=True,
    )

    got = exchange(slots)
    *parts, send, keep, sums = call(
        "input_back",
        input_back_kernel,
        [*parts4, ((D // 2 + 16, D), bf16), ((D // 2, D), f32), ((1, 3 * E), f32)],
        (hidden_in, query_t, key_t, value_t, got, out_whole, vec),
        scratch=[
            pltpu.VMEM((CH, D), f32),
            pltpu.VMEM((CH, D), bf16),
            pltpu.VMEM((CH, D), bf16),
            pltpu.VMEM((CH, D), bf16),
            pltpu.VMEM((D, D), f32),
            pltpu.VMEM((D // 2 + 16, D), bf16),
            pltpu.VMEM((TOK, D), f32),
            pltpu.VMEM((R, T, D), bf16),
            pltpu.VMEM((3, E, D), bf16),
            pltpu.SemaphoreType.DMA((6,)),
        ],
        far_in=range(4),
        far=range(6),
        after=(added, *layers[1:]),
    )
    parts = scatter_narrow(parts)
    slots, b_query, b_key, b_value = call(
        "input_add",
        input_add_kernel,
        [slots_shape, ((E,), f32), ((E,), f32), ((E,), f32)],
        (keep, other_core(send), last_slots, sums, vec),
        scratch=[
            pltpu.VMEM((D // 2, D), f32),
            pltpu.VMEM((D // 2 + 16, D), bf16),
            pltpu.VMEM((NW, G, D + D // 3), bf16),
            pltpu.SemaphoreType.DMA((NW,)),
        ],
        any_in=(1,),
        far_in=(0, 2),
        far=(0,),
        aliases={2: 0},
    )
    (input_low,) = call("input_chunk", input_chunk_kernel, [chunk_low], (parts[0], grad_one, *parts[1:]),
        scratch=[pltpu.VMEM((CH, D), f32), pltpu.VMEM((CH, D), f32), pltpu.SemaphoreType.DMA((2,))],
        cost=COST, far_in=(0, 1),
    )
    (layer_out,) = call("layer_out", spread_kernel, [whole_out], layers)
    (grad_input,) = call("grad_input", spread_kernel, [whole_out], gather_narrow(input_low))
    flat = ((D,), f32)
    grad_up, grad_down, g_query, g_key, g_value, g_out, g_two, s_two, b_down, g_one, s_one, b_out, b_up = call(
        "input_sum", input_sum_kernel, [((G, F), f32)] * 2 + [((G, E), f32)] * 4 + [flat] * 7, (exchange(slots),)
    )
    return (
        layer_out, grad_input, g_query, b_query, g_key, b_key, g_value, b_value, g_out.T, b_out,
        g_one, s_one, grad_up, b_up, grad_down.T, b_down, g_two, s_two,
    )


def solution(mesh):
    tokens, whole = P("dp", "wide", None), P()
    column, vector = P(None, "narrow"), P("narrow")
    rows_split, columns_split = P(("dp", "wide"), "narrow"), P("narrow", ("dp", "wide"))
    in_specs = (
        tokens, P("dp", "wide"), column, vector, column, vector, column, vector, P("narrow", None), whole,
        whole, whole, P("wide", "narrow"), vector, P("narrow", "wide"), whole, whole, whole, tokens,
    )
    out_specs = (
        tokens, tokens, rows_split, vector, rows_split, vector, rows_split, vector, columns_split, whole,
        whole, whole, rows_split, vector, columns_split, whole, whole, whole,
    )
    return jax.shard_map(body, mesh=mesh, in_specs=in_specs, out_specs=out_specs, check_vma=False)
```

```python
import functools
import math

import jax
import jax.numpy as jnp
import numpy as np
from jax import lax
from jax.experimental import pallas as pl
from jax.experimental.pallas import tpu as pltpu
from jax.sharding import PartitionSpec as P

D = 768
HD = 64
R = 3
T = 128
NH = 3
E = NH * HD
F = 768
NW = 16
NN = 4
TOK = R * T
L = NW * T
C = T // NN
CH = R * C
PAIRS = R * NH
G = D // (2 * NW)
WG = 1792
QKV = 640
FIRST_ROWS, LAST_ROWS = 14 * G, 6 * G
SLOT = 3 * HD + 16
AUG = HD + 16
EPSILON = 1e-12
BIG = 1e30
LOG2E = math.log2(math.e)
LN2 = math.log(2.0)
COST = 10**11
f32, bf16 = jnp.float32, jnp.bfloat16


def dot(a, b, dims):
    return lax.dot_general(a, b, (dims, ((), ())), preferred_element_type=f32)


NORMAL, BOTH_LAST, BOTH_FIRST = ((1,), (0,)), ((1,), (1,)), ((0,), (0,))


def in_far_memory(arrays):
    return [pltpu.with_memory_space_constraint(a, pltpu.HBM) if a.size > 1024 else a for a in arrays]


def call(
    name, kernel, outs, args, scratch=(), cost=1024, mib=16, after=(), far_in=(), any_in=(), near=(), far=(), aliases={},
    token=False,
):
    if token:
        outs = [*outs, ((8, 128), f32)]

    def run(*refs):
        end = len(args) + len(after)
        if token:
            at = end + len(outs) - 1
            refs[at][...] = jnp.zeros((8, 128), f32)
            refs = refs[:at] + refs[at + 1 :]
        kernel(*refs[: len(args)], *refs[end:])

    def shape(k, s, t):
        return pltpu.VMEM(s, t) if k in near else pltpu.HBM(s, t) if k in far else jax.ShapeDtypeStruct(s, t)

    args = [pltpu.with_memory_space_constraint(a, pltpu.HBM) if k in far_in else a for k, a in enumerate(args)]
    after = in_far_memory(after)
    return pl.pallas_call(
        run,
        out_shape=[shape(k, s, t) for k, (s, t) in enumerate(outs)],
        in_specs=[
            pl.BlockSpec(memory_space=pltpu.HBM if k in far_in else pl.ANY if k in any_in else pltpu.VMEM)
            for k in range(len(args))
        ]
        + [pl.BlockSpec(memory_space=pl.ANY) for _ in after],
        out_specs=[pl.BlockSpec(memory_space=pltpu.HBM if k in far else pltpu.VMEM) for k in range(len(outs))],
        scratch_shapes=list(scratch),
        input_output_aliases=aliases,
        compiler_params=pltpu.CompilerParams(vmem_limit_bytes=mib * 1024 * 1024),
        cost_estimate=pl.CostEstimate(flops=cost, bytes_accessed=1024, transcendentals=0),
        name=name,
    )(*args, *after)


def later(x, *after):
    return pl.pallas_call(
        lambda *refs: None,
        out_shape=jax.ShapeDtypeStruct(x.shape, x.dtype),
        in_specs=[pl.BlockSpec(memory_space=pltpu.HBM)] + [pl.BlockSpec(memory_space=pl.ANY) for _ in after],
        out_specs=pl.BlockSpec(memory_space=pltpu.HBM),
        input_output_aliases={0: 0},
        cost_estimate=pl.CostEstimate(flops=1024, bytes_accessed=1024, transcendentals=0),
        name="later",
    )(x, *in_far_memory(after))


def copies(pairs, sems):
    made = [pltpu.make_async_copy(a, b, sems.at[k]) for k, (a, b) in enumerate(pairs)]
    for copy in made:
        copy.start()
    return made


def row_of(ref):
    return ref[...].reshape(1, ref.shape[-1])


def split3(v):
    hi = v.astype(bf16).astype(f32)
    rest = v - hi
    mid = rest.astype(bf16).astype(f32)
    return hi, mid, (rest - mid).astype(bf16).astype(f32)


def sine_cosine(angle):
    turns = jnp.floor(angle * (2.0 / math.pi) + 0.5)
    r = ((angle - turns * 1.5703125) - turns * 4.837512969970703125e-4) - turns * 7.54978995489188e-8
    z = r * r
    sine = r + r * z * (-1.6666654611e-1 + z * (8.3321608736e-3 + z * -1.9515295891e-4))
    cosine = 1.0 - 0.5 * z + z * z * (4.166664568298827e-2 + z * (-1.388731625493765e-3 + z * 2.443315711809948e-5))
    quarter = turns - 4.0 * jnp.floor(turns * 0.25)
    odd = (quarter == 1.0) | (quarter == 3.0)
    sin_abs = jnp.where(odd, cosine, sine)
    cos_abs = jnp.where(odd, sine, cosine)
    return jnp.where(quarter >= 2.0, -sin_abs, sin_abs), jnp.where((quarter == 1.0) | (quarter == 2.0), -cos_abs, cos_abs)


def swap_pairs(t):
    rows = lax.broadcasted_iota(jnp.int32, t.shape, 0)
    return jnp.where(rows % 2 == 0, pltpu.roll(t, HD - 1, 0), pltpu.roll(t, 1, 0))


def project_kernel(x_far, seg, wq, bq, wk, bk, wv, bv, slots, x, near, bias0, bias1, bias2, ids, sems):
    pairs = [(x_far, x), (wq, near.at[0]), (bq, bias0), (wk, near.at[1]), (bk, bias1)]
    pairs += [(wv, near.at[2]), (bv, bias2), (seg, ids)]
    loads = copies(pairs, sems)
    for load in loads:
        load.wait()
    flat = x[...].reshape(TOK, D)
    for j, b in enumerate((bias0, bias1, bias2)):
        w = near.at[j]
        bias = jnp.broadcast_to(row_of(b), (T, E)).T
        yt = (dot(w[...], flat, BOTH_LAST) + jnp.concatenate([bias] * R, axis=1)).astype(bf16)
        for r in range(R):
            for h in range(NH):
                slots[r * NH + h, j * HD : (j + 1) * HD, :] = yt[h * HD : (h + 1) * HD, r * T : (r + 1) * T]
    for r in range(R):
        block = jnp.broadcast_to(ids[r : r + 1, :].astype(f32), (16, T)).astype(bf16)
        for h in range(NH):
            slots[r * NH + h, 3 * HD :, :] = block


def stack_kernel(a, b, c, d, out, sems):
    for copy in copies([(part, out.at[s]) for s, part in enumerate((a, b, c, d))], sems):
        copy.wait()


def attend_kernel(
    got, freq, out_far, q_far, k_far, v_far, o_far, cos_far, sin_far,
    out, q_t, k_t, v_t, o_t, cos_t, sin_t, k_nat, sems,
):
    @pl.when(lax.axis_index("wide") < PAIRS)
    def _():
        ids = [got[w, 3 * HD :, :].astype(f32)[0:1, :] for w in range(NW)]
        starts = []
        for d in range(1, 5):
            below = jnp.zeros((1, T), f32)
            for w in range(NW):
                below = below + jnp.where(ids[w] < d, 1.0, 0.0)
            starts.append(jnp.sum(below, axis=1, keepdims=True))
        odd = lax.broadcasted_iota(jnp.int32, (HD, T), 0) % 2 == 1
        ext = lax.broadcasted_iota(jnp.int32, (16, T), 0)
        lane = lax.broadcasted_iota(jnp.int32, (1, T), 1).astype(f32)
        for w in range(NW):
            at = slice(w * T, (w + 1) * T)
            start = jnp.zeros((1, T), f32)
            for d in range(1, 5):
                start = jnp.where(ids[w] == d, starts[d - 1], start)
            sine, cosine = sine_cosine(freq[...] * (lane + (w * T) - start))
            sine = jnp.where(odd, sine, -sine)
            cos_t[:, at] = cosine
            sin_t[:, at] = sine
            query = got[w, 0:HD, :].astype(f32)
            key = got[w, HD : 2 * HD, :].astype(f32)
            query = (query * cosine + swap_pairs(query) * sine) * (HD**-0.5 * LOG2E)
            key = key * cosine + swap_pairs(key) * sine
            same = ids[w] == ext.astype(f32)
            doc = ext < 5
            key_ext = jnp.where(doc, jnp.where(same, 1.0, 0.0), jnp.where(ext < 8, 1.0, 0.0))
            q_t[0:HD, at] = query.astype(bf16)
            q_t[HD:AUG, at] = jnp.where(doc, jnp.where(same, 0.0, -BIG), 0.0).astype(bf16)
            k_t[0:HD, at] = key.astype(bf16)
            k_t[HD:AUG, at] = key_ext.astype(bf16)
            k_nat[at, :] = jnp.concatenate([key, key_ext], axis=0).T.astype(bf16)
            v_t[0:HD, at] = got[w, 2 * HD : 3 * HD, :]
            v_t[HD:AUG, at] = jnp.where(ext < 3, 1.0, 0.0).astype(bf16)

        stores = copies([(k_t, k_far), (v_t, v_far), (cos_t, cos_far), (sin_t, sin_far)], sems)

        def tile(i, carry):
            at = pl.ds(pl.multiple_of(i * 256, 256), 256)
            s = dot(k_nat[...], q_t[:, at], NORMAL)
            top = jnp.max(s, axis=0, keepdims=True)
            p = jnp.exp2(s - top).astype(bf16)
            o = dot(v_t[...], p, NORMAL)
            total = o[HD : HD + 1, :]
            o = o[0:HD, :] / total
            o_t[:, at] = o
            natural = o.T
            for j in range(2 * NN):
                block = natural[j * C : (j + 1) * C, :]
                out[2 * NN * i + j] = jnp.concatenate([block[0 : C // 2], block[C // 2 :]], axis=1).astype(bf16)
            hi, mid, lo = split3(-(top + jnp.log(total) * LOG2E))
            rows = lax.broadcasted_iota(jnp.int32, (16, 256), 0)
            more = jnp.where(rows == 5, hi, jnp.where(rows == 6, mid, jnp.where(rows == 7, lo, 0.0)))
            q_t[HD:AUG, at] = (q_t[HD:AUG, at].astype(f32) + more).astype(bf16)
            return carry

        lax.fori_loop(0, L // 256, tile, 0)
        last = [(out, out_far, 4), (q_t, q_far, 5), (o_t, o_far, 6)]
        last = [pltpu.make_async_copy(a, b, sems.at[k]) for a, b, k in last]
        for store in last:
            store.start()
        for store in stores + last:
            store.wait()


def attend_back_kernel(
    got_far, o_far, q_far, k_far, v_far, cos_far, sin_far, out_far,
    out, got, o_t, q_t, k_t, v_t, cos_t, sin_t, do_t, do_nat, q_nat, k_nat, v_nat, dq_t, sems,
):
    @pl.when(lax.axis_index("wide") < PAIRS)
    def _():
        pairs = [(q_far, q_t), (k_far, k_t), (v_far, v_t), (got_far, got), (o_far, o_t), (cos_far, cos_t), (sin_far, sin_t)]
        loads = copies(pairs, sems)
        for load in loads[:3]:
            load.wait()
        ext = lax.broadcasted_iota(jnp.int32, (16, T), 0)
        for w in range(NW):
            at = slice(w * T, (w + 1) * T)
            q_nat[at, :] = q_t[0:HD, at].astype(f32).T.astype(bf16)
            k_nat[at, :] = k_t[:, at].astype(f32).T.astype(bf16)
            v_nat[at, :] = v_t[:, at].astype(f32).T.astype(bf16)
        for load in loads[3:]:
            load.wait()
        for w in range(NW):
            at = slice(w * T, (w + 1) * T)
            pieces = []
            for n in range(NN):
                piece = got[w * NN + n].astype(f32)
                pieces += [piece[:, 0:HD], piece[:, HD:]]
            natural = jnp.concatenate(pieces, axis=0)
            do_nat[at, :] = natural.astype(bf16)
            grad = natural.T
            delta = -jnp.sum(grad * o_t[:, at], axis=0, keepdims=True)
            hi, mid, lo = split3(delta)
            do_t[0:HD, at] = grad.astype(bf16)
            do_t[HD:AUG, at] = jnp.where(
                ext == 0, hi, jnp.where(ext == 1, mid, jnp.where(ext == 2, lo, 0.0))
            ).astype(bf16)
        dq_t[...] = jnp.zeros((HD, L), f32)

        def folded(t):
            total = t[:, 0:T]
            for k in range(1, t.shape[1] // T):
                total = total + t[:, k * T : (k + 1) * T]
            return total

        def tile(j, carry):
            sum_key, sum_value = carry
            at = pl.ds(pl.multiple_of(j * 256, 256), 256)
            p = jnp.exp2(dot(k_nat[at, :], q_t[...], NORMAL))
            dp = dot(v_nat[at, :], do_t[...], NORMAL)
            ds = (p * dp).astype(bf16)
            dv = dot(p.astype(bf16), do_nat[...], NORMAL).T.astype(bf16)
            dk = dot(ds, q_nat[...], NORMAL).T * LN2
            dk = (dk * cos_t[:, at] - swap_pairs(dk) * sin_t[:, at]).astype(bf16)
            dq_t[...] += dot(k_t[0:HD, at], ds, NORMAL)
            for k in range(2):
                out[2 * j + k, HD : 2 * HD, :] = dk[:, k * T : (k + 1) * T]
                out[2 * j + k, 2 * HD : 3 * HD, :] = dv[:, k * T : (k + 1) * T]
            return sum_key + folded(dk.astype(f32)), sum_value + folded(dv.astype(f32))

        zero = jnp.zeros((HD, T), f32)
        sum_key, sum_value = lax.fori_loop(0, L // 256, tile, (zero, zero), unroll=2)
        sum_query = zero
        stores = []
        for w in range(NW):
            at = slice(w * T, (w + 1) * T)
            dq = dq_t[:, at] * (HD**-0.5)
            dq = (dq * cos_t[:, at] - swap_pairs(dq) * sin_t[:, at]).astype(bf16)
            out[w, 0:HD, :] = dq
            stores += copies([(out.at[w, 0 : 3 * HD, :], out_far.at[w, 0 : 3 * HD, :])], sems.at[w:])
            sum_query = sum_query + dq.astype(f32)
        rows = [jnp.sum(t.T, axis=0, keepdims=True) for t in (sum_query, sum_key, sum_value)]
        first = jnp.concatenate([rows[0], rows[1]], axis=1)
        second = jnp.concatenate([rows[2], rows[2]], axis=1)
        first_hi, second_hi = first.astype(bf16).astype(f32), second.astype(bf16).astype(f32)
        block = jnp.where(
            ext == 0,
            first_hi,
            jnp.where(ext == 1, second_hi, jnp.where(ext == 2, first - first_hi, second - second_hi)),
        )
        block = jnp.where(ext < 4, block, 0.0).astype(bf16)
        for w in range(NW):
            out[w, 3 * HD :, :] = block
        for store in stores:
            store.wait()
        stores = copies([(out.at[:, 3 * HD :, :], out_far.at[:, 3 * HD :, :])], sems)
        stores[0].wait()


def chunk_rows(c, r):
    return pl.ds(pl.multiple_of(r * T + c * C, C), C)


def row_mean(t):
    return jnp.mean(t, axis=-1, keepdims=True)


def column_sum(t):
    return jnp.sum(t, axis=0, keepdims=True)


def gelu_and_slope(pre):
    half = 0.5 * (1.0 + lax.erf(pre * (2.0**-0.5)))
    return (pre * half).astype(bf16), half + pre * jnp.exp(-0.5 * pre * pre) * (1.0 / math.sqrt(2.0 * math.pi))


ATTN, NORMED, FIRST = 0, 32, 128
FFN, OUT, SUMS, LAST = 0, 96, 192, 208


def first_kernel(
    w0, m1, m2, m3, u1, u2, u3, x, attn, b_out, g_one, s_one, w_out_far, state_far, pack0, pack1, pack2, pack3,
    w_out, state, heads, packs, sems,
):
    n, c = lax.axis_index("narrow"), lax.axis_index("dp")
    pairs = [(w0, w_out.at[0:E, :])]
    for s, (mine, other) in enumerate(((m1, u1), (m2, u2), (m3, u3)), 1):
        for source, core in ((mine, c), (other, 1 - c)):
            pairs.append((source, w_out.at[pl.ds(pl.multiple_of(s * E + core * (E // 2), E // 2), E // 2), :]))
    loads = copies(pairs, sems)
    for s in range(NN):
        for r in range(R):
            for h in range(NH):
                block = attn[(r * NH + h) * NN + (n + NN - s) % NN]
                at = s * E + h * HD
                heads[r * C : r * C + C // 2, at : at + HD] = block[:, 0:HD]
                heads[r * C + C // 2 : (r + 1) * C, at : at + HD] = block[:, HD:]
    mine = pl.ds(pl.multiple_of(n * C, C), C)
    tokens = jnp.concatenate([x[r, mine, :] for r in range(R)], axis=0).astype(f32)
    for load in loads:
        load.wait()
    stores = copies([(w_out, w_out_far)], sems.at[5:])
    residual = tokens + (dot(heads[...], w_out[...], NORMAL) + row_of(b_out))
    center = residual - row_mean(residual)
    rstd = lax.rsqrt(row_mean(center * center) + EPSILON)
    unit = center * rstd
    state[:, 0:D] = unit
    state[:, D:] = jnp.broadcast_to(rstd, (CH, T))
    stores += copies([(state, state_far)], sems.at[4:])
    low = (unit * row_of(g_one) + row_of(s_one)).astype(bf16)
    for s, pack in enumerate((pack0, pack1, pack2, pack3)):
        packs[s, NORMED:FIRST, :] = low
        for r in range(R):
            packs[s, ATTN:NORMED, 256 * r : 256 * r + E] = heads[r * C : (r + 1) * C, s * E : (s + 1) * E]
        stores.append(pltpu.make_async_copy(packs.at[s], pack, sems.at[s]))
        stores[-1].start()
    for store in stores:
        store.wait()


def middle_kernel(
    every_far, state_far, cot_far, w_out_far, g_one_far, s_one_far, b0_far, b_down_far, g_two_far, s_two_far, b1, b2, b3,
    slots_far, one_far, pack_far, layer_far,
    state, cot, w_out, g_one, s_one, b0, b_down, g_two, s_two,
    weights, slope, grad_one, slots, pack, layer, sems,
):
    n = lax.axis_index("narrow")
    pairs = [(state_far, state), (cot_far, cot), (w_out_far, w_out), (g_one_far, g_one), (s_one_far, s_one)]
    pairs += [(b0_far, b0), (b_down_far, b_down), (g_two_far, g_two), (s_two_far, s_two)]
    first = copies(pairs, sems.at[8:])
    pairs = [(every_far.at[which, :, s], weights.at[which, s]) for which in range(2) for s in range(NN)]
    loads = copies(pairs, sems)
    for load in first:
        load.wait()
    mine = pl.ds(pl.multiple_of(n * C, C), C)
    ct = jnp.concatenate([cot[r, mine, :] for r in range(R)], axis=0).astype(f32)
    unit, rstd = state[:, 0:D], state[:, D : D + 1]
    normed = unit * row_of(g_one) + row_of(s_one)
    low = normed.astype(bf16)

    def weight(which, s):
        return weights[which, s].reshape(D, F)

    total = None
    for s, b in enumerate((b0, b1, b2, b3)):
        loads[s].wait()
        hidden, slope[s] = gelu_and_slope(dot(low, weight(0, s), NORMAL) + row_of(b))
        loads[NN + s].wait()
        term = dot(hidden, weight(1, s), BOTH_LAST)
        total = term if s == 0 else total + term
    residual = normed + (total + row_of(b_down))
    center = residual - row_mean(residual)
    rstd_two = lax.rsqrt(row_mean(center * center) + EPSILON)
    unit_two = center * rstd_two
    layer[...] = (unit_two * row_of(g_two) + row_of(s_two)).astype(bf16)
    scaled = ct * row_of(g_two)
    grad_two = rstd_two * (scaled - row_mean(scaled) - unit_two * row_mean(scaled * unit_two))
    low_two = grad_two.astype(bf16)
    pack[FFN:OUT, :] = low_two
    total = None
    for s in range(NN):
        pre = (slope[s] * dot(low_two, weight(1, s), NORMAL)).astype(bf16)
        term = dot(pre, weight(0, s), BOTH_LAST)
        total = term if s == 0 else total + term
    grad = grad_two + total
    scaled = grad * row_of(g_one)
    one = rstd * (scaled - row_mean(scaled) - unit * row_mean(scaled * unit))
    grad_one[...] = one
    low_one = one.astype(bf16)
    every = dot(low_one, w_out[...], BOTH_LAST)
    for s in range(NN):
        for r in range(R):
            for h in range(NH):
                block = every[r * C : (r + 1) * C, s * E + h * HD : s * E + (h + 1) * HD]
                slot = jnp.concatenate([block[0 : C // 2], block[C // 2 :]], axis=1).astype(bf16)
                slots[(r * NH + h) * NN + (n + NN - s) % NN] = slot
    stores = copies([(slots, slots_far), (grad_one, one_far), (layer, layer_far)], sems)
    pack[OUT:SUMS, :] = low_one
    sums = [ct * unit_two, ct, low_two.astype(f32), grad * unit, grad, low_one.astype(f32)]
    pack[SUMS:LAST, :] = jnp.concatenate([column_sum(t) for t in sums] + [jnp.zeros((10, D), f32)], axis=0).astype(bf16)
    stores += copies([(pack, pack_far)], sems.at[3:])
    for store in stores:
        store.wait()


def hidden_kernel(a0, a1, a2, a3, every_far, b_up, hidden_far, slope_far, firsts, weights, hidden, slope, sems):
    pairs = [(p, firsts.at[s]) for s, p in enumerate((a0, a1, a2, a3))] + [(every_far.at[0, :, 0], weights)]
    for load in copies(pairs, sems):
        load.wait()
    normed = firsts[:, NORMED:FIRST, :].reshape(TOK, D)
    act, slant = gelu_and_slope(dot(normed, weights[...].reshape(D, F), NORMAL) + row_of(b_up))
    hidden[...] = act
    slope[...] = slant
    for store in copies([(hidden, hidden_far), (slope, slope_far)], sems):
        store.wait()


def weights_kernel(
    a0, a1, a2, a3, p0, p1, p2, p3, every_far, hidden_far, slope_far,
    send0_far, send1_far, send2_far, send3_far, keep_far, sums_far,
    firsts, packs, weights, hidden, slope, whole, sums, vectors, sems,
):
    n, c = lax.axis_index("narrow"), lax.axis_index("dp")
    pairs = [(every_far.at[1, :, 0], weights), (slope_far, slope)]
    pairs += [(p, packs.at[s]) for s, p in enumerate((p0, p1, p2, p3))]
    pairs += [(p, firsts.at[s]) for s, p in enumerate((a0, a1, a2, a3))] + [(hidden_far, hidden)]
    loads = copies(pairs, sems)
    for load in loads[:6]:
        load.wait()
    grad_ffn = packs[:, FFN:OUT, :].reshape(TOK, D)
    pre = (slope[...] * dot(grad_ffn, weights[...].reshape(D, F), NORMAL)).astype(bf16)
    for load in loads[6:]:
        load.wait()
    whole[:, 0:F] = dot(firsts[:, NORMED:FIRST, :].reshape(TOK, D), pre, BOTH_FIRST).astype(bf16)
    whole[:, F : 2 * F] = dot(grad_ffn, hidden[...], BOTH_FIRST).astype(bf16)
    heads = [firsts[s, ATTN:NORMED, 256 * r : 256 * r + E] for s in range(NN) for r in range(R)]
    heads = jnp.concatenate(heads, axis=0)
    whole[:, 2 * F : 2 * F + E] = dot(packs[:, OUT:SUMS, :].reshape(TOK, D), heads, BOTH_FIRST).astype(bf16)
    half = D // 2
    pairs = [(whole.at[pl.ds(pl.multiple_of(c * half, half), half), :], keep_far)]
    for k, far in enumerate((send0_far, send1_far, send2_far, send3_far)):
        pairs.append((whole.at[pl.ds(pl.multiple_of((1 - c) * half + 96 * k, 96), 96), :], far))
    stores = copies(pairs, sems)
    for s in range(NN):
        vectors[(n + NN - s) % NN] = packs[s, SUMS:LAST, :].astype(f32)[0:8, :]
    total = vectors[0] + vectors[1] + vectors[2] + vectors[3]
    row = lax.broadcasted_iota(jnp.int32, (8, D), 0)
    sums[...] = jnp.where(row == 6, column_sum(pre.astype(f32)), total)
    stores += copies([(sums, sums_far)], sems.at[5:])
    for store in stores:
        store.wait()


def blocks_of(block):
    return jnp.concatenate([block[:, k : k + T] for k in range(0, block.shape[1], T)], axis=0).astype(bf16)


def input_weights_kernel(x_far, got, grad, send_far, keep_far, sums, whole, bias, x, sems):
    c = lax.axis_index("dp")
    load = copies([(x_far, x)], sems)[0]
    grads = []
    for j in range(3):
        grad_t = jnp.concatenate(
            [
                jnp.concatenate([got[r * NH + h, j * HD : (j + 1) * HD, :] for h in range(NH)], axis=0)
                for r in range(R)
            ],
            axis=1,
        )
        grads.append(grad_t.astype(f32).T.astype(bf16))
    grads = jnp.concatenate(grads, axis=1)
    grad[...] = grads
    heads = []
    for h in range(NH):
        block = got[h, 3 * HD :, :].astype(f32)
        for r in range(1, R):
            block = block + got[r * NH + h, 3 * HD :, :].astype(f32)
        heads.append(block)
    first = jnp.concatenate([b[0:1, 0:HD] + b[2:3, 0:HD] for b in heads], axis=1)
    second = jnp.concatenate([b[0:1, HD:] + b[2:3, HD:] for b in heads], axis=1)
    third = jnp.concatenate([b[1:2, 0:HD] + b[3:4, 0:HD] for b in heads], axis=1)
    row = jnp.concatenate([first, second, third], axis=1)
    sums[...] = row
    hi, mid, lo = split3(row)
    bias[:, 0 : 3 * E] = jnp.concatenate([hi, mid, lo, jnp.zeros((13, 3 * E), f32)], axis=0).astype(bf16)
    load.wait()
    whole[:, 0 : 3 * E] = dot(x[...].reshape(TOK, D), grads, BOTH_FIRST).astype(bf16)
    half = D // 2
    pairs = [(bias, send_far.at[half:, :])]
    pairs.append((whole.at[pl.ds(pl.multiple_of((1 - c) * half, half), half), :], send_far.at[0:half, :]))
    pairs.append((whole.at[pl.ds(pl.multiple_of(c * half, half), half), :], keep_far))
    for store in copies(pairs, sems):
        store.wait()


def input_back_kernel(
    wq, wk, wv, grad, part0_far, part1_far, part2_far, part3_far, part0, part1, part2, part3, wide_part, near, sems
):
    n = lax.axis_index("narrow")
    for load in copies([(wq, near.at[0]), (wk, near.at[1]), (wv, near.at[2])], sems):
        load.wait()
    wide_part[...] = dot(grad[...], near[...].reshape(3 * E, D), NORMAL)
    for r in range(R):
        to = slice(r * C, (r + 1) * C)
        part0[to, :] = wide_part[chunk_rows(n, r), :]
        for s, part in ((1, part1), (2, part2), (3, part3)):
            part[to, :] = wide_part[chunk_rows((n + s) % NN, r), :].astype(bf16)
    pairs = [(part0, part0_far), (part1, part1_far), (part2, part2_far), (part3, part3_far)]
    for store in copies(pairs, sems):
        store.wait()


def blocks_of(block):
    return jnp.concatenate([block[:, k : k + T] for k in range(0, block.shape[1], T)], axis=0).astype(bf16)


def slot_sums(vec, vec_got):
    rows = vec[...] + vec_got[...]
    lanes = D // 3
    return jnp.concatenate([rows[:, lanes * k : lanes * (k + 1)] for k in range(3)], axis=0)


def first_add_kernel(
    keep_far, vec_far, got0, got1, got2, got3, vec_got_far, slots_far, tail, keep, got, vec, vec_got, slots, sems
):
    pairs = [(far, got.at[96 * k : 96 * (k + 1), :]) for k, far in enumerate((got0, got1, got2, got3))]
    pairs += [(vec_far, vec), (vec_got_far, vec_got), (keep_far, keep)]
    for load in copies(pairs, sems):
        load.wait()
    rows = slot_sums(vec, vec_got)
    lanes = 2 * F + T
    stores = []
    for w in range(NW):
        at = slice(w * G, (w + 1) * G)
        both = keep[at, :].astype(f32) + got[at, :].astype(f32)
        slots[w] = blocks_of(jnp.concatenate([both[:, 0:lanes], rows[:, 0:T]], axis=1))
        tail[at, :] = jnp.concatenate([both[:, lanes : lanes + HD], rows[:, T : T + HD]], axis=1)
        tail[D // 2 + w * G : D // 2 + (w + 1) * G, :] = jnp.concatenate([rows[:, T + HD :], rows[:, T + HD :]], axis=1)
        stores += copies([(slots.at[w], slots_far.at[w, 0:FIRST_ROWS, :])], sems.at[w:])
    for store in stores:
        store.wait()


def last_add_kernel(
    qkv_far, slots_in, qkv_got_far, tail, sums, slots_far, b_q, b_k, b_v, qkv, qkv_got, slots, sems
):
    for load in copies([(qkv_far, qkv), (qkv_got_far, qkv_got)], sems):
        load.wait()
    stores = []
    for w in range(NW):
        at = slice(w * G, (w + 1) * G)
        other = slice(D // 2 + w * G, D // 2 + (w + 1) * G)
        both = qkv[at, 0 : 3 * E].astype(f32) + qkv_got[at, 0 : 3 * E].astype(f32)
        parts = [tail[at, 0:HD], both, tail[at, HD:], tail[other, 0:HD]]
        slots[w] = blocks_of(jnp.concatenate(parts, axis=1))
        stores += copies([(slots.at[w], slots_far.at[w, FIRST_ROWS:, :])], sems.at[w:])
    bias = qkv_got[D // 2 :, 0 : 3 * E].astype(f32)
    hi, mid, lo = split3(sums[...])
    total = (hi + bias[0:1, :]) + ((mid + bias[1:2, :]) + (lo + bias[2:3, :]))
    for k, ref in enumerate((b_q, b_k, b_v)):
        ref[...] = total[:, k * E : (k + 1) * E].reshape(E)
    for store in stores:
        store.wait()


def last_sum_kernel(got, g_q, g_k, g_v, up, down, out, g_two, s_two, b_down, g_one, s_one, b_out, b_up):
    total = got[0].astype(f32)
    for w in range(1, NW):
        total = total + got[w].astype(f32)
    total = jnp.concatenate([total[k : k + G, :] for k in range(0, FIRST_ROWS + LAST_ROWS, G)], axis=1)
    up[...] = total[:, 0:F]
    down[...] = total[:, F : 2 * F]
    lanes = 2 * F + T
    out[...] = jnp.concatenate([total[:, 2 * F : lanes], total[:, lanes + T : lanes + T + HD]], axis=1)
    begin = lanes + T + HD
    for k, ref in enumerate((g_q, g_k, g_v)):
        ref[...] = total[:, begin + k * E : begin + (k + 1) * E]
    rows = jnp.concatenate([total[:, lanes : lanes + T], total[:, begin + 3 * E :]], axis=1)
    vec = jnp.concatenate([rows[8 * k : 8 * (k + 1), :] for k in range(3)], axis=1)
    for k, ref in enumerate((g_two, s_two, b_down, g_one, s_one, b_out, b_up)):
        ref[...] = vec[k : k + 1, :].reshape(D)


def input_chunk_kernel(part_far, one_far, part1, part2, part3, low, part0, grad_one, sems):
    for load in copies([(part_far, part0), (one_far, grad_one)], sems):
        load.wait()
    total = part0[...] + part1[...].astype(f32) + part2[...].astype(f32) + part3[...].astype(f32)
    low[...] = (grad_one[...] + total).astype(bf16)


def spread_kernel(g0, g1, g2, g3, out):
    n = lax.axis_index("narrow")
    for s, part in enumerate((g0, g1, g2, g3)):
        at = pl.ds(pl.multiple_of((n + NN - s) % NN * C, C), C)
        for r in range(R):
            out[r, at, :] = part[r * C : (r + 1) * C, :].astype(f32)


def shifted(x, s):
    return lax.ppermute(x, "narrow", [(i, (i + s) % NN) for i in range(NN)])


def gather_narrow(x):
    return (x, shifted(x, 1), shifted(x, 2), shifted(x, 3))


def scatter_narrow(parts):
    return (parts[0], shifted(parts[1], 1), shifted(parts[2], 2), shifted(parts[3], 3))


def other_core(x):
    return lax.ppermute(x, "dp", [(0, 1), (1, 0)])


def exchange(slots):
    return lax.all_to_all(slots, "wide", 0, 0, tiled=True)


def exchange_all(slots):
    return lax.all_to_all(slots, ("wide", "narrow"), 0, 0, tiled=True)


def body(
    hidden_in, segments, weight_query, bias_query, weight_key, bias_key, weight_value, bias_value,
    weight_out, bias_out, gain_one, shift_one, weight_up, bias_up, weight_down, bias_down,
    gain_two, shift_two, cotangent,
):
    frequency = np.repeat(np.power(10000.0, -np.arange(0, HD, 2) / HD), 2).astype(np.float32)
    frequency = jnp.asarray(np.broadcast_to(frequency[:, None], (HD, T)))
    shard = jnp.where(lax.axis_index("dp") == 0, weight_up, weight_down.T)
    shards = gather_narrow(shard)
    mine = lax.dynamic_slice_in_dim(weight_out, lax.axis_index("dp") * (E // 2), E // 2, 0)
    weights_got = gather_narrow(mine)[1:]
    weights_out = (weight_out, *weights_got, *(other_core(w) for w in weights_got))
    biases_up = gather_narrow(bias_up)
    query_t, key_t, value_t = weight_query.T, weight_key.T, weight_value.T

    slots, token = call(
        "project",
        project_kernel,
        [((NW, SLOT, T), bf16)],
        (hidden_in, segments, query_t, bias_query, key_t, bias_key, value_t, bias_value),
        scratch=[
            pltpu.VMEM((R, T, D), bf16),
            pltpu.VMEM((3, E, D), bf16),
            pltpu.VMEM((E,), f32),
            pltpu.VMEM((E,), f32),
            pltpu.VMEM((E,), f32),
            pltpu.VMEM((R, T), jnp.int32),
            pltpu.SemaphoreType.DMA((8,)),
        ],
        far_in=range(8),
        token=True,
    )
    (shards,) = call(
        "stack",
        stack_kernel,
        [((NN, D // NW, F), bf16)],
        shards,
        scratch=[pltpu.SemaphoreType.DMA((NN,))],
        any_in=range(NN),
        far=(0,),
        after=(token,),
    )
    every = lax.all_gather(shards, ("dp", "wide")).reshape(2, NW, NN, D // NW, F)
    got = exchange(slots)
    out_slots, q_t, k_t, v_t, o_t, cos_t, sin_t = call(
        "attend",
        attend_kernel,
        [
            ((NW * NN, C // 2, 2 * HD), bf16),
            ((AUG, L), bf16),
            ((AUG, L), bf16),
            ((AUG, L), bf16),
            ((HD, L), f32),
            ((HD, L), f32),
            ((HD, L), f32),
        ],
        (got, frequency),
        scratch=[
            pltpu.VMEM((NW * NN, C // 2, 2 * HD), bf16),
            pltpu.VMEM((AUG, L), bf16),
            pltpu.VMEM((AUG, L), bf16),
            pltpu.VMEM((AUG, L), bf16),
            pltpu.VMEM((HD, L), f32),
            pltpu.VMEM((HD, L), f32),
            pltpu.VMEM((HD, L), f32),
            pltpu.VMEM((L, AUG), bf16),
            pltpu.SemaphoreType.DMA((7,)),
        ],
        after=weights_got,
        far=range(7),
    )
    attn = exchange_all(out_slots)
    chunk_f32, chunk_low = ((CH, D), f32), ((CH, D), bf16)
    parts4 = [chunk_f32, chunk_low, chunk_low, chunk_low]
    slot_shape = (NW * NN, C // 2, 2 * HD)
    w_out, state, *firsts, token = call(
        "first",
        first_kernel,
        [((D, D), bf16), ((CH, D + T), f32)] + [((FIRST, D), bf16)] * NN,
        (*weights_out, hidden_in, attn, bias_out, gain_one, shift_one),
        scratch=[
            pltpu.VMEM((D, D), bf16),
            pltpu.VMEM((CH, D + T), f32),
            pltpu.VMEM((CH, D), bf16),
            pltpu.VMEM((NN, FIRST, D), bf16),
            pltpu.SemaphoreType.DMA((7,)),
        ],
        far_in=range(7),
        far=range(6),
        token=True,
        after=biases_up[1:],
    )
    firsts = (firsts[0], *(shifted(firsts[s], NN - s) for s in range(1, NN)))
    every = later(every, token)
    slots, grad_one, pack, layer = call(
        "middle",
        middle_kernel,
        [(slot_shape, bf16), chunk_f32, ((LAST, D), bf16), chunk_low],
        (
            every, state, cotangent, w_out, gain_one, shift_one, biases_up[0], bias_down, gain_two, shift_two,
            *biases_up[1:],
        ),
        scratch=[
            pltpu.VMEM((CH, D + T), f32),
            pltpu.VMEM((R, T, D), bf16),
            pltpu.VMEM((D, D), bf16),
            *[pltpu.VMEM((D,), f32)] * 6,
            pltpu.VMEM((2, NN, NW, D // NW, F), bf16),
            pltpu.VMEM((NN, CH, F), f32),
            pltpu.VMEM((CH, D), f32),
            pltpu.VMEM(slot_shape, bf16),
            pltpu.VMEM((LAST, D), bf16),
            pltpu.VMEM((CH, D), bf16),
            pltpu.SemaphoreType.DMA((17,)),
        ],
        mib=32,
        far_in=range(10),
        far=range(4),
    )
    got = exchange_all(later(slots, *firsts[1:]))
    packs = gather_narrow(pack)
    firsts = (firsts[0], firsts[3], firsts[2], firsts[1])
    hidden, slope, token = call(
        "hidden",
        hidden_kernel,
        [((TOK, F), bf16), ((TOK, F), f32)],
        (*firsts, every, bias_up),
        scratch=[
            pltpu.VMEM((NN, FIRST, D), bf16),
            pltpu.VMEM((NW, D // NW, F), bf16),
            pltpu.VMEM((TOK, F), bf16),
            pltpu.VMEM((TOK, F), f32),
            pltpu.SemaphoreType.DMA((5,)),
        ],
        far_in=range(5),
        far=(0, 1),
        token=True,
    )
    slots, token = call(
        "attend_back",
        attend_back_kernel,
        [((NW, SLOT, T), bf16)],
        (got, o_t, q_t, k_t, v_t, cos_t, sin_t),
        scratch=[
            pltpu.VMEM((NW, SLOT, T), bf16),
            pltpu.VMEM((NW * NN, C // 2, 2 * HD), bf16),
            pltpu.VMEM((HD, L), f32),
            pltpu.VMEM((AUG, L), bf16),
            pltpu.VMEM((AUG, L), bf16),
            pltpu.VMEM((AUG, L), bf16),
            pltpu.VMEM((HD, L), f32),
            pltpu.VMEM((HD, L), f32),
            pltpu.VMEM((AUG, L), bf16),
            pltpu.VMEM((L, HD), bf16),
            pltpu.VMEM((L, HD), bf16),
            pltpu.VMEM((L, AUG), bf16),
            pltpu.VMEM((L, AUG), bf16),
            pltpu.VMEM((HD, L), f32),
            pltpu.SemaphoreType.DMA((NW,)),
        ],
        any_in=(0,),
        far_in=range(1, 7),
        far=(0,),
        after=(token, *packs[1:]),
        token=True,
    )
    *sends, up_keep, vec = call(
        "weights",
        weights_kernel,
        [((96, WG), bf16)] * 4 + [((D // 2, WG), bf16), ((8, D), f32)],
        (*firsts, *packs, every, hidden, slope),
        scratch=[
            pltpu.VMEM((NN, FIRST, D), bf16),
            pltpu.VMEM((NN, LAST, D), bf16),
            pltpu.VMEM((NW, D // NW, F), bf16),
            pltpu.VMEM((TOK, F), bf16),
            pltpu.VMEM((TOK, F), f32),
            pltpu.VMEM((D, WG), bf16),
            pltpu.VMEM((8, D), f32),
            pltpu.VMEM((NN, 8, D), f32),
            pltpu.SemaphoreType.DMA((11,)),
        ],
        mib=32,
        far_in=range(11),
        far=range(6),
        after=(token,),
    )
    got = exchange(slots)
    last_shape = (NW, FIRST_ROWS + LAST_ROWS, T)
    slots, tail, added = call(
        "first_add",
        first_add_kernel,
        [(last_shape, bf16), ((D, T), f32)],
        (up_keep, vec, *(other_core(send) for send in sends), other_core(vec)),
        scratch=[
            pltpu.VMEM((D // 2, WG), bf16),
            pltpu.VMEM((D // 2, WG), bf16),
            pltpu.VMEM((8, D), f32),
            pltpu.VMEM((8, D), f32),
            pltpu.VMEM((NW, FIRST_ROWS, T), bf16),
            pltpu.SemaphoreType.DMA((NW,)),
        ],
        far_in=range(2),
        any_in=range(2, 7),
        far=(0,),
        token=True,
    )
    grad, send, keep, sums = call(
        "input_weights",
        input_weights_kernel,
        [((TOK, 3 * E), bf16), ((D // 2 + 16, QKV), bf16), ((D // 2, QKV), bf16), ((1, 3 * E), f32)],
        (hidden_in, got),
        scratch=[
            pltpu.VMEM((D, QKV), bf16),
            pltpu.VMEM((16, QKV), bf16),
            pltpu.VMEM((R, T, D), bf16),
            pltpu.SemaphoreType.DMA((3,)),
        ],
        far_in=(0,),
        far=(1, 2),
        after=(added,),
    )
    parts = call(
        "input_back",
        input_back_kernel,
        parts4,
        (query_t, key_t, value_t, grad),
        scratch=[
            pltpu.VMEM((CH, D), f32),
            pltpu.VMEM((CH, D), bf16),
            pltpu.VMEM((CH, D), bf16),
            pltpu.VMEM((CH, D), bf16),
            pltpu.VMEM((TOK, D), f32),
            pltpu.VMEM((3, E, D), bf16),
            pltpu.SemaphoreType.DMA((4,)),
        ],
        far_in=range(3),
        far=range(4),
    )
    parts = scatter_narrow(parts)
    slots, b_query, b_key, b_value = call(
        "last_add",
        last_add_kernel,
        [(last_shape, bf16), ((E,), f32), ((E,), f32), ((E,), f32)],
        (keep, slots, other_core(send), tail, sums),
        scratch=[
            pltpu.VMEM((D // 2, QKV), bf16),
            pltpu.VMEM((D // 2 + 16, QKV), bf16),
            pltpu.VMEM((NW, LAST_ROWS, T), bf16),
            pltpu.SemaphoreType.DMA((NW,)),
        ],
        far_in=range(2),
        any_in=(2,),
        far=(0,),
        aliases={1: 0},
    )
    (input_low,) = call("input_chunk", input_chunk_kernel, [chunk_low], (parts[0], grad_one, *parts[1:]),
        scratch=[pltpu.VMEM((CH, D), f32), pltpu.VMEM((CH, D), f32), pltpu.SemaphoreType.DMA((2,))],
        cost=COST, far_in=(0, 1),
    )
    layers = gather_narrow(later(layer, parts[2]))
    whole_out = ((R, T, D), f32)
    (layer_out,) = call("layer_out", spread_kernel, [whole_out], layers)
    (grad_input,) = call("grad_input", spread_kernel, [whole_out], gather_narrow(input_low))
    flat = ((D,), f32)
    g_query, g_key, g_value, grad_up, grad_down, g_out, g_two, s_two, b_down, g_one, s_one, b_out, b_up = call(
        "last_sum",
        last_sum_kernel,
        [((G, E), f32)] * 3 + [((G, F), f32)] * 2 + [((G, E), f32)] + [flat] * 7,
        (exchange(slots),),
    )
    return (
        layer_out, grad_input, g_query, b_query, g_key, b_key, g_value, b_value, g_out.T, b_out,
        g_one, s_one, grad_up, b_up, grad_down.T, b_down, g_two, s_two,
    )


def solution(mesh):
    tokens, whole = P("dp", "wide", None), P()
    column, vector = P(None, "narrow"), P("narrow")
    rows_split, columns_split = P(("dp", "wide"), "narrow"), P("narrow", ("dp", "wide"))
    in_specs = (
        tokens, P("dp", "wide"), column, vector, column, vector, column, vector, P("narrow", None), whole,
        whole, whole, P("wide", "narrow"), vector, P("narrow", "wide"), whole, whole, whole, tokens,
    )
    out_specs = (
        tokens, tokens, rows_split, vector, rows_split, vector, rows_split, vector, columns_split, whole,
        whole, whole, rows_split, vector, columns_split, whole, whole, whole,
    )
    return jax.shard_map(body, mesh=mesh, in_specs=in_specs, out_specs=out_specs, check_vma=False)
```

```python
import functools
import math

import jax
import jax.numpy as jnp
import numpy as np
from jax import lax
from jax.experimental import pallas as pl
from jax.experimental.pallas import tpu as pltpu
from jax.sharding import PartitionSpec as P

D = 768
HD = 64
R = 3
T = 128
NH = 3
E = NH * HD
F = 768
NW = 16
NN = 4
TOK = R * T
L = NW * T
C = T // NN
CH = R * C
PAIRS = R * NH
G = D // (2 * NW)
FIRST_ROWS, LAST_ROWS, BIAS_ROWS = 12 * G, 6 * G, 16
SLOT = 3 * HD + 16
VECTORS = 8 * D // T
AUG = HD + 16
EPSILON = 1e-12
BIG = 1e30
LOG2E = math.log2(math.e)
LN2 = math.log(2.0)
COST = 10**11
f32, bf16 = jnp.float32, jnp.bfloat16


def dot(a, b, dims):
    return lax.dot_general(a, b, (dims, ((), ())), preferred_element_type=f32)


NORMAL, BOTH_LAST, BOTH_FIRST = ((1,), (0,)), ((1,), (1,)), ((0,), (0,))


def in_far_memory(arrays):
    return [pltpu.with_memory_space_constraint(a, pltpu.HBM) if a.size > 1024 else a for a in arrays]


def call(
    name, kernel, outs, args, scratch=(), cost=1024, mib=16, after=(), far_in=(), any_in=(), near=(), far=(), aliases={},
    token=False,
):
    if token:
        outs = [*outs, ((8, 128), f32)]

    def run(*refs):
        end = len(args) + len(after)
        if token:
            at = end + len(outs) - 1
            refs[at][...] = jnp.zeros((8, 128), f32)
            refs = refs[:at] + refs[at + 1 :]
        kernel(*refs[: len(args)], *refs[end:])

    def shape(k, s, t):
        return pltpu.VMEM(s, t) if k in near else pltpu.HBM(s, t) if k in far else jax.ShapeDtypeStruct(s, t)

    args = [pltpu.with_memory_space_constraint(a, pltpu.HBM) if k in far_in else a for k, a in enumerate(args)]
    after = in_far_memory(after)
    return pl.pallas_call(
        run,
        out_shape=[shape(k, s, t) for k, (s, t) in enumerate(outs)],
        in_specs=[
            pl.BlockSpec(memory_space=pltpu.HBM if k in far_in else pl.ANY if k in any_in else pltpu.VMEM)
            for k in range(len(args))
        ]
        + [pl.BlockSpec(memory_space=pl.ANY) for _ in after],
        out_specs=[pl.BlockSpec(memory_space=pltpu.HBM if k in far else pltpu.VMEM) for k in range(len(outs))],
        scratch_shapes=list(scratch),
        input_output_aliases=aliases,
        compiler_params=pltpu.CompilerParams(vmem_limit_bytes=mib * 1024 * 1024),
        cost_estimate=pl.CostEstimate(flops=cost, bytes_accessed=1024, transcendentals=0),
        name=name,
    )(*args, *after)


def later(x, *after, anywhere=()):
    after = [*in_far_memory(after), *anywhere]
    return pl.pallas_call(
        lambda *refs: None,
        out_shape=jax.ShapeDtypeStruct(x.shape, x.dtype),
        in_specs=[pl.BlockSpec(memory_space=pltpu.HBM)] + [pl.BlockSpec(memory_space=pl.ANY) for _ in after],
        out_specs=pl.BlockSpec(memory_space=pltpu.HBM),
        input_output_aliases={0: 0},
        cost_estimate=pl.CostEstimate(flops=1024, bytes_accessed=1024, transcendentals=0),
        name="later",
    )(x, *after)


def copies(pairs, sems):
    made = [pltpu.make_async_copy(a, b, sems.at[k]) for k, (a, b) in enumerate(pairs)]
    for copy in made:
        copy.start()
    return made


def row_of(ref):
    return ref[...].reshape(1, ref.shape[-1])


def split3(v):
    hi = v.astype(bf16).astype(f32)
    rest = v - hi
    mid = rest.astype(bf16).astype(f32)
    return hi, mid, (rest - mid).astype(bf16).astype(f32)


def sine_cosine(angle):
    turns = jnp.floor(angle * (2.0 / math.pi) + 0.5)
    r = ((angle - turns * 1.5703125) - turns * 4.837512969970703125e-4) - turns * 7.54978995489188e-8
    z = r * r
    sine = r + r * z * (-1.6666654611e-1 + z * (8.3321608736e-3 + z * -1.9515295891e-4))
    cosine = 1.0 - 0.5 * z + z * z * (4.166664568298827e-2 + z * (-1.388731625493765e-3 + z * 2.443315711809948e-5))
    quarter = turns - 4.0 * jnp.floor(turns * 0.25)
    odd = (quarter == 1.0) | (quarter == 3.0)
    sin_abs = jnp.where(odd, cosine, sine)
    cos_abs = jnp.where(odd, sine, cosine)
    return jnp.where(quarter >= 2.0, -sin_abs, sin_abs), jnp.where((quarter == 1.0) | (quarter == 2.0), -cos_abs, cos_abs)


def swap_pairs(t):
    rows = lax.broadcasted_iota(jnp.int32, t.shape, 0)
    return jnp.where(rows % 2 == 0, pltpu.roll(t, HD - 1, 0), pltpu.roll(t, 1, 0))


def project_kernel(x_far, seg, wq, bq, wk, bk, wv, bv, slots, x, near, bias0, bias1, bias2, ids, sems):
    pairs = [(x_far, x), (wq, near.at[0]), (bq, bias0), (wk, near.at[1]), (bk, bias1)]
    pairs += [(wv, near.at[2]), (bv, bias2), (seg, ids)]
    loads = copies(pairs, sems)
    for load in loads:
        load.wait()
    flat = x[...].reshape(TOK, D)
    for j, b in enumerate((bias0, bias1, bias2)):
        w = near.at[j]
        bias = jnp.broadcast_to(row_of(b), (T, E)).T
        yt = (dot(w[...], flat, BOTH_LAST) + jnp.concatenate([bias] * R, axis=1)).astype(bf16)
        for r in range(R):
            for h in range(NH):
                slots[r * NH + h, j * HD : (j + 1) * HD, :] = yt[h * HD : (h + 1) * HD, r * T : (r + 1) * T]
    for r in range(R):
        block = jnp.broadcast_to(ids[r : r + 1, :].astype(f32), (16, T)).astype(bf16)
        for h in range(NH):
            slots[r * NH + h, 3 * HD :, :] = block


def stack_kernel(a, b, c, d, out, sems):
    for copy in copies([(part, out.at[s]) for s, part in enumerate((a, b, c, d))], sems):
        copy.wait()


def attend_kernel(
    got, freq, out_far, q_far, k_far, qn_far, kn_far, vn_far, o_far, cos_far, sin_far,
    out, q_t, k_t, v_t, q_nat, k_nat, v_nat, o_t, cos_t, sin_t, s_even, s_odd, lse_t, sems,
):
    @pl.when(lax.axis_index("wide") < PAIRS)
    def _():
        ids = [got[w, 3 * HD :, :].astype(f32)[0:1, :] for w in range(NW)]
        starts = []
        for d in range(1, 5):
            below = jnp.zeros((1, T), f32)
            for w in range(NW):
                below = below + jnp.where(ids[w] < d, 1.0, 0.0)
            starts.append(jnp.sum(below, axis=1, keepdims=True))
        odd = lax.broadcasted_iota(jnp.int32, (HD, T), 0) % 2 == 1
        ext = lax.broadcasted_iota(jnp.int32, (16, T), 0)
        lane = lax.broadcasted_iota(jnp.int32, (1, T), 1).astype(f32)
        for w in range(NW):
            at = slice(w * T, (w + 1) * T)
            start = jnp.zeros((1, T), f32)
            for d in range(1, 5):
                start = jnp.where(ids[w] == d, starts[d - 1], start)
            sine, cosine = sine_cosine(freq[...] * (lane + (w * T) - start))
            sine = jnp.where(odd, sine, -sine)
            cos_t[:, at] = cosine
            sin_t[:, at] = sine
            query = got[w, 0:HD, :].astype(f32)
            key = got[w, HD : 2 * HD, :].astype(f32)
            query = (query * cosine + swap_pairs(query) * sine) * (HD**-0.5 * LOG2E)
            key = key * cosine + swap_pairs(key) * sine
            same = ids[w] == ext.astype(f32)
            doc = ext < 5
            key_ext = jnp.where(doc, jnp.where(same, 1.0, 0.0), jnp.where(ext < 8, 1.0, 0.0))
            q_t[0:HD, at] = query.astype(bf16)
            q_t[HD:AUG, at] = jnp.where(doc, jnp.where(same, 0.0, -BIG), 0.0).astype(bf16)
            k_t[0:HD, at] = key.astype(bf16)
            k_t[HD:AUG, at] = key_ext.astype(bf16)
            k_nat[at, :] = jnp.concatenate([key, key_ext], axis=0).T.astype(bf16)
            value = got[w, 2 * HD : 3 * HD, :].astype(f32)
            value = jnp.concatenate([value, jnp.where(ext < 3, 1.0, 0.0)], axis=0)
            v_t[:, at] = value.astype(bf16)
            v_nat[at, :] = value.T.astype(bf16)
            q_nat[at, :] = query.T.astype(bf16)

        pairs = [(k_t, k_far), (cos_t, cos_far), (sin_t, sin_far), (q_nat, qn_far), (k_nat, kn_far), (v_nat, vn_far)]
        stores = copies(pairs, sems)

        def scores(i, s_ref):
            at = pl.ds(pl.multiple_of(i * 256, 256), 256)
            s_ref[...] = dot(k_nat[...], q_t[:, at], NORMAL)

        def tile(i, s_ref):
            at = pl.ds(pl.multiple_of(i * 256, 256), 256)
            s = s_ref[...]
            top = jnp.max(s, axis=0, keepdims=True)
            p = jnp.exp2(s - top).astype(bf16)
            o = dot(v_t[...], p, NORMAL)
            total = o[HD : HD + 1, :]
            o = o[0:HD, :] / total
            o_t[:, at] = o
            natural = o.T
            for j in range(2 * NN):
                block = natural[j * C : (j + 1) * C, :]
                out[2 * NN * i + j] = jnp.concatenate([block[0 : C // 2], block[C // 2 :]], axis=1).astype(bf16)
            hi, mid, lo = split3(-(top + jnp.log(total) * LOG2E))
            rows = lax.broadcasted_iota(jnp.int32, (16, 256), 0)
            more = jnp.where(rows == 5, hi, jnp.where(rows == 6, mid, jnp.where(rows == 7, lo, 0.0)))
            lse_t[:, at] = more

        def two_tiles(k, carry):
            scores(2 * k + 1, s_odd)
            tile(2 * k, s_even)
            scores(jnp.minimum(2 * k + 2, L // 256 - 1), s_even)
            tile(2 * k + 1, s_odd)
            return carry

        scores(0, s_even)
        lax.fori_loop(0, L // 512, two_tiles, 0)
        q_t[HD:AUG, :] = (q_t[HD:AUG, :].astype(f32) + lse_t[...]).astype(bf16)
        last = [(out, out_far, 6), (q_t, q_far, 7), (o_t, o_far, 8)]
        last = [pltpu.make_async_copy(a, b, sems.at[k]) for a, b, k in last]
        for store in last:
            store.start()
        for store in stores + last:
            store.wait()


def attend_back_kernel(
    got_far, q_far, k_far, qn_far, kn_far, vn_far, o_far, cos_far, sin_far, v0, v1, v2, v3, out_far,
    out, near, vectors, got, o_t, q_t, k_t, cos_t, sin_t, do_t, do_nat, q_nat, k_nat, v_nat, dq_t, sems,
):
    n, attends = lax.axis_index("narrow"), lax.axis_index("wide") < PAIRS
    pairs = [(got_far, got), (o_far, o_t), (qn_far, q_nat), (kn_far, k_nat), (vn_far, v_nat), (q_far, q_t)]
    pairs += [(k_far, k_t), (cos_far, cos_t), (sin_far, sin_t)]
    loads = [pltpu.make_async_copy(a, b, sems.at[k]) for k, (a, b) in enumerate(pairs)]

    @pl.when(attends)
    def _():
        for load in loads:
            load.start()

    for s, load in enumerate(copies([(v, near.at[s]) for s, v in enumerate((v0, v1, v2, v3))], sems.at[len(loads) :])):
        load.wait()
        vectors[(n + NN - s) % NN] = near[s].astype(f32)
    total = (vectors[0] + vectors[1] + vectors[2] + vectors[3])[0:8, :]
    block = jnp.concatenate([total[:, k : k + T] for k in range(0, D, T)], axis=0).astype(bf16)
    for w in range(NW):
        out[w, SLOT:, :] = block
    store = copies([(out.at[:, SLOT:, :], out_far.at[:, SLOT:, :])], sems.at[NW:])[0]

    @pl.when(attends)
    def _():
        ext = lax.broadcasted_iota(jnp.int32, (16, T), 0)
        for load in loads[:2]:
            load.wait()
        for w in range(NW):
            at = slice(w * T, (w + 1) * T)
            pieces = []
            for n in range(NN):
                piece = got[w * NN + n].astype(f32)
                pieces += [piece[:, 0:HD], piece[:, HD:]]
            natural = jnp.concatenate(pieces, axis=0)
            do_nat[at, :] = natural.astype(bf16)
            grad = natural.T
            delta = -jnp.sum(grad * o_t[:, at], axis=0, keepdims=True)
            hi, mid, lo = split3(delta)
            do_t[0:HD, at] = grad.astype(bf16)
            do_t[HD:AUG, at] = jnp.where(
                ext == 0, hi, jnp.where(ext == 1, mid, jnp.where(ext == 2, lo, 0.0))
            ).astype(bf16)
        dq_t[...] = jnp.zeros((HD, L), f32)
        for load in loads[2:]:
            load.wait()

        def folded(t):
            total = t[:, 0:T]
            for k in range(1, t.shape[1] // T):
                total = total + t[:, k * T : (k + 1) * T]
            return total

        def tile(j, carry):
            sum_key, sum_value = carry
            at = pl.ds(pl.multiple_of(j * 256, 256), 256)
            p = jnp.exp2(dot(k_nat[at, :], q_t[...], NORMAL))
            dp = dot(v_nat[at, :], do_t[...], NORMAL)
            ds = (p * dp).astype(bf16)
            dv = dot(p.astype(bf16), do_nat[...], NORMAL).T.astype(bf16)
            dk = dot(ds, q_nat[...], NORMAL).T * LN2
            dk = (dk * cos_t[:, at] - swap_pairs(dk) * sin_t[:, at]).astype(bf16)
            dq_t[...] += dot(k_t[0:HD, at], ds, NORMAL)
            for k in range(2):
                out[2 * j + k, HD : 2 * HD, :] = dk[:, k * T : (k + 1) * T]
                out[2 * j + k, 2 * HD : 3 * HD, :] = dv[:, k * T : (k + 1) * T]
            return sum_key + folded(dk.astype(f32)), sum_value + folded(dv.astype(f32))

        zero = jnp.zeros((HD, T), f32)
        sum_key, sum_value = lax.fori_loop(0, L // 256, tile, (zero, zero), unroll=2)
        sum_query = zero
        stores = []
        for w in range(NW):
            at = slice(w * T, (w + 1) * T)
            dq = dq_t[:, at] * (HD**-0.5)
            dq = (dq * cos_t[:, at] - swap_pairs(dq) * sin_t[:, at]).astype(bf16)
            out[w, 0:HD, :] = dq
            stores += copies([(out.at[w, 0 : 3 * HD, :], out_far.at[w, 0 : 3 * HD, :])], sems.at[w:])
            sum_query = sum_query + dq.astype(f32)
        rows = [jnp.sum(t.T, axis=0, keepdims=True) for t in (sum_query, sum_key, sum_value)]
        first = jnp.concatenate([rows[0], rows[1]], axis=1)
        second = jnp.concatenate([rows[2], rows[2]], axis=1)
        first_hi, second_hi = first.astype(bf16).astype(f32), second.astype(bf16).astype(f32)
        block = jnp.where(
            ext == 0,
            first_hi,
            jnp.where(ext == 1, second_hi, jnp.where(ext == 2, first - first_hi, second - second_hi)),
        )
        block = jnp.where(ext < 4, block, 0.0).astype(bf16)
        for w in range(NW):
            out[w, 3 * HD : SLOT, :] = block
        for store in stores:
            store.wait()
        stores = copies([(out.at[:, 3 * HD : SLOT, :], out_far.at[:, 3 * HD : SLOT, :])], sems)
        stores[0].wait()

    store.wait()


def chunk_rows(c, r):
    return pl.ds(pl.multiple_of(r * T + c * C, C), C)


def row_mean(t):
    return jnp.mean(t, axis=-1, keepdims=True)


def column_sum(t):
    return jnp.sum(t, axis=0, keepdims=True)


def gelu_and_slope(pre):
    half = 0.5 * (1.0 + lax.erf(pre * (2.0**-0.5)))
    return (pre * half).astype(bf16), half + pre * jnp.exp(-0.5 * pre * pre) * (1.0 / math.sqrt(2.0 * math.pi))


ATTN, NORMED, FIRST = 0, 32, 128
FFN, OUT, LAST = 0, 96, 192


def first_kernel(
    w0, m1, m2, m3, u1, u2, u3, x, attn, b_out, g_one, s_one, w_out_far, state_far, pack0, pack1, pack2, pack3,
    w_out, state, heads, packs, sems,
):
    n, c = lax.axis_index("narrow"), lax.axis_index("dp")
    pairs = [(w0, w_out.at[0:E, :])]
    for s, (mine, other) in enumerate(((m1, u1), (m2, u2), (m3, u3)), 1):
        for source, core in ((mine, c), (other, 1 - c)):
            pairs.append((source, w_out.at[pl.ds(pl.multiple_of(s * E + core * (E // 2), E // 2), E // 2), :]))
    loads = copies(pairs, sems)
    for s in range(NN):
        for r in range(R):
            for h in range(NH):
                block = attn[(r * NH + h) * NN + (n + NN - s) % NN]
                at = s * E + h * HD
                heads[r * C : r * C + C // 2, at : at + HD] = block[:, 0:HD]
                heads[r * C + C // 2 : (r + 1) * C, at : at + HD] = block[:, HD:]
    mine = pl.ds(pl.multiple_of(n * C, C), C)
    tokens = jnp.concatenate([x[r, mine, :] for r in range(R)], axis=0).astype(f32)
    for load in loads:
        load.wait()
    stores = copies([(w_out, w_out_far)], sems.at[5:])
    residual = tokens + (dot(heads[...], w_out[...], NORMAL) + row_of(b_out))
    center = residual - row_mean(residual)
    rstd = lax.rsqrt(row_mean(center * center) + EPSILON)
    unit = center * rstd
    state[:, 0:D] = unit
    state[:, D:] = jnp.broadcast_to(rstd, (CH, T))
    stores += copies([(state, state_far)], sems.at[4:])
    low = (unit * row_of(g_one) + row_of(s_one)).astype(bf16)
    for s, pack in enumerate((pack0, pack1, pack2, pack3)):
        packs[s, NORMED:FIRST, :] = low
        for r in range(R):
            packs[s, ATTN:NORMED, 256 * r : 256 * r + E] = heads[r * C : (r + 1) * C, s * E : (s + 1) * E]
        stores.append(pltpu.make_async_copy(packs.at[s], pack, sems.at[s]))
        stores[-1].start()
    for store in stores:
        store.wait()


def middle_kernel(
    every_far, state_far, cot_far, w_out_far, g_one_far, s_one_far, b0_far, b_down_far, g_two_far, s_two_far, b1, b2, b3,
    slots_far, one_far, pack_far, layer_far, sums_far,
    state, cot, w_out, g_one, s_one, b0, b_down, g_two, s_two,
    weights, slope, grad_one, slots, pack, layer, totals, sems,
):
    n = lax.axis_index("narrow")
    pairs = [(state_far, state), (cot_far, cot), (w_out_far, w_out), (g_one_far, g_one), (s_one_far, s_one)]
    pairs += [(b0_far, b0), (b_down_far, b_down), (g_two_far, g_two), (s_two_far, s_two)]
    first = copies(pairs, sems.at[8:])
    pairs = [(every_far.at[which, :, s], weights.at[which, s]) for which in range(2) for s in range(NN)]
    loads = copies(pairs, sems)
    for load in first:
        load.wait()
    mine = pl.ds(pl.multiple_of(n * C, C), C)
    ct = jnp.concatenate([cot[r, mine, :] for r in range(R)], axis=0).astype(f32)
    unit, rstd = state[:, 0:D], state[:, D : D + 1]
    normed = unit * row_of(g_one) + row_of(s_one)
    low = normed.astype(bf16)

    def weight(which, s):
        return weights[which, s].reshape(D, F)

    total = None
    for s, b in enumerate((b0, b1, b2, b3)):
        loads[s].wait()
        hidden, slope[s] = gelu_and_slope(dot(low, weight(0, s), NORMAL) + row_of(b))
        loads[NN + s].wait()
        term = dot(hidden, weight(1, s), BOTH_LAST)
        total = term if s == 0 else total + term
    residual = normed + (total + row_of(b_down))
    center = residual - row_mean(residual)
    rstd_two = lax.rsqrt(row_mean(center * center) + EPSILON)
    unit_two = center * rstd_two
    layer[...] = (unit_two * row_of(g_two) + row_of(s_two)).astype(bf16)
    scaled = ct * row_of(g_two)
    grad_two = rstd_two * (scaled - row_mean(scaled) - unit_two * row_mean(scaled * unit_two))
    low_two = grad_two.astype(bf16)
    pack[FFN:OUT, :] = low_two
    total = None
    for s in range(NN):
        pre = (slope[s] * dot(low_two, weight(1, s), NORMAL)).astype(bf16)
        term = dot(pre, weight(0, s), BOTH_LAST)
        total = term if s == 0 else total + term
    grad = grad_two + total
    scaled = grad * row_of(g_one)
    one = rstd * (scaled - row_mean(scaled) - unit * row_mean(scaled * unit))
    grad_one[...] = one
    low_one = one.astype(bf16)
    every = dot(low_one, w_out[...], BOTH_LAST)
    for s in range(NN):
        for r in range(R):
            for h in range(NH):
                block = every[r * C : (r + 1) * C, s * E + h * HD : s * E + (h + 1) * HD]
                slot = jnp.concatenate([block[0 : C // 2], block[C // 2 :]], axis=1).astype(bf16)
                slots[(r * NH + h) * NN + (n + NN - s) % NN] = slot
    stores = copies([(slots, slots_far), (grad_one, one_far), (layer, layer_far)], sems)
    pack[OUT:LAST, :] = low_one
    stores += copies([(pack, pack_far)], sems.at[3:])
    sums = [ct * unit_two, ct, low_two.astype(f32), grad * unit, grad, low_one.astype(f32)]
    totals[...] = jnp.concatenate([column_sum(t) for t in sums] + [jnp.zeros((10, D), f32)], axis=0).astype(bf16)
    stores += copies([(totals, sums_far)], sems.at[4:])
    for store in stores:
        store.wait()


def hidden_kernel(a0, a1, a2, a3, every_far, b_up, hidden_far, slope_far, firsts, weights, hidden, slope, sems):
    pairs = [(p, firsts.at[s]) for s, p in enumerate((a0, a1, a2, a3))] + [(every_far.at[0, :, 0], weights)]
    for load in copies(pairs, sems):
        load.wait()
    normed = firsts[:, NORMED:FIRST, :].reshape(TOK, D)
    act, slant = gelu_and_slope(dot(normed, weights[...].reshape(D, F), NORMAL) + row_of(b_up))
    hidden[...] = act
    slope[...] = slant
    for store in copies([(hidden, hidden_far), (slope, slope_far)], sems):
        store.wait()


def weights_kernel(
    a0, a1, a2, a3, p0, p1, p2, p3, every_far, hidden_far, slope_far,
    send0_far, send1_far, send2_far, send3_far, keep_far, out_whole, bias,
    firsts, packs, weights, hidden, slope, whole, sems,
):
    c = lax.axis_index("dp")
    pairs = [(every_far.at[1, :, 0], weights), (slope_far, slope)]
    pairs += [(p, packs.at[s]) for s, p in enumerate((p0, p1, p2, p3))]
    pairs += [(p, firsts.at[s]) for s, p in enumerate((a0, a1, a2, a3))] + [(hidden_far, hidden)]
    loads = copies(pairs, sems)
    for load in loads[:6]:
        load.wait()
    grad_ffn = packs[:, FFN:OUT, :].reshape(TOK, D)
    pre = (slope[...] * dot(grad_ffn, weights[...].reshape(D, F), NORMAL)).astype(bf16)
    for load in loads[6:]:
        load.wait()
    whole[:, 0:F] = dot(firsts[:, NORMED:FIRST, :].reshape(TOK, D), pre, BOTH_FIRST).astype(bf16)
    whole[:, F : 2 * F] = dot(grad_ffn, hidden[...], BOTH_FIRST).astype(bf16)
    half = D // 2
    pairs = [(whole.at[pl.ds(pl.multiple_of(c * half, half), half), :], keep_far)]
    for k, far in enumerate((send0_far, send1_far, send2_far, send3_far)):
        pairs.append((whole.at[pl.ds(pl.multiple_of((1 - c) * half + 96 * k, 96), 96), :], far))
    stores = copies(pairs, sems)
    heads = [firsts[s, ATTN:NORMED, 256 * r : 256 * r + E] for s in range(NN) for r in range(R)]
    heads = jnp.concatenate(heads, axis=0)
    out_whole[...] = dot(packs[:, OUT:LAST, :].reshape(TOK, D), heads, BOTH_FIRST).astype(bf16)
    bias[...] = jnp.broadcast_to(column_sum(pre.astype(f32)), (8, F))
    for store in stores:
        store.wait()


def blocks_of(block):
    return jnp.concatenate([block[:, k : k + T] for k in range(0, block.shape[1], T)], axis=0).astype(bf16)


def input_back_kernel(
    wq, wk, wv, got, part0_far, part1_far, part2_far, part3_far, grad,
    part0, part1, part2, part3, wide_part, near, sems,
):
    n = lax.axis_index("narrow")
    loads = copies([(wq, near.at[0]), (wk, near.at[1]), (wv, near.at[2])], sems)
    grads = []
    for j in range(3):
        grad_t = jnp.concatenate(
            [
                jnp.concatenate([got[r * NH + h, j * HD : (j + 1) * HD, :] for h in range(NH)], axis=0)
                for r in range(R)
            ],
            axis=1,
        )
        grads.append(grad_t.astype(f32).T.astype(bf16))
    grads = jnp.concatenate(grads, axis=1)
    grad[...] = grads
    for load in loads:
        load.wait()
    wide_part[...] = dot(grads, near[...].reshape(3 * E, D), NORMAL)
    for r in range(R):
        to = slice(r * C, (r + 1) * C)
        part0[to, :] = wide_part[chunk_rows(n, r), :]
        for s, part in ((1, part1), (2, part2), (3, part3)):
            part[to, :] = wide_part[chunk_rows((n + s) % NN, r), :].astype(bf16)
    pairs = [(part0, part0_far), (part1, part1_far), (part2, part2_far), (part3, part3_far)]
    for store in copies(pairs, sems):
        store.wait()


def input_weights_kernel(x_far, got, out_whole, grad, send_far, keep_far, sums, whole, bias, x, sems):
    c = lax.axis_index("dp")
    load = copies([(x_far, x)], sems)[0]
    heads = []
    for h in range(NH):
        block = got[h, 3 * HD : SLOT, :].astype(f32)
        for r in range(1, R):
            block = block + got[r * NH + h, 3 * HD : SLOT, :].astype(f32)
        heads.append(block)
    first = jnp.concatenate([b[0:1, 0:HD] + b[2:3, 0:HD] for b in heads], axis=1)
    second = jnp.concatenate([b[0:1, HD:] + b[2:3, HD:] for b in heads], axis=1)
    third = jnp.concatenate([b[1:2, 0:HD] + b[3:4, 0:HD] for b in heads], axis=1)
    total = got[0, SLOT:, :].astype(f32)
    for w in range(1, NW):
        total = total + got[w, SLOT:, :].astype(f32)
    total = jnp.concatenate([total[k : k + 8, :] for k in range(0, VECTORS, 8)], axis=1)
    row = jnp.concatenate([first, second, third, jnp.zeros((1, E), f32)], axis=1)
    sums[...] = jnp.concatenate([total[0:6, :], row, row], axis=0)
    hi, mid, lo = split3(sums[...])
    bias[...] = jnp.concatenate([hi[0:7, :], mid[0:7, :], lo[6:7, :], lo[6:7, :]], axis=0).astype(bf16)
    whole[:, 3 * E :] = out_whole[...]
    load.wait()
    whole[:, 0 : 3 * E] = dot(x[...].reshape(TOK, D), grad[...], BOTH_FIRST).astype(bf16)
    half = D // 2
    pairs = [(bias, send_far.at[half:, :])]
    pairs.append((whole.at[pl.ds(pl.multiple_of((1 - c) * half, half), half), :], send_far.at[0:half, :]))
    pairs.append((whole.at[pl.ds(pl.multiple_of(c * half, half), half), :], keep_far))
    for store in copies(pairs, sems):
        store.wait()


def first_add_kernel(keep_far, got0, got1, got2, got3, bias, bias_got, slots_far, keep, got, slots, more, sems):
    pairs = [(far, got.at[96 * k : 96 * (k + 1), :]) for k, far in enumerate((got0, got1, got2, got3))]
    loads = copies([*pairs, (keep_far, keep)], sems)
    row = bias[...] + bias_got[...]
    row = jnp.concatenate([row[0:1, k : k + T] for k in range(0, F, T)] + [jnp.zeros((10, T), f32)], axis=0)
    for w in range(NW):
        more[w] = row.astype(bf16)
    for load in loads:
        load.wait()
    stores = copies([(more, slots_far.at[:, FIRST_ROWS + LAST_ROWS :, :])], sems.at[NW:])
    for w in range(NW):
        at = slice(w * G, (w + 1) * G)
        slots[w] = blocks_of(keep[at, :].astype(f32) + got[at, :].astype(f32))
        stores += copies([(slots.at[w], slots_far.at[w, 0:FIRST_ROWS, :])], sems.at[w:])
    for store in stores:
        store.wait()


def last_add_kernel(
    keep_far, slots_in, got_far, sums, slots_far, b_q, b_k, b_v, g_two, s_two, b_down, g_one, s_one, b_out,
    keep, got, slots, sems,
):
    for load in copies([(keep_far, keep), (got_far, got)], sems):
        load.wait()
    stores = []
    for w in range(NW):
        at = slice(w * G, (w + 1) * G)
        slots[w] = blocks_of(keep[at, :].astype(f32) + got[at, :].astype(f32))
        stores += copies([(slots.at[w], slots_far.at[w, FIRST_ROWS : FIRST_ROWS + LAST_ROWS, :])], sems.at[w:])
    other = got[D // 2 :, :].astype(f32)
    hi, mid, lo = split3(sums[...])
    total = (hi[0:7, :] + other[0:7, :]) + (mid[0:7, :] + other[7:14, :])
    bias = total[6:7, :] + (lo[6:7, :] + other[14:15, :])
    for k, ref in enumerate((b_q, b_k, b_v)):
        ref[...] = bias[:, k * E : (k + 1) * E].reshape(E)
    for k, ref in enumerate((g_two, s_two, b_down, g_one, s_one, b_out)):
        ref[...] = total[k : k + 1, :].reshape(D)
    for store in stores:
        store.wait()


def last_sum_kernel(got, g_q, g_k, g_v, out, up, down, b_up):
    total = got[0].astype(f32)
    for w in range(1, NW):
        total = total + got[w].astype(f32)
    end = FIRST_ROWS + LAST_ROWS
    b_up[...] = jnp.concatenate([total[end + k : end + k + 1, :] for k in range(F // T)], axis=1).reshape(F)
    total = jnp.concatenate([total[k : k + G, :] for k in range(0, end, G)], axis=1)
    up[...] = total[:, 0:F]
    down[...] = total[:, F : 2 * F]
    for k, ref in enumerate((g_q, g_k, g_v, out)):
        ref[...] = total[:, 2 * F + k * E : 2 * F + (k + 1) * E]


def input_chunk_kernel(part_far, one_far, part1, part2, part3, low, part0, grad_one, sems):
    for load in copies([(part_far, part0), (one_far, grad_one)], sems):
        load.wait()
    total = part0[...] + part1[...].astype(f32) + part2[...].astype(f32) + part3[...].astype(f32)
    low[...] = (grad_one[...] + total).astype(bf16)


def spread_kernel(g0, g1, g2, g3, out):
    n = lax.axis_index("narrow")
    for s, part in enumerate((g0, g1, g2, g3)):
        at = pl.ds(pl.multiple_of((n + NN - s) % NN * C, C), C)
        for r in range(R):
            out[r, at, :] = part[r * C : (r + 1) * C, :].astype(f32)


def shifted(x, s):
    return lax.ppermute(x, "narrow", [(i, (i + s) % NN) for i in range(NN)])


def gather_narrow(x):
    return (x, shifted(x, 1), shifted(x, 2), shifted(x, 3))


def scatter_narrow(parts):
    return (parts[0], shifted(parts[1], 1), shifted(parts[2], 2), shifted(parts[3], 3))


def other_core(x):
    return lax.ppermute(x, "dp", [(0, 1), (1, 0)])


def exchange(slots):
    return lax.all_to_all(slots, "wide", 0, 0, tiled=True)


def exchange_all(slots):
    return lax.all_to_all(slots, ("wide", "narrow"), 0, 0, tiled=True)


def body(
    hidden_in, segments, weight_query, bias_query, weight_key, bias_key, weight_value, bias_value,
    weight_out, bias_out, gain_one, shift_one, weight_up, bias_up, weight_down, bias_down,
    gain_two, shift_two, cotangent,
):
    frequency = np.repeat(np.power(10000.0, -np.arange(0, HD, 2) / HD), 2).astype(np.float32)
    frequency = jnp.asarray(np.broadcast_to(frequency[:, None], (HD, T)))
    shard = jnp.where(lax.axis_index("dp") == 0, weight_up, weight_down.T)
    shards = gather_narrow(shard)
    mine = lax.dynamic_slice_in_dim(weight_out, lax.axis_index("dp") * (E // 2), E // 2, 0)
    weights_got = gather_narrow(mine)[1:]
    weights_out = (weight_out, *weights_got, *(other_core(w) for w in weights_got))
    biases_up = gather_narrow(bias_up)
    query_t, key_t, value_t = weight_query.T, weight_key.T, weight_value.T

    slots, token = call(
        "project",
        project_kernel,
        [((NW, SLOT, T), bf16)],
        (hidden_in, segments, query_t, bias_query, key_t, bias_key, value_t, bias_value),
        scratch=[
            pltpu.VMEM((R, T, D), bf16),
            pltpu.VMEM((3, E, D), bf16),
            pltpu.VMEM((E,), f32),
            pltpu.VMEM((E,), f32),
            pltpu.VMEM((E,), f32),
            pltpu.VMEM((R, T), jnp.int32),
            pltpu.SemaphoreType.DMA((8,)),
        ],
        far_in=range(8),
        token=True,
    )
    (shards,) = call(
        "stack",
        stack_kernel,
        [((NN, D // NW, F), bf16)],
        shards,
        scratch=[pltpu.SemaphoreType.DMA((NN,))],
        any_in=range(NN),
        far=(0,),
        after=(token,),
    )
    every = lax.all_gather(shards, ("dp", "wide")).reshape(2, NW, NN, D // NW, F)
    got = exchange(slots)
    out_slots, *saved = call(
        "attend",
        attend_kernel,
        [
            ((NW * NN, C // 2, 2 * HD), bf16),
            ((AUG, L), bf16),
            ((AUG, L), bf16),
            ((L, HD), bf16),
            ((L, AUG), bf16),
            ((L, AUG), bf16),
            ((HD, L), f32),
            ((HD, L), f32),
            ((HD, L), f32),
        ],
        (got, frequency),
        scratch=[
            pltpu.VMEM((NW * NN, C // 2, 2 * HD), bf16),
            pltpu.VMEM((AUG, L), bf16),
            pltpu.VMEM((AUG, L), bf16),
            pltpu.VMEM((AUG, L), bf16),
            pltpu.VMEM((L, HD), bf16),
            pltpu.VMEM((L, AUG), bf16),
            pltpu.VMEM((L, AUG), bf16),
            pltpu.VMEM((HD, L), f32),
            pltpu.VMEM((HD, L), f32),
            pltpu.VMEM((HD, L), f32),
            pltpu.VMEM((L, 256), f32),
            pltpu.VMEM((L, 256), f32),
            pltpu.VMEM((16, L), f32),
            pltpu.SemaphoreType.DMA((9,)),
        ],
        mib=24,
        after=weights_got,
        far=range(9),
    )
    attn = exchange_all(out_slots)
    chunk_f32, chunk_low = ((CH, D), f32), ((CH, D), bf16)
    parts4 = [chunk_f32, chunk_low, chunk_low, chunk_low]
    slot_shape = (NW * NN, C // 2, 2 * HD)
    w_out, state, *firsts, token = call(
        "first",
        first_kernel,
        [((D, D), bf16), ((CH, D + T), f32)] + [((FIRST, D), bf16)] * NN,
        (*weights_out, hidden_in, attn, bias_out, gain_one, shift_one),
        scratch=[
            pltpu.VMEM((D, D), bf16),
            pltpu.VMEM((CH, D + T), f32),
            pltpu.VMEM((CH, D), bf16),
            pltpu.VMEM((NN, FIRST, D), bf16),
            pltpu.SemaphoreType.DMA((7,)),
        ],
        far_in=range(7),
        far=range(6),
        token=True,
        after=biases_up[1:],
    )
    firsts = (firsts[0], *(shifted(firsts[s], NN - s) for s in range(1, NN)))
    every = later(every, token)
    slots, grad_one, pack, layer, totals = call(
        "middle",
        middle_kernel,
        [(slot_shape, bf16), chunk_f32, ((LAST, D), bf16), chunk_low, ((16, D), bf16)],
        (
            every, state, cotangent, w_out, gain_one, shift_one, biases_up[0], bias_down, gain_two, shift_two,
            *biases_up[1:],
        ),
        scratch=[
            pltpu.VMEM((CH, D + T), f32),
            pltpu.VMEM((R, T, D), bf16),
            pltpu.VMEM((D, D), bf16),
            *[pltpu.VMEM((D,), f32)] * 6,
            pltpu.VMEM((2, NN, NW, D // NW, F), bf16),
            pltpu.VMEM((NN, CH, F), f32),
            pltpu.VMEM((CH, D), f32),
            pltpu.VMEM(slot_shape, bf16),
            pltpu.VMEM((LAST, D), bf16),
            pltpu.VMEM((CH, D), bf16),
            pltpu.VMEM((16, D), bf16),
            pltpu.SemaphoreType.DMA((17,)),
        ],
        mib=32,
        far_in=range(10),
        far=range(5),
    )
    got = exchange_all(later(slots, *firsts[1:]))
    firsts = (firsts[0], firsts[3], firsts[2], firsts[1])
    hidden, slope = call(
        "hidden",
        hidden_kernel,
        [((TOK, F), bf16), ((TOK, F), f32)],
        (*firsts, every, bias_up),
        scratch=[
            pltpu.VMEM((NN, FIRST, D), bf16),
            pltpu.VMEM((NW, D // NW, F), bf16),
            pltpu.VMEM((TOK, F), bf16),
            pltpu.VMEM((TOK, F), f32),
            pltpu.SemaphoreType.DMA((5,)),
        ],
        far_in=range(5),
        far=(0, 1),
    )
    totals = gather_narrow(totals)
    packs = gather_narrow(later(pack, hidden, got, *totals[1:]))
    slots, token = call(
        "attend_back",
        attend_back_kernel,
        [((NW, SLOT + VECTORS, T), bf16)],
        (got, *saved, *totals),
        scratch=[
            pltpu.VMEM((NW, SLOT + VECTORS, T), bf16),
            pltpu.VMEM((NN, 16, D), bf16),
            pltpu.VMEM((NN, 16, D), f32),
            pltpu.VMEM((NW * NN, C // 2, 2 * HD), bf16),
            pltpu.VMEM((HD, L), f32),
            pltpu.VMEM((AUG, L), bf16),
            pltpu.VMEM((AUG, L), bf16),
            pltpu.VMEM((HD, L), f32),
            pltpu.VMEM((HD, L), f32),
            pltpu.VMEM((AUG, L), bf16),
            pltpu.VMEM((L, HD), bf16),
            pltpu.VMEM((L, HD), bf16),
            pltpu.VMEM((L, AUG), bf16),
            pltpu.VMEM((L, AUG), bf16),
            pltpu.VMEM((HD, L), f32),
            pltpu.SemaphoreType.DMA((NW + 1,)),
        ],
        far_in=range(13),
        far=(0,),
        token=True,
    )
    *sends, up_keep, out_whole, bias = call(
        "weights",
        weights_kernel,
        [((96, 2 * F), bf16)] * 4 + [((D // 2, 2 * F), bf16), ((D, E), bf16), ((8, D), f32)],
        (*firsts, *packs, every, hidden, slope),
        scratch=[
            pltpu.VMEM((NN, FIRST, D), bf16),
            pltpu.VMEM((NN, LAST, D), bf16),
            pltpu.VMEM((NW, D // NW, F), bf16),
            pltpu.VMEM((TOK, F), bf16),
            pltpu.VMEM((TOK, F), f32),
            pltpu.VMEM((D, 2 * F), bf16),
            pltpu.SemaphoreType.DMA((11,)),
        ],
        mib=32,
        far_in=range(11),
        far=range(5),
        cost=COST,
        after=(token,),
    )
    got = exchange(slots)
    last_shape = (NW, FIRST_ROWS + LAST_ROWS + BIAS_ROWS, T)
    slots, added = call(
        "first_add",
        first_add_kernel,
        [(last_shape, bf16)],
        (up_keep, *(other_core(send) for send in sends), bias, other_core(bias)),
        scratch=[
            pltpu.VMEM((D // 2, 2 * F), bf16),
            pltpu.VMEM((D // 2, 2 * F), bf16),
            pltpu.VMEM((NW, FIRST_ROWS, T), bf16),
            pltpu.VMEM((NW, BIAS_ROWS, T), bf16),
            pltpu.SemaphoreType.DMA((NW + 1,)),
        ],
        far_in=(0,),
        any_in=range(1, 5),
        far=(0,),
        token=True,
    )
    *parts, grad = call(
        "input_back",
        input_back_kernel,
        [*parts4, ((TOK, 3 * E), bf16)],
        (query_t, key_t, value_t, got),
        scratch=[
            pltpu.VMEM((CH, D), f32),
            pltpu.VMEM((CH, D), bf16),
            pltpu.VMEM((CH, D), bf16),
            pltpu.VMEM((CH, D), bf16),
            pltpu.VMEM((TOK, D), f32),
            pltpu.VMEM((3, E, D), bf16),
            pltpu.SemaphoreType.DMA((4,)),
        ],
        far_in=range(3),
        far=range(4),
        after=(added,),
    )
    send, keep, sums = call(
        "input_weights",
        input_weights_kernel,
        [((D // 2 + 16, D), bf16), ((D // 2, D), bf16), ((8, D), f32)],
        (hidden_in, got, out_whole, grad),
        scratch=[
            pltpu.VMEM((D, D), bf16),
            pltpu.VMEM((16, D), bf16),
            pltpu.VMEM((R, T, D), bf16),
            pltpu.SemaphoreType.DMA((3,)),
        ],
        far_in=(0,),
        far=(0, 1),
    )
    parts = scatter_narrow(parts)
    slots, b_query, b_key, b_value, g_two, s_two, b_down, g_one, s_one, b_out = call(
        "last_add",
        last_add_kernel,
        [(last_shape, bf16)] + [((E,), f32)] * 3 + [((D,), f32)] * 6,
        (keep, slots, other_core(send), sums),
        scratch=[
            pltpu.VMEM((D // 2, D), bf16),
            pltpu.VMEM((D // 2 + 16, D), bf16),
            pltpu.VMEM((NW, LAST_ROWS, T), bf16),
            pltpu.SemaphoreType.DMA((NW,)),
        ],
        far_in=range(2),
        any_in=(2,),
        far=(0,),
        aliases={1: 0},
    )
    (input_low,) = call("input_chunk", input_chunk_kernel, [chunk_low], (parts[0], grad_one, *parts[1:]),
        scratch=[pltpu.VMEM((CH, D), f32), pltpu.VMEM((CH, D), f32), pltpu.SemaphoreType.DMA((2,))],
        cost=COST, far_in=(0, 1),
    )
    layers = gather_narrow(later(layer, parts[2]))
    whole_out = ((R, T, D), f32)
    (layer_out,) = call("layer_out", spread_kernel, [whole_out], layers)
    (grad_input,) = call("grad_input", spread_kernel, [whole_out], gather_narrow(input_low))
    g_query, g_key, g_value, g_out, grad_up, grad_down, b_up = call(
        "last_sum", last_sum_kernel, [((G, E), f32)] * 4 + [((G, F), f32)] * 2 + [((F,), f32)], (exchange(slots),)
    )
    return (
        layer_out, grad_input, g_query, b_query, g_key, b_key, g_value, b_value, g_out.T, b_out,
        g_one, s_one, grad_up, b_up, grad_down.T, b_down, g_two, s_two,
    )


def solution(mesh):
    tokens, whole = P("dp", "wide", None), P()
    column, vector = P(None, "narrow"), P("narrow")
    rows_split, columns_split = P(("dp", "wide"), "narrow"), P("narrow", ("dp", "wide"))
    in_specs = (
        tokens, P("dp", "wide"), column, vector, column, vector, column, vector, P("narrow", None), whole,
        whole, whole, P("wide", "narrow"), vector, P("narrow", "wide"), whole, whole, whole, tokens,
    )
    out_specs = (
        tokens, tokens, rows_split, vector, rows_split, vector, rows_split, vector, columns_split, whole,
        whole, whole, rows_split, vector, columns_split, whole, whole, whole,
    )
    return jax.shard_map(body, mesh=mesh, in_specs=in_specs, out_specs=out_specs, check_vma=False)
```

```python
import functools
import math

import jax
import jax.numpy as jnp
import numpy as np
from jax import lax
from jax.experimental import pallas as pl
from jax.experimental.pallas import tpu as pltpu
from jax.sharding import PartitionSpec as P

D = 768
HD = 64
R = 3
T = 128
NH = 3
E = NH * HD
F = 768
NW = 16
NN = 4
TOK = R * T
L = NW * T
C = T // NN
CH = R * C
PAIRS = R * NH
G = D // (2 * NW)
FIRST_ROWS, LAST_ROWS, BIAS_ROWS = 12 * G, 6 * G, 16
SLOT = 3 * HD + 16
VECTORS = 8 * D // T
AUG = HD + 16
EPSILON = 1e-12
BIG = 1e30
LOG2E = math.log2(math.e)
LN2 = math.log(2.0)
COST = 10**11
f32, bf16 = jnp.float32, jnp.bfloat16


def dot(a, b, dims):
    return lax.dot_general(a, b, (dims, ((), ())), preferred_element_type=f32)


NORMAL, BOTH_LAST, BOTH_FIRST = ((1,), (0,)), ((1,), (1,)), ((0,), (0,))


def in_far_memory(arrays):
    return [pltpu.with_memory_space_constraint(a, pltpu.HBM) if a.size > 1024 else a for a in arrays]


def call(
    name, kernel, outs, args, scratch=(), cost=1024, mib=16, after=(), far_in=(), any_in=(), near=(), far=(), aliases={},
    token=False,
):
    if token:
        outs = [*outs, ((8, 128), f32)]

    def run(*refs):
        end = len(args) + len(after)
        if token:
            at = end + len(outs) - 1
            refs[at][...] = jnp.zeros((8, 128), f32)
            refs = refs[:at] + refs[at + 1 :]
        kernel(*refs[: len(args)], *refs[end:])

    def shape(k, s, t):
        return pltpu.VMEM(s, t) if k in near else pltpu.HBM(s, t) if k in far else jax.ShapeDtypeStruct(s, t)

    args = [pltpu.with_memory_space_constraint(a, pltpu.HBM) if k in far_in else a for k, a in enumerate(args)]
    after = in_far_memory(after)
    return pl.pallas_call(
        run,
        out_shape=[shape(k, s, t) for k, (s, t) in enumerate(outs)],
        in_specs=[
            pl.BlockSpec(memory_space=pltpu.HBM if k in far_in else pl.ANY if k in any_in else pltpu.VMEM)
            for k in range(len(args))
        ]
        + [pl.BlockSpec(memory_space=pl.ANY) for _ in after],
        out_specs=[pl.BlockSpec(memory_space=pltpu.HBM if k in far else pltpu.VMEM) for k in range(len(outs))],
        scratch_shapes=list(scratch),
        input_output_aliases=aliases,
        compiler_params=pltpu.CompilerParams(vmem_limit_bytes=mib * 1024 * 1024),
        cost_estimate=pl.CostEstimate(flops=cost, bytes_accessed=1024, transcendentals=0),
        name=name,
    )(*args, *after)


def later(x, *after, anywhere=()):
    after = [*in_far_memory(after), *anywhere]
    return pl.pallas_call(
        lambda *refs: None,
        out_shape=jax.ShapeDtypeStruct(x.shape, x.dtype),
        in_specs=[pl.BlockSpec(memory_space=pltpu.HBM)] + [pl.BlockSpec(memory_space=pl.ANY) for _ in after],
        out_specs=pl.BlockSpec(memory_space=pltpu.HBM),
        input_output_aliases={0: 0},
        cost_estimate=pl.CostEstimate(flops=1024, bytes_accessed=1024, transcendentals=0),
        name="later",
    )(x, *after)


def copies(pairs, sems):
    made = [pltpu.make_async_copy(a, b, sems.at[k]) for k, (a, b) in enumerate(pairs)]
    for copy in made:
        copy.start()
    return made


def row_of(ref):
    return ref[...].reshape(1, ref.shape[-1])


def split3(v):
    hi = v.astype(bf16).astype(f32)
    rest = v - hi
    mid = rest.astype(bf16).astype(f32)
    return hi, mid, (rest - mid).astype(bf16).astype(f32)


def sine_cosine(angle):
    turns = jnp.floor(angle * (2.0 / math.pi) + 0.5)
    r = ((angle - turns * 1.5703125) - turns * 4.837512969970703125e-4) - turns * 7.54978995489188e-8
    z = r * r
    sine = r + r * z * (-1.6666654611e-1 + z * (8.3321608736e-3 + z * -1.9515295891e-4))
    cosine = 1.0 - 0.5 * z + z * z * (4.166664568298827e-2 + z * (-1.388731625493765e-3 + z * 2.443315711809948e-5))
    quarter = turns - 4.0 * jnp.floor(turns * 0.25)
    odd = (quarter == 1.0) | (quarter == 3.0)
    sin_abs = jnp.where(odd, cosine, sine)
    cos_abs = jnp.where(odd, sine, cosine)
    return jnp.where(quarter >= 2.0, -sin_abs, sin_abs), jnp.where((quarter == 1.0) | (quarter == 2.0), -cos_abs, cos_abs)


def swap_pairs(t):
    rows = lax.broadcasted_iota(jnp.int32, t.shape, 0)
    return jnp.where(rows % 2 == 0, pltpu.roll(t, HD - 1, 0), pltpu.roll(t, 1, 0))


def project_kernel(x_far, seg, wq, bq, wk, bk, wv, bv, slots, x, near, bias0, bias1, bias2, ids, sems):
    pairs = [(x_far, x), (wq, near.at[0]), (bq, bias0), (wk, near.at[1]), (bk, bias1)]
    pairs += [(wv, near.at[2]), (bv, bias2), (seg, ids)]
    loads = copies(pairs, sems)
    for load in loads:
        load.wait()
    flat = x[...].reshape(TOK, D)
    for j, b in enumerate((bias0, bias1, bias2)):
        w = near.at[j]
        bias = jnp.broadcast_to(row_of(b), (T, E)).T
        yt = (dot(w[...], flat, BOTH_LAST) + jnp.concatenate([bias] * R, axis=1)).astype(bf16)
        for r in range(R):
            for h in range(NH):
                slots[r * NH + h, j * HD : (j + 1) * HD, :] = yt[h * HD : (h + 1) * HD, r * T : (r + 1) * T]
    for r in range(R):
        block = jnp.broadcast_to(ids[r : r + 1, :].astype(f32), (16, T)).astype(bf16)
        for h in range(NH):
            slots[r * NH + h, 3 * HD :, :] = block


def stack_kernel(a, b, c, d, out, sems):
    for copy in copies([(part, out.at[s]) for s, part in enumerate((a, b, c, d))], sems):
        copy.wait()


def attend_kernel(
    got, freq, out_far, q_far, k_far, qn_far, kn_far, vn_far, o_far, cos_far, sin_far,
    out, q_t, k_t, v_t, q_nat, k_nat, v_nat, o_t, cos_t, sin_t, s_even, s_odd, lse_t, sems,
):
    @pl.when(lax.axis_index("wide") < PAIRS)
    def _():
        ids = [got[w, 3 * HD :, :].astype(f32)[0:1, :] for w in range(NW)]
        starts = []
        for d in range(1, 5):
            below = jnp.zeros((1, T), f32)
            for w in range(NW):
                below = below + jnp.where(ids[w] < d, 1.0, 0.0)
            starts.append(jnp.sum(below, axis=1, keepdims=True))
        odd = lax.broadcasted_iota(jnp.int32, (HD, T), 0) % 2 == 1
        ext = lax.broadcasted_iota(jnp.int32, (16, T), 0)
        lane = lax.broadcasted_iota(jnp.int32, (1, T), 1).astype(f32)
        for w in range(NW):
            at = slice(w * T, (w + 1) * T)
            start = jnp.zeros((1, T), f32)
            for d in range(1, 5):
                start = jnp.where(ids[w] == d, starts[d - 1], start)
            sine, cosine = sine_cosine(freq[...] * (lane + (w * T) - start))
            sine = jnp.where(odd, sine, -sine)
            cos_t[:, at] = cosine
            sin_t[:, at] = sine
            query = got[w, 0:HD, :].astype(f32)
            key = got[w, HD : 2 * HD, :].astype(f32)
            query = (query * cosine + swap_pairs(query) * sine) * (HD**-0.5 * LOG2E)
            key = key * cosine + swap_pairs(key) * sine
            same = ids[w] == ext.astype(f32)
            doc = ext < 5
            key_ext = jnp.where(doc, jnp.where(same, 1.0, 0.0), jnp.where(ext < 8, 1.0, 0.0))
            q_t[0:HD, at] = query.astype(bf16)
            q_t[HD:AUG, at] = jnp.where(doc, jnp.where(same, 0.0, -BIG), 0.0).astype(bf16)
            k_t[0:HD, at] = key.astype(bf16)
            k_t[HD:AUG, at] = key_ext.astype(bf16)
            k_nat[at, :] = jnp.concatenate([key, key_ext], axis=0).T.astype(bf16)
            value = got[w, 2 * HD : 3 * HD, :].astype(f32)
            value = jnp.concatenate([value, jnp.where(ext < 3, 1.0, 0.0)], axis=0)
            v_t[:, at] = value.astype(bf16)
            v_nat[at, :] = value.T.astype(bf16)
            q_nat[at, :] = query.T.astype(bf16)

        pairs = [(k_t, k_far), (cos_t, cos_far), (sin_t, sin_far), (q_nat, qn_far), (k_nat, kn_far), (v_nat, vn_far)]
        stores = copies(pairs, sems)

        def scores(i, s_ref):
            at = pl.ds(pl.multiple_of(i * 256, 256), 256)
            s_ref[...] = dot(k_nat[...], q_t[:, at], NORMAL)

        def tile(i, s_ref):
            at = pl.ds(pl.multiple_of(i * 256, 256), 256)
            s = s_ref[...]
            top = jnp.max(s, axis=0, keepdims=True)
            p = jnp.exp2(s - top).astype(bf16)
            o = dot(v_t[...], p, NORMAL)
            total = o[HD : HD + 1, :]
            o = o[0:HD, :] / total
            o_t[:, at] = o
            natural = o.T
            for j in range(2 * NN):
                block = natural[j * C : (j + 1) * C, :]
                out[2 * NN * i + j] = jnp.concatenate([block[0 : C // 2], block[C // 2 :]], axis=1).astype(bf16)
            hi, mid, lo = split3(-(top + jnp.log(total) * LOG2E))
            rows = lax.broadcasted_iota(jnp.int32, (16, 256), 0)
            more = jnp.where(rows == 5, hi, jnp.where(rows == 6, mid, jnp.where(rows == 7, lo, 0.0)))
            lse_t[:, at] = more

        def two_tiles(k, carry):
            scores(2 * k + 1, s_odd)
            tile(2 * k, s_even)
            scores(jnp.minimum(2 * k + 2, L // 256 - 1), s_even)
            tile(2 * k + 1, s_odd)
            return carry

        scores(0, s_even)
        lax.fori_loop(0, L // 512, two_tiles, 0)
        q_t[HD:AUG, :] = (q_t[HD:AUG, :].astype(f32) + lse_t[...]).astype(bf16)
        last = [(out, out_far, 6), (q_t, q_far, 7), (o_t, o_far, 8)]
        last = [pltpu.make_async_copy(a, b, sems.at[k]) for a, b, k in last]
        for store in last:
            store.start()
        for store in stores + last:
            store.wait()


def attend_back_kernel(
    got_far, q_far, k_far, qn_far, kn_far, vn_far, o_far, cos_far, sin_far, v0, v1, v2, v3, out_far,
    out, near, vectors, got, o_t, q_t, k_t, cos_t, sin_t, do_t, do_nat, q_nat, k_nat, v_nat, dq_t, sems,
):
    n, attends = lax.axis_index("narrow"), lax.axis_index("wide") < PAIRS
    pairs = [(got_far, got), (o_far, o_t), (qn_far, q_nat), (kn_far, k_nat), (vn_far, v_nat), (q_far, q_t)]
    pairs += [(k_far, k_t), (cos_far, cos_t), (sin_far, sin_t)]
    loads = [pltpu.make_async_copy(a, b, sems.at[k]) for k, (a, b) in enumerate(pairs)]

    @pl.when(attends)
    def _():
        for load in loads:
            load.start()

    for s, load in enumerate(copies([(v, near.at[s]) for s, v in enumerate((v0, v1, v2, v3))], sems.at[len(loads) :])):
        load.wait()
        vectors[(n + NN - s) % NN] = near[s].astype(f32)
    total = (vectors[0] + vectors[1] + vectors[2] + vectors[3])[0:8, :]
    block = jnp.concatenate([total[:, k : k + T] for k in range(0, D, T)], axis=0).astype(bf16)
    for w in range(NW):
        out[w, SLOT:, :] = block
    store = copies([(out.at[:, SLOT:, :], out_far.at[:, SLOT:, :])], sems.at[NW:])[0]

    @pl.when(attends)
    def _():
        ext = lax.broadcasted_iota(jnp.int32, (16, T), 0)
        for load in loads[:2]:
            load.wait()
        for w in range(NW):
            at = slice(w * T, (w + 1) * T)
            pieces = []
            for n in range(NN):
                piece = got[w * NN + n].astype(f32)
                pieces += [piece[:, 0:HD], piece[:, HD:]]
            natural = jnp.concatenate(pieces, axis=0)
            do_nat[at, :] = natural.astype(bf16)
            grad = natural.T
            delta = -jnp.sum(grad * o_t[:, at], axis=0, keepdims=True)
            hi, mid, lo = split3(delta)
            do_t[0:HD, at] = grad.astype(bf16)
            do_t[HD:AUG, at] = jnp.where(
                ext == 0, hi, jnp.where(ext == 1, mid, jnp.where(ext == 2, lo, 0.0))
            ).astype(bf16)
        dq_t[...] = jnp.zeros((HD, L), f32)
        for load in loads[2:]:
            load.wait()

        def folded(t):
            total = t[:, 0:T]
            for k in range(1, t.shape[1] // T):
                total = total + t[:, k * T : (k + 1) * T]
            return total

        def tile(j, carry):
            sum_key, sum_value = carry
            at = pl.ds(pl.multiple_of(j * 256, 256), 256)
            p = jnp.exp2(dot(k_nat[at, :], q_t[...], NORMAL))
            dp = dot(v_nat[at, :], do_t[...], NORMAL)
            ds = (p * dp).astype(bf16)
            dv = dot(p.astype(bf16), do_nat[...], NORMAL).T.astype(bf16)
            dk = dot(ds, q_nat[...], NORMAL).T * LN2
            dk = (dk * cos_t[:, at] - swap_pairs(dk) * sin_t[:, at]).astype(bf16)
            dq_t[...] += dot(k_t[0:HD, at], ds, NORMAL)
            for k in range(2):
                out[2 * j + k, HD : 2 * HD, :] = dk[:, k * T : (k + 1) * T]
                out[2 * j + k, 2 * HD : 3 * HD, :] = dv[:, k * T : (k + 1) * T]
            return sum_key + folded(dk.astype(f32)), sum_value + folded(dv.astype(f32))

        zero = jnp.zeros((HD, T), f32)
        sum_key, sum_value = lax.fori_loop(0, L // 256, tile, (zero, zero), unroll=2)
        sum_query = zero
        stores = []
        for w in range(NW):
            at = slice(w * T, (w + 1) * T)
            dq = dq_t[:, at] * (HD**-0.5)
            dq = (dq * cos_t[:, at] - swap_pairs(dq) * sin_t[:, at]).astype(bf16)
            out[w, 0:HD, :] = dq
            stores += copies([(out.at[w, 0 : 3 * HD, :], out_far.at[w, 0 : 3 * HD, :])], sems.at[w:])
            sum_query = sum_query + dq.astype(f32)
        rows = [jnp.sum(t.T, axis=0, keepdims=True) for t in (sum_query, sum_key, sum_value)]
        first = jnp.concatenate([rows[0], rows[1]], axis=1)
        second = jnp.concatenate([rows[2], rows[2]], axis=1)
        first_hi, second_hi = first.astype(bf16).astype(f32), second.astype(bf16).astype(f32)
        block = jnp.where(
            ext == 0,
            first_hi,
            jnp.where(ext == 1, second_hi, jnp.where(ext == 2, first - first_hi, second - second_hi)),
        )
        block = jnp.where(ext < 4, block, 0.0).astype(bf16)
        for w in range(NW):
            out[w, 3 * HD : SLOT, :] = block
        for store in stores:
            store.wait()
        stores = copies([(out.at[:, 3 * HD : SLOT, :], out_far.at[:, 3 * HD : SLOT, :])], sems)
        stores[0].wait()

    store.wait()


def chunk_rows(c, r):
    return pl.ds(pl.multiple_of(r * T + c * C, C), C)


def row_mean(t):
    return jnp.mean(t, axis=-1, keepdims=True)


def column_sum(t):
    return jnp.sum(t, axis=0, keepdims=True)


def gelu_and_slope(pre):
    half = 0.5 * (1.0 + lax.erf(pre * (2.0**-0.5)))
    return (pre * half).astype(bf16), half + pre * jnp.exp(-0.5 * pre * pre) * (1.0 / math.sqrt(2.0 * math.pi))


ATTN, NORMED, FIRST = 0, 32, 128
FFN, OUT, LAST = 0, 96, 192


def first_kernel(
    w0, m1, m2, m3, u1, u2, u3, x, attn, b_out, g_one, s_one, w_out_far, state_far, pack0, pack1, pack2, pack3,
    w_out, state, heads, packs, sems,
):
    n, c = lax.axis_index("narrow"), lax.axis_index("dp")
    pairs = [(w0, w_out.at[0:E, :])]
    for s, (mine, other) in enumerate(((m1, u1), (m2, u2), (m3, u3)), 1):
        for source, core in ((mine, c), (other, 1 - c)):
            pairs.append((source, w_out.at[pl.ds(pl.multiple_of(s * E + core * (E // 2), E // 2), E // 2), :]))
    loads = copies(pairs, sems)
    for s in range(NN):
        for r in range(R):
            for h in range(NH):
                block = attn[(r * NH + h) * NN + (n + NN - s) % NN]
                at = s * E + h * HD
                heads[r * C : r * C + C // 2, at : at + HD] = block[:, 0:HD]
                heads[r * C + C // 2 : (r + 1) * C, at : at + HD] = block[:, HD:]
    mine = pl.ds(pl.multiple_of(n * C, C), C)
    tokens = jnp.concatenate([x[r, mine, :] for r in range(R)], axis=0).astype(f32)
    for load in loads:
        load.wait()
    stores = copies([(w_out, w_out_far)], sems.at[5:])
    residual = tokens + (dot(heads[...], w_out[...], NORMAL) + row_of(b_out))
    center = residual - row_mean(residual)
    rstd = lax.rsqrt(row_mean(center * center) + EPSILON)
    unit = center * rstd
    state[:, 0:D] = unit
    state[:, D:] = jnp.broadcast_to(rstd, (CH, T))
    stores += copies([(state, state_far)], sems.at[4:])
    low = (unit * row_of(g_one) + row_of(s_one)).astype(bf16)
    for s, pack in enumerate((pack0, pack1, pack2, pack3)):
        packs[s, NORMED:FIRST, :] = low
        for r in range(R):
            packs[s, ATTN:NORMED, 256 * r : 256 * r + E] = heads[r * C : (r + 1) * C, s * E : (s + 1) * E]
        stores.append(pltpu.make_async_copy(packs.at[s], pack, sems.at[s]))
        stores[-1].start()
    for store in stores:
        store.wait()


def middle_kernel(
    every_far, state_far, cot_far, w_out_far, g_one_far, s_one_far, b0_far, b_down_far, g_two_far, s_two_far, b1, b2, b3,
    slots_far, one_far, pack_far, layer_far, sums_far,
    state, cot, w_out, g_one, s_one, b0, b_down, g_two, s_two,
    weights, slope, grad_one, slots, pack, layer, totals, sems,
):
    n = lax.axis_index("narrow")
    pairs = [(state_far, state), (cot_far, cot), (w_out_far, w_out), (g_one_far, g_one), (s_one_far, s_one)]
    pairs += [(b0_far, b0), (b_down_far, b_down), (g_two_far, g_two), (s_two_far, s_two)]
    first = copies(pairs, sems.at[8:])
    pairs = [(every_far.at[which, :, s], weights.at[which, s]) for s in range(NN) for which in range(2)]
    loads = copies(pairs, sems)
    for load in first:
        load.wait()
    mine = pl.ds(pl.multiple_of(n * C, C), C)
    ct = jnp.concatenate([cot[r, mine, :] for r in range(R)], axis=0).astype(f32)
    unit, rstd = state[:, 0:D], state[:, D : D + 1]
    normed = unit * row_of(g_one) + row_of(s_one)
    low = normed.astype(bf16)

    def weight(which, s):
        return weights[which, s].reshape(D, F)

    total = None
    for s, b in enumerate((b0, b1, b2, b3)):
        loads[2 * s].wait()
        hidden, slope[s] = gelu_and_slope(dot(low, weight(0, s), NORMAL) + row_of(b))
        loads[2 * s + 1].wait()
        term = dot(hidden, weight(1, s), BOTH_LAST)
        total = term if s == 0 else total + term
    residual = normed + (total + row_of(b_down))
    center = residual - row_mean(residual)
    rstd_two = lax.rsqrt(row_mean(center * center) + EPSILON)
    unit_two = center * rstd_two
    layer[...] = (unit_two * row_of(g_two) + row_of(s_two)).astype(bf16)
    scaled = ct * row_of(g_two)
    grad_two = rstd_two * (scaled - row_mean(scaled) - unit_two * row_mean(scaled * unit_two))
    low_two = grad_two.astype(bf16)
    pack[FFN:OUT, :] = low_two
    total = None
    for s in range(NN):
        pre = (slope[s] * dot(low_two, weight(1, s), NORMAL)).astype(bf16)
        term = dot(pre, weight(0, s), BOTH_LAST)
        total = term if s == 0 else total + term
    grad = grad_two + total
    scaled = grad * row_of(g_one)
    one = rstd * (scaled - row_mean(scaled) - unit * row_mean(scaled * unit))
    grad_one[...] = one
    low_one = one.astype(bf16)
    every = dot(low_one, w_out[...], BOTH_LAST)
    for s in range(NN):
        for r in range(R):
            for h in range(NH):
                block = every[r * C : (r + 1) * C, s * E + h * HD : s * E + (h + 1) * HD]
                slot = jnp.concatenate([block[0 : C // 2], block[C // 2 :]], axis=1).astype(bf16)
                slots[(r * NH + h) * NN + (n + NN - s) % NN] = slot
    stores = copies([(slots, slots_far), (grad_one, one_far), (layer, layer_far)], sems)
    pack[OUT:LAST, :] = low_one
    stores += copies([(pack, pack_far)], sems.at[3:])
    sums = [ct * unit_two, ct, low_two.astype(f32), grad * unit, grad, low_one.astype(f32)]
    totals[...] = jnp.concatenate([column_sum(t) for t in sums] + [jnp.zeros((10, D), f32)], axis=0).astype(bf16)
    stores += copies([(totals, sums_far)], sems.at[4:])
    for store in stores:
        store.wait()


def hidden_kernel(a0, a1, a2, a3, every_far, b_up, hidden_far, slope_far, firsts, weights, hidden, slope, sems):
    pairs = [(p, firsts.at[s]) for s, p in enumerate((a0, a1, a2, a3))] + [(every_far.at[0, :, 0], weights)]
    for load in copies(pairs, sems):
        load.wait()
    normed = firsts[:, NORMED:FIRST, :].reshape(TOK, D)
    act, slant = gelu_and_slope(dot(normed, weights[...].reshape(D, F), NORMAL) + row_of(b_up))
    hidden[...] = act
    slope[...] = slant
    for store in copies([(hidden, hidden_far), (slope, slope_far)], sems):
        store.wait()


def weights_kernel(
    a0, a1, a2, a3, p0, p1, p2, p3, every_far, hidden_far, slope_far,
    send0_far, send1_far, send2_far, send3_far, keep_far, out_whole, bias,
    firsts, packs, weights, hidden, slope, whole, sems,
):
    c = lax.axis_index("dp")
    pairs = [(every_far.at[1, :, 0], weights), (slope_far, slope)]
    pairs += [(p, packs.at[s]) for s, p in enumerate((p0, p1, p2, p3))]
    pairs += [(p, firsts.at[s]) for s, p in enumerate((a0, a1, a2, a3))] + [(hidden_far, hidden)]
    loads = copies(pairs, sems)
    for load in loads[:6]:
        load.wait()
    grad_ffn = packs[:, FFN:OUT, :].reshape(TOK, D)
    pre = (slope[...] * dot(grad_ffn, weights[...].reshape(D, F), NORMAL)).astype(bf16)
    for load in loads[6:]:
        load.wait()
    whole[:, 0:F] = dot(firsts[:, NORMED:FIRST, :].reshape(TOK, D), pre, BOTH_FIRST).astype(bf16)
    whole[:, F : 2 * F] = dot(grad_ffn, hidden[...], BOTH_FIRST).astype(bf16)
    half = D // 2
    pairs = [(whole.at[pl.ds(pl.multiple_of(c * half, half), half), :], keep_far)]
    for k, far in enumerate((send0_far, send1_far, send2_far, send3_far)):
        pairs.append((whole.at[pl.ds(pl.multiple_of((1 - c) * half + 96 * k, 96), 96), :], far))
    stores = copies(pairs, sems)
    heads = [firsts[s, ATTN:NORMED, 256 * r : 256 * r + E] for s in range(NN) for r in range(R)]
    heads = jnp.concatenate(heads, axis=0)
    out_whole[...] = dot(packs[:, OUT:LAST, :].reshape(TOK, D), heads, BOTH_FIRST).astype(bf16)
    bias[...] = jnp.broadcast_to(column_sum(pre.astype(f32)), (8, F))
    for store in stores:
        store.wait()


def blocks_of(block):
    return jnp.concatenate([block[:, k : k + T] for k in range(0, block.shape[1], T)], axis=0).astype(bf16)


def input_weights_kernel(x_far, got, out_whole, grad, send_far, keep_far, sums, whole, bias, x, sems):
    c = lax.axis_index("dp")
    load = copies([(x_far, x)], sems)[0]
    grads = []
    for j in range(3):
        grad_t = jnp.concatenate(
            [
                jnp.concatenate([got[r * NH + h, j * HD : (j + 1) * HD, :] for h in range(NH)], axis=0)
                for r in range(R)
            ],
            axis=1,
        )
        grads.append(grad_t.astype(f32).T.astype(bf16))
    grads = jnp.concatenate(grads, axis=1)
    grad[...] = grads
    heads = []
    for h in range(NH):
        block = got[h, 3 * HD : SLOT, :].astype(f32)
        for r in range(1, R):
            block = block + got[r * NH + h, 3 * HD : SLOT, :].astype(f32)
        heads.append(block)
    first = jnp.concatenate([b[0:1, 0:HD] + b[2:3, 0:HD] for b in heads], axis=1)
    second = jnp.concatenate([b[0:1, HD:] + b[2:3, HD:] for b in heads], axis=1)
    third = jnp.concatenate([b[1:2, 0:HD] + b[3:4, 0:HD] for b in heads], axis=1)
    row = jnp.concatenate([first, second, third], axis=1)
    total = got[0, SLOT:, :].astype(f32)
    for w in range(1, NW):
        total = total + got[w, SLOT:, :].astype(f32)
    total = jnp.concatenate([total[k : k + 8, :] for k in range(0, VECTORS, 8)], axis=1)
    row = jnp.concatenate([row, jnp.zeros((1, E), f32)], axis=1)
    sums[...] = jnp.concatenate([total[0:6, :], row, row], axis=0)
    hi, mid, lo = split3(sums[...])
    bias[...] = jnp.concatenate([hi[0:7, :], mid[0:7, :], lo[6:7, :], lo[6:7, :]], axis=0).astype(bf16)
    whole[:, 3 * E :] = out_whole[...]
    load.wait()
    whole[:, 0 : 3 * E] = dot(x[...].reshape(TOK, D), grads, BOTH_FIRST).astype(bf16)
    half = D // 2
    pairs = [(bias, send_far.at[half:, :])]
    pairs.append((whole.at[pl.ds(pl.multiple_of((1 - c) * half, half), half), :], send_far.at[0:half, :]))
    pairs.append((whole.at[pl.ds(pl.multiple_of(c * half, half), half), :], keep_far))
    for store in copies(pairs, sems):
        store.wait()


def input_back_kernel(
    wq, wk, wv, grad, part0_far, part1_far, part2_far, part3_far, part0, part1, part2, part3, wide_part, near, sems
):
    n = lax.axis_index("narrow")
    for load in copies([(wq, near.at[0]), (wk, near.at[1]), (wv, near.at[2])], sems):
        load.wait()
    wide_part[...] = dot(grad[...], near[...].reshape(3 * E, D), NORMAL)
    for r in range(R):
        to = slice(r * C, (r + 1) * C)
        part0[to, :] = wide_part[chunk_rows(n, r), :]
        for s, part in ((1, part1), (2, part2), (3, part3)):
            part[to, :] = wide_part[chunk_rows((n + s) % NN, r), :].astype(bf16)
    pairs = [(part0, part0_far), (part1, part1_far), (part2, part2_far), (part3, part3_far)]
    for store in copies(pairs, sems):
        store.wait()


def first_add_kernel(keep_far, got0, got1, got2, got3, bias, bias_got, slots_far, keep, got, slots, more, sems):
    pairs = [(far, got.at[96 * k : 96 * (k + 1), :]) for k, far in enumerate((got0, got1, got2, got3))]
    loads = copies([*pairs, (keep_far, keep)], sems)
    row = bias[...] + bias_got[...]
    row = jnp.concatenate([row[0:1, k : k + T] for k in range(0, F, T)] + [jnp.zeros((10, T), f32)], axis=0)
    for w in range(NW):
        more[w] = row.astype(bf16)
    for load in loads:
        load.wait()
    stores = copies([(more, slots_far.at[:, FIRST_ROWS + LAST_ROWS :, :])], sems.at[NW:])
    for w in range(NW):
        at = slice(w * G, (w + 1) * G)
        slots[w] = blocks_of(keep[at, :].astype(f32) + got[at, :].astype(f32))
        stores += copies([(slots.at[w], slots_far.at[w, 0:FIRST_ROWS, :])], sems.at[w:])
    for store in stores:
        store.wait()


def last_add_kernel(
    keep_far, slots_in, got_far, sums, slots_far, b_q, b_k, b_v, g_two, s_two, b_down, g_one, s_one, b_out,
    keep, got, slots, sems,
):
    for load in copies([(keep_far, keep), (got_far, got)], sems):
        load.wait()
    stores = []
    for w in range(NW):
        at = slice(w * G, (w + 1) * G)
        slots[w] = blocks_of(keep[at, :].astype(f32) + got[at, :].astype(f32))
        stores += copies([(slots.at[w], slots_far.at[w, FIRST_ROWS : FIRST_ROWS + LAST_ROWS, :])], sems.at[w:])
    other = got[D // 2 :, :].astype(f32)
    hi, mid, lo = split3(sums[...])
    total = (hi[0:7, :] + other[0:7, :]) + (mid[0:7, :] + other[7:14, :])
    bias = total[6:7, :] + (lo[6:7, :] + other[14:15, :])
    for k, ref in enumerate((b_q, b_k, b_v)):
        ref[...] = bias[:, k * E : (k + 1) * E].reshape(E)
    for k, ref in enumerate((g_two, s_two, b_down, g_one, s_one, b_out)):
        ref[...] = total[k : k + 1, :].reshape(D)
    for store in stores:
        store.wait()


def last_sum_kernel(got, g_q, g_k, g_v, out, up, down, b_up):
    total = got[0].astype(f32)
    for w in range(1, NW):
        total = total + got[w].astype(f32)
    end = FIRST_ROWS + LAST_ROWS
    b_up[...] = jnp.concatenate([total[end + k : end + k + 1, :] for k in range(F // T)], axis=1).reshape(F)
    total = jnp.concatenate([total[k : k + G, :] for k in range(0, end, G)], axis=1)
    up[...] = total[:, 0:F]
    down[...] = total[:, F : 2 * F]
    for k, ref in enumerate((g_q, g_k, g_v, out)):
        ref[...] = total[:, 2 * F + k * E : 2 * F + (k + 1) * E]


def input_chunk_kernel(part_far, one_far, part1, part2, part3, low, part0, grad_one, sems):
    for load in copies([(part_far, part0), (one_far, grad_one)], sems):
        load.wait()
    total = part0[...] + part1[...].astype(f32) + part2[...].astype(f32) + part3[...].astype(f32)
    low[...] = (grad_one[...] + total).astype(bf16)


def spread_kernel(g0, g1, g2, g3, out):
    n = lax.axis_index("narrow")
    for s, part in enumerate((g0, g1, g2, g3)):
        at = pl.ds(pl.multiple_of((n + NN - s) % NN * C, C), C)
        for r in range(R):
            out[r, at, :] = part[r * C : (r + 1) * C, :].astype(f32)


def shifted(x, s):
    return lax.ppermute(x, "narrow", [(i, (i + s) % NN) for i in range(NN)])


def gather_narrow(x):
    return (x, shifted(x, 1), shifted(x, 2), shifted(x, 3))


def scatter_narrow(parts):
    return (parts[0], shifted(parts[1], 1), shifted(parts[2], 2), shifted(parts[3], 3))


def other_core(x):
    return lax.ppermute(x, "dp", [(0, 1), (1, 0)])


def exchange(slots):
    return lax.all_to_all(slots, "wide", 0, 0, tiled=True)


def exchange_all(slots):
    return lax.all_to_all(slots, ("wide", "narrow"), 0, 0, tiled=True)


def body(
    hidden_in, segments, weight_query, bias_query, weight_key, bias_key, weight_value, bias_value,
    weight_out, bias_out, gain_one, shift_one, weight_up, bias_up, weight_down, bias_down,
    gain_two, shift_two, cotangent,
):
    frequency = np.repeat(np.power(10000.0, -np.arange(0, HD, 2) / HD), 2).astype(np.float32)
    frequency = jnp.asarray(np.broadcast_to(frequency[:, None], (HD, T)))
    shard = jnp.where(lax.axis_index("dp") == 0, weight_up, weight_down.T)
    shards = gather_narrow(shard)
    mine = lax.dynamic_slice_in_dim(weight_out, lax.axis_index("dp") * (E // 2), E // 2, 0)
    weights_got = gather_narrow(mine)[1:]
    weights_out = (weight_out, *weights_got, *(other_core(w) for w in weights_got))
    biases_up = gather_narrow(bias_up)
    query_t, key_t, value_t = weight_query.T, weight_key.T, weight_value.T

    slots, token = call(
        "project",
        project_kernel,
        [((NW, SLOT, T), bf16)],
        (hidden_in, segments, query_t, bias_query, key_t, bias_key, value_t, bias_value),
        scratch=[
            pltpu.VMEM((R, T, D), bf16),
            pltpu.VMEM((3, E, D), bf16),
            pltpu.VMEM((E,), f32),
            pltpu.VMEM((E,), f32),
            pltpu.VMEM((E,), f32),
            pltpu.VMEM((R, T), jnp.int32),
            pltpu.SemaphoreType.DMA((8,)),
        ],
        far_in=range(8),
        token=True,
    )
    (shards,) = call(
        "stack",
        stack_kernel,
        [((NN, D // NW, F), bf16)],
        shards,
        scratch=[pltpu.SemaphoreType.DMA((NN,))],
        any_in=range(NN),
        far=(0,),
        after=(token,),
    )
    every = lax.all_gather(shards, ("dp", "wide")).reshape(2, NW, NN, D // NW, F)
    got = exchange(slots)
    out_slots, *saved = call(
        "attend",
        attend_kernel,
        [
            ((NW * NN, C // 2, 2 * HD), bf16),
            ((AUG, L), bf16),
            ((AUG, L), bf16),
            ((L, HD), bf16),
            ((L, AUG), bf16),
            ((L, AUG), bf16),
            ((HD, L), f32),
            ((HD, L), f32),
            ((HD, L), f32),
        ],
        (got, frequency),
        scratch=[
            pltpu.VMEM((NW * NN, C // 2, 2 * HD), bf16),
            pltpu.VMEM((AUG, L), bf16),
            pltpu.VMEM((AUG, L), bf16),
            pltpu.VMEM((AUG, L), bf16),
            pltpu.VMEM((L, HD), bf16),
            pltpu.VMEM((L, AUG), bf16),
            pltpu.VMEM((L, AUG), bf16),
            pltpu.VMEM((HD, L), f32),
            pltpu.VMEM((HD, L), f32),
            pltpu.VMEM((HD, L), f32),
            pltpu.VMEM((L, 256), f32),
            pltpu.VMEM((L, 256), f32),
            pltpu.VMEM((16, L), f32),
            pltpu.SemaphoreType.DMA((9,)),
        ],
        mib=24,
        after=weights_got,
        far=range(9),
    )
    attn = exchange_all(out_slots)
    chunk_f32, chunk_low = ((CH, D), f32), ((CH, D), bf16)
    parts4 = [chunk_f32, chunk_low, chunk_low, chunk_low]
    slot_shape = (NW * NN, C // 2, 2 * HD)
    w_out, state, *firsts, token = call(
        "first",
        first_kernel,
        [((D, D), bf16), ((CH, D + T), f32)] + [((FIRST, D), bf16)] * NN,
        (*weights_out, hidden_in, attn, bias_out, gain_one, shift_one),
        scratch=[
            pltpu.VMEM((D, D), bf16),
            pltpu.VMEM((CH, D + T), f32),
            pltpu.VMEM((CH, D), bf16),
            pltpu.VMEM((NN, FIRST, D), bf16),
            pltpu.SemaphoreType.DMA((7,)),
        ],
        far_in=range(7),
        far=range(6),
        token=True,
        after=biases_up[1:],
    )
    firsts = (firsts[0], *(shifted(firsts[s], NN - s) for s in range(1, NN)))
    every = later(every, token)
    slots, grad_one, pack, layer, totals = call(
        "middle",
        middle_kernel,
        [(slot_shape, bf16), chunk_f32, ((LAST, D), bf16), chunk_low, ((16, D), bf16)],
        (
            every, state, cotangent, w_out, gain_one, shift_one, biases_up[0], bias_down, gain_two, shift_two,
            *biases_up[1:],
        ),
        scratch=[
            pltpu.VMEM((CH, D + T), f32),
            pltpu.VMEM((R, T, D), bf16),
            pltpu.VMEM((D, D), bf16),
            *[pltpu.VMEM((D,), f32)] * 6,
            pltpu.VMEM((2, NN, NW, D // NW, F), bf16),
            pltpu.VMEM((NN, CH, F), f32),
            pltpu.VMEM((CH, D), f32),
            pltpu.VMEM(slot_shape, bf16),
            pltpu.VMEM((LAST, D), bf16),
            pltpu.VMEM((CH, D), bf16),
            pltpu.VMEM((16, D), bf16),
            pltpu.SemaphoreType.DMA((17,)),
        ],
        mib=32,
        far_in=range(10),
        far=range(5),
    )
    got = exchange_all(later(slots, *firsts[1:]))
    firsts = (firsts[0], firsts[3], firsts[2], firsts[1])
    hidden, slope = call(
        "hidden",
        hidden_kernel,
        [((TOK, F), bf16), ((TOK, F), f32)],
        (*firsts, every, bias_up),
        scratch=[
            pltpu.VMEM((NN, FIRST, D), bf16),
            pltpu.VMEM((NW, D // NW, F), bf16),
            pltpu.VMEM((TOK, F), bf16),
            pltpu.VMEM((TOK, F), f32),
            pltpu.SemaphoreType.DMA((5,)),
        ],
        far_in=range(5),
        far=(0, 1),
    )
    totals = gather_narrow(totals)
    packs = gather_narrow(later(pack, hidden, got, *totals[1:]))
    slots, token = call(
        "attend_back",
        attend_back_kernel,
        [((NW, SLOT + VECTORS, T), bf16)],
        (got, *saved, *totals),
        scratch=[
            pltpu.VMEM((NW, SLOT + VECTORS, T), bf16),
            pltpu.VMEM((NN, 16, D), bf16),
            pltpu.VMEM((NN, 16, D), f32),
            pltpu.VMEM((NW * NN, C // 2, 2 * HD), bf16),
            pltpu.VMEM((HD, L), f32),
            pltpu.VMEM((AUG, L), bf16),
            pltpu.VMEM((AUG, L), bf16),
            pltpu.VMEM((HD, L), f32),
            pltpu.VMEM((HD, L), f32),
            pltpu.VMEM((AUG, L), bf16),
            pltpu.VMEM((L, HD), bf16),
            pltpu.VMEM((L, HD), bf16),
            pltpu.VMEM((L, AUG), bf16),
            pltpu.VMEM((L, AUG), bf16),
            pltpu.VMEM((HD, L), f32),
            pltpu.SemaphoreType.DMA((NW + 1,)),
        ],
        far_in=range(13),
        far=(0,),
        token=True,
    )
    *sends, up_keep, out_whole, bias = call(
        "weights",
        weights_kernel,
        [((96, 2 * F), bf16)] * 4 + [((D // 2, 2 * F), bf16), ((D, E), bf16), ((8, D), f32)],
        (*firsts, *packs, every, hidden, slope),
        scratch=[
            pltpu.VMEM((NN, FIRST, D), bf16),
            pltpu.VMEM((NN, LAST, D), bf16),
            pltpu.VMEM((NW, D // NW, F), bf16),
            pltpu.VMEM((TOK, F), bf16),
            pltpu.VMEM((TOK, F), f32),
            pltpu.VMEM((D, 2 * F), bf16),
            pltpu.SemaphoreType.DMA((11,)),
        ],
        mib=32,
        far_in=range(11),
        far=range(5),
        cost=COST,
        after=(token,),
    )
    got = exchange(slots)
    last_shape = (NW, FIRST_ROWS + LAST_ROWS + BIAS_ROWS, T)
    slots, added = call(
        "first_add",
        first_add_kernel,
        [(last_shape, bf16)],
        (up_keep, *(other_core(send) for send in sends), bias, other_core(bias)),
        scratch=[
            pltpu.VMEM((D // 2, 2 * F), bf16),
            pltpu.VMEM((D // 2, 2 * F), bf16),
            pltpu.VMEM((NW, FIRST_ROWS, T), bf16),
            pltpu.VMEM((NW, BIAS_ROWS, T), bf16),
            pltpu.SemaphoreType.DMA((NW + 1,)),
        ],
        far_in=(0,),
        any_in=range(1, 5),
        far=(0,),
        token=True,
    )
    grad, send, keep, sums = call(
        "input_weights",
        input_weights_kernel,
        [((TOK, 3 * E), bf16), ((D // 2 + 16, D), bf16), ((D // 2, D), bf16), ((8, D), f32)],
        (hidden_in, got, out_whole),
        scratch=[
            pltpu.VMEM((D, D), bf16),
            pltpu.VMEM((16, D), bf16),
            pltpu.VMEM((R, T, D), bf16),
            pltpu.SemaphoreType.DMA((3,)),
        ],
        far_in=(0,),
        far=(1, 2),
        after=(added,),
    )
    *parts, done = call(
        "input_back",
        input_back_kernel,
        parts4,
        (query_t, key_t, value_t, grad),
        scratch=[
            pltpu.VMEM((CH, D), f32),
            pltpu.VMEM((CH, D), bf16),
            pltpu.VMEM((CH, D), bf16),
            pltpu.VMEM((CH, D), bf16),
            pltpu.VMEM((TOK, D), f32),
            pltpu.VMEM((3, E, D), bf16),
            pltpu.SemaphoreType.DMA((4,)),
        ],
        far_in=range(3),
        far=range(4),
        token=True,
    )
    slots, b_query, b_key, b_value, g_two, s_two, b_down, g_one, s_one, b_out, token = call(
        "last_add",
        last_add_kernel,
        [(last_shape, bf16)] + [((E,), f32)] * 3 + [((D,), f32)] * 6,
        (keep, slots, other_core(send), sums),
        scratch=[
            pltpu.VMEM((D // 2, D), bf16),
            pltpu.VMEM((D // 2 + 16, D), bf16),
            pltpu.VMEM((NW, LAST_ROWS, T), bf16),
            pltpu.SemaphoreType.DMA((NW,)),
        ],
        far_in=range(2),
        any_in=(2,),
        far=(0,),
        aliases={1: 0},
        after=(done,),
        token=True,
    )
    parts = scatter_narrow([parts[0], *(later(part, anywhere=(token,)) for part in parts[1:])])
    (input_low,) = call("input_chunk", input_chunk_kernel, [chunk_low], (parts[0], grad_one, *parts[1:]),
        scratch=[pltpu.VMEM((CH, D), f32), pltpu.VMEM((CH, D), f32), pltpu.SemaphoreType.DMA((2,))],
        far_in=(0, 1),
    )
    layers = gather_narrow(later(layer, anywhere=(token,)))
    whole_out = ((R, T, D), f32)
    (layer_out,) = call("layer_out", spread_kernel, [whole_out], layers)
    (grad_input,) = call("grad_input", spread_kernel, [whole_out], gather_narrow(input_low))
    g_query, g_key, g_value, g_out, grad_up, grad_down, b_up = call(
        "last_sum", last_sum_kernel, [((G, E), f32)] * 4 + [((G, F), f32)] * 2 + [((F,), f32)], (exchange(slots),)
    )
    return (
        layer_out, grad_input, g_query, b_query, g_key, b_key, g_value, b_value, g_out.T, b_out,
        g_one, s_one, grad_up, b_up, grad_down.T, b_down, g_two, s_two,
    )


def solution(mesh):
    tokens, whole = P("dp", "wide", None), P()
    column, vector = P(None, "narrow"), P("narrow")
    rows_split, columns_split = P(("dp", "wide"), "narrow"), P("narrow", ("dp", "wide"))
    in_specs = (
        tokens, P("dp", "wide"), column, vector, column, vector, column, vector, P("narrow", None), whole,
        whole, whole, P("wide", "narrow"), vector, P("narrow", "wide"), whole, whole, whole, tokens,
    )
    out_specs = (
        tokens, tokens, rows_split, vector, rows_split, vector, rows_split, vector, columns_split, whole,
        whole, whole, rows_split, vector, columns_split, whole, whole, whole,
    )
    return jax.shard_map(body, mesh=mesh, in_specs=in_specs, out_specs=out_specs, check_vma=False)
```

```python
import functools
import math

import jax
import jax.numpy as jnp
import numpy as np
from jax import lax
from jax.experimental import pallas as pl
from jax.experimental.pallas import tpu as pltpu
from jax.sharding import PartitionSpec as P

D = 768
HD = 64
R = 3
T = 128
NH = 3
E = NH * HD
F = 768
NW = 16
NN = 4
TOK = R * T
L = NW * T
C = T // NN
CH = R * C
PAIRS = R * NH
G = D // (2 * NW)
FIRST_ROWS, LAST_ROWS, BIAS_ROWS = 12 * G, 6 * G, 16
SLOT = 3 * HD + 16
VECTORS = 8 * D // T
AUG = HD + 16
EPSILON = 1e-12
BIG = 1e30
LOG2E = math.log2(math.e)
LN2 = math.log(2.0)
COST = 10**11
f32, bf16 = jnp.float32, jnp.bfloat16


def dot(a, b, dims):
    return lax.dot_general(a, b, (dims, ((), ())), preferred_element_type=f32)


NORMAL, BOTH_LAST, BOTH_FIRST = ((1,), (0,)), ((1,), (1,)), ((0,), (0,))


def in_far_memory(arrays):
    return [pltpu.with_memory_space_constraint(a, pltpu.HBM) if a.size > 1024 else a for a in arrays]


def call(
    name, kernel, outs, args, scratch=(), cost=1024, mib=16, after=(), far_in=(), any_in=(), near=(), far=(), aliases={},
    token=False,
):
    if token:
        outs = [*outs, ((8, 128), f32)]

    def run(*refs):
        end = len(args) + len(after)
        if token:
            at = end + len(outs) - 1
            refs[at][...] = jnp.zeros((8, 128), f32)
            refs = refs[:at] + refs[at + 1 :]
        kernel(*refs[: len(args)], *refs[end:])

    def shape(k, s, t):
        return pltpu.VMEM(s, t) if k in near else pltpu.HBM(s, t) if k in far else jax.ShapeDtypeStruct(s, t)

    args = [pltpu.with_memory_space_constraint(a, pltpu.HBM) if k in far_in else a for k, a in enumerate(args)]
    after = in_far_memory(after)
    return pl.pallas_call(
        run,
        out_shape=[shape(k, s, t) for k, (s, t) in enumerate(outs)],
        in_specs=[
            pl.BlockSpec(memory_space=pltpu.HBM if k in far_in else pl.ANY if k in any_in else pltpu.VMEM)
            for k in range(len(args))
        ]
        + [pl.BlockSpec(memory_space=pl.ANY) for _ in after],
        out_specs=[pl.BlockSpec(memory_space=pltpu.HBM if k in far else pltpu.VMEM) for k in range(len(outs))],
        scratch_shapes=list(scratch),
        input_output_aliases=aliases,
        compiler_params=pltpu.CompilerParams(vmem_limit_bytes=mib * 1024 * 1024),
        cost_estimate=pl.CostEstimate(flops=cost, bytes_accessed=1024, transcendentals=0),
        name=name,
    )(*args, *after)


def later(x, *after, anywhere=()):
    after = [*in_far_memory(after), *anywhere]
    return pl.pallas_call(
        lambda *refs: None,
        out_shape=jax.ShapeDtypeStruct(x.shape, x.dtype),
        in_specs=[pl.BlockSpec(memory_space=pltpu.HBM)] + [pl.BlockSpec(memory_space=pl.ANY) for _ in after],
        out_specs=pl.BlockSpec(memory_space=pltpu.HBM),
        input_output_aliases={0: 0},
        cost_estimate=pl.CostEstimate(flops=1024, bytes_accessed=1024, transcendentals=0),
        name="later",
    )(x, *after)


def copies(pairs, sems):
    made = [pltpu.make_async_copy(a, b, sems.at[k]) for k, (a, b) in enumerate(pairs)]
    for copy in made:
        copy.start()
    return made


def row_of(ref):
    return ref[...].reshape(1, ref.shape[-1])


def split3(v):
    hi = v.astype(bf16).astype(f32)
    rest = v - hi
    mid = rest.astype(bf16).astype(f32)
    return hi, mid, (rest - mid).astype(bf16).astype(f32)


def sine_cosine(angle):
    turns = jnp.floor(angle * (2.0 / math.pi) + 0.5)
    r = ((angle - turns * 1.5703125) - turns * 4.837512969970703125e-4) - turns * 7.54978995489188e-8
    z = r * r
    sine = r + r * z * (-1.6666654611e-1 + z * (8.3321608736e-3 + z * -1.9515295891e-4))
    cosine = 1.0 - 0.5 * z + z * z * (4.166664568298827e-2 + z * (-1.388731625493765e-3 + z * 2.443315711809948e-5))
    quarter = turns - 4.0 * jnp.floor(turns * 0.25)
    odd = (quarter == 1.0) | (quarter == 3.0)
    sin_abs = jnp.where(odd, cosine, sine)
    cos_abs = jnp.where(odd, sine, cosine)
    return jnp.where(quarter >= 2.0, -sin_abs, sin_abs), jnp.where((quarter == 1.0) | (quarter == 2.0), -cos_abs, cos_abs)


def swap_pairs(t):
    rows = lax.broadcasted_iota(jnp.int32, t.shape, 0)
    return jnp.where(rows % 2 == 0, pltpu.roll(t, HD - 1, 0), pltpu.roll(t, 1, 0))


def project_kernel(x_far, seg, wq, bq, wk, bk, wv, bv, slots, x, near, bias0, bias1, bias2, ids, sems):
    pairs = [(x_far, x), (wq, near.at[0]), (bq, bias0), (wk, near.at[1]), (bk, bias1)]
    pairs += [(wv, near.at[2]), (bv, bias2), (seg, ids)]
    loads = copies(pairs, sems)
    for load in loads:
        load.wait()
    flat = x[...].reshape(TOK, D)
    for j, b in enumerate((bias0, bias1, bias2)):
        w = near.at[j]
        bias = jnp.broadcast_to(row_of(b), (T, E)).T
        yt = (dot(w[...], flat, BOTH_LAST) + jnp.concatenate([bias] * R, axis=1)).astype(bf16)
        for r in range(R):
            for h in range(NH):
                slots[r * NH + h, j * HD : (j + 1) * HD, :] = yt[h * HD : (h + 1) * HD, r * T : (r + 1) * T]
    for r in range(R):
        block = jnp.broadcast_to(ids[r : r + 1, :].astype(f32), (16, T)).astype(bf16)
        for h in range(NH):
            slots[r * NH + h, 3 * HD :, :] = block


def stack_kernel(a, b, c, d, out, sems):
    for copy in copies([(part, out.at[s]) for s, part in enumerate((a, b, c, d))], sems):
        copy.wait()


def attend_kernel(
    got, freq, out_far, q_far, k_far, qn_far, kn_far, vn_far, o_far, cos_far, sin_far,
    out, q_t, k_t, v_t, q_nat, k_nat, v_nat, o_t, cos_t, sin_t, s_even, s_odd, lse_t, sems,
):
    @pl.when(lax.axis_index("wide") < PAIRS)
    def _():
        ids = [got[w, 3 * HD :, :].astype(f32)[0:1, :] for w in range(NW)]
        starts = []
        for d in range(1, 5):
            below = jnp.zeros((1, T), f32)
            for w in range(NW):
                below = below + jnp.where(ids[w] < d, 1.0, 0.0)
            starts.append(jnp.sum(below, axis=1, keepdims=True))
        odd = lax.broadcasted_iota(jnp.int32, (HD, T), 0) % 2 == 1
        ext = lax.broadcasted_iota(jnp.int32, (16, T), 0)
        lane = lax.broadcasted_iota(jnp.int32, (1, T), 1).astype(f32)
        for w in range(NW):
            at = slice(w * T, (w + 1) * T)
            start = jnp.zeros((1, T), f32)
            for d in range(1, 5):
                start = jnp.where(ids[w] == d, starts[d - 1], start)
            sine, cosine = sine_cosine(freq[...] * (lane + (w * T) - start))
            sine = jnp.where(odd, sine, -sine)
            cos_t[:, at] = cosine
            sin_t[:, at] = sine
            query = got[w, 0:HD, :].astype(f32)
            key = got[w, HD : 2 * HD, :].astype(f32)
            query = (query * cosine + swap_pairs(query) * sine) * (HD**-0.5 * LOG2E)
            key = key * cosine + swap_pairs(key) * sine
            same = ids[w] == ext.astype(f32)
            doc = ext < 5
            key_ext = jnp.where(doc, jnp.where(same, 1.0, 0.0), jnp.where(ext < 8, 1.0, 0.0))
            q_t[0:HD, at] = query.astype(bf16)
            q_t[HD:AUG, at] = jnp.where(doc, jnp.where(same, 0.0, -BIG), 0.0).astype(bf16)
            k_t[0:HD, at] = key.astype(bf16)
            k_t[HD:AUG, at] = key_ext.astype(bf16)
            k_nat[at, :] = jnp.concatenate([key, key_ext], axis=0).T.astype(bf16)
            value = got[w, 2 * HD : 3 * HD, :].astype(f32)
            value = jnp.concatenate([value, jnp.where(ext < 3, 1.0, 0.0)], axis=0)
            v_t[:, at] = value.astype(bf16)
            v_nat[at, :] = value.T.astype(bf16)
            q_nat[at, :] = query.T.astype(bf16)

        pairs = [(k_t, k_far), (cos_t, cos_far), (sin_t, sin_far), (q_nat, qn_far), (k_nat, kn_far), (v_nat, vn_far)]
        stores = copies(pairs, sems)

        def scores(i, s_ref):
            at = pl.ds(pl.multiple_of(i * 256, 256), 256)
            s_ref[...] = dot(k_nat[...], q_t[:, at], NORMAL)

        def tile(i, s_ref):
            at = pl.ds(pl.multiple_of(i * 256, 256), 256)
            s = s_ref[...]
            top = jnp.max(s, axis=0, keepdims=True)
            p = jnp.exp2(s - top).astype(bf16)
            o = dot(v_t[...], p, NORMAL)
            total = o[HD : HD + 1, :]
            o = o[0:HD, :] / total
            o_t[:, at] = o
            natural = o.T
            for j in range(2 * NN):
                block = natural[j * C : (j + 1) * C, :]
                out[2 * NN * i + j] = jnp.concatenate([block[0 : C // 2], block[C // 2 :]], axis=1).astype(bf16)
            hi, mid, lo = split3(-(top + jnp.log(total) * LOG2E))
            rows = lax.broadcasted_iota(jnp.int32, (16, 256), 0)
            more = jnp.where(rows == 5, hi, jnp.where(rows == 6, mid, jnp.where(rows == 7, lo, 0.0)))
            lse_t[:, at] = more

        def two_tiles(k, carry):
            scores(2 * k + 1, s_odd)
            tile(2 * k, s_even)
            scores(jnp.minimum(2 * k + 2, L // 256 - 1), s_even)
            tile(2 * k + 1, s_odd)
            return carry

        scores(0, s_even)
        lax.fori_loop(0, L // 512, two_tiles, 0)
        q_t[HD:AUG, :] = (q_t[HD:AUG, :].astype(f32) + lse_t[...]).astype(bf16)
        last = [(out, out_far, 6), (q_t, q_far, 7), (o_t, o_far, 8)]
        last = [pltpu.make_async_copy(a, b, sems.at[k]) for a, b, k in last]
        for store in last:
            store.start()
        for store in stores + last:
            store.wait()


def attend_back_kernel(
    got_far, q_far, k_far, qn_far, kn_far, vn_far, o_far, cos_far, sin_far, v0, v1, v2, v3, out_far,
    out, near, vectors, got, o_t, q_t, k_t, cos_t, sin_t, do_t, do_nat, q_nat, k_nat, v_nat, dq_t, sems,
):
    n, attends = lax.axis_index("narrow"), lax.axis_index("wide") < PAIRS
    pairs = [(got_far, got), (o_far, o_t), (qn_far, q_nat), (kn_far, k_nat), (vn_far, v_nat), (q_far, q_t)]
    pairs += [(k_far, k_t), (cos_far, cos_t), (sin_far, sin_t)]
    loads = [pltpu.make_async_copy(a, b, sems.at[k]) for k, (a, b) in enumerate(pairs)]

    @pl.when(attends)
    def _():
        for load in loads:
            load.start()

    for s, load in enumerate(copies([(v, near.at[s]) for s, v in enumerate((v0, v1, v2, v3))], sems.at[len(loads) :])):
        load.wait()
        vectors[(n + NN - s) % NN] = near[s].astype(f32)
    total = (vectors[0] + vectors[1] + vectors[2] + vectors[3])[0:8, :]
    block = jnp.concatenate([total[:, k : k + T] for k in range(0, D, T)], axis=0).astype(bf16)
    for w in range(NW):
        out[w, SLOT:, :] = block
    store = copies([(out.at[:, SLOT:, :], out_far.at[:, SLOT:, :])], sems.at[NW:])[0]

    @pl.when(attends)
    def _():
        ext = lax.broadcasted_iota(jnp.int32, (16, T), 0)
        for load in loads[:2]:
            load.wait()
        for w in range(NW):
            at = slice(w * T, (w + 1) * T)
            pieces = []
            for n in range(NN):
                piece = got[w * NN + n].astype(f32)
                pieces += [piece[:, 0:HD], piece[:, HD:]]
            natural = jnp.concatenate(pieces, axis=0)
            do_nat[at, :] = natural.astype(bf16)
            grad = natural.T
            delta = -jnp.sum(grad * o_t[:, at], axis=0, keepdims=True)
            hi, mid, lo = split3(delta)
            do_t[0:HD, at] = grad.astype(bf16)
            do_t[HD:AUG, at] = jnp.where(
                ext == 0, hi, jnp.where(ext == 1, mid, jnp.where(ext == 2, lo, 0.0))
            ).astype(bf16)
        dq_t[...] = jnp.zeros((HD, L), f32)
        for load in loads[2:]:
            load.wait()

        def folded(t):
            total = t[:, 0:T]
            for k in range(1, t.shape[1] // T):
                total = total + t[:, k * T : (k + 1) * T]
            return total

        def tile(j, carry):
            sum_key, sum_value = carry
            at = pl.ds(pl.multiple_of(j * 256, 256), 256)
            p = jnp.exp2(dot(k_nat[at, :], q_t[...], NORMAL))
            dp = dot(v_nat[at, :], do_t[...], NORMAL)
            ds = (p * dp).astype(bf16)
            dv = dot(p.astype(bf16), do_nat[...], NORMAL).T.astype(bf16)
            dk = dot(ds, q_nat[...], NORMAL).T * LN2
            dk = (dk * cos_t[:, at] - swap_pairs(dk) * sin_t[:, at]).astype(bf16)
            dq_t[...] += dot(k_t[0:HD, at], ds, NORMAL)
            for k in range(2):
                out[2 * j + k, HD : 2 * HD, :] = dk[:, k * T : (k + 1) * T]
                out[2 * j + k, 2 * HD : 3 * HD, :] = dv[:, k * T : (k + 1) * T]
            return sum_key + folded(dk.astype(f32)), sum_value + folded(dv.astype(f32))

        zero = jnp.zeros((HD, T), f32)
        sum_key, sum_value = lax.fori_loop(0, L // 256, tile, (zero, zero), unroll=2)
        sum_query = zero
        stores = []
        for w in range(NW):
            at = slice(w * T, (w + 1) * T)
            dq = dq_t[:, at] * (HD**-0.5)
            dq = (dq * cos_t[:, at] - swap_pairs(dq) * sin_t[:, at]).astype(bf16)
            out[w, 0:HD, :] = dq
            stores += copies([(out.at[w, 0 : 3 * HD, :], out_far.at[w, 0 : 3 * HD, :])], sems.at[w:])
            sum_query = sum_query + dq.astype(f32)
        rows = [jnp.sum(t.T, axis=0, keepdims=True) for t in (sum_query, sum_key, sum_value)]
        first = jnp.concatenate([rows[0], rows[1]], axis=1)
        second = jnp.concatenate([rows[2], rows[2]], axis=1)
        first_hi, second_hi = first.astype(bf16).astype(f32), second.astype(bf16).astype(f32)
        block = jnp.where(
            ext == 0,
            first_hi,
            jnp.where(ext == 1, second_hi, jnp.where(ext == 2, first - first_hi, second - second_hi)),
        )
        block = jnp.where(ext < 4, block, 0.0).astype(bf16)
        for w in range(NW):
            out[w, 3 * HD : SLOT, :] = block
        stores += copies([(out.at[:, 3 * HD : SLOT, :], out_far.at[:, 3 * HD : SLOT, :])], sems.at[NW + 1 :])
        for store in stores:
            store.wait()

    store.wait()


def chunk_rows(c, r):
    return pl.ds(pl.multiple_of(r * T + c * C, C), C)


def row_mean(t):
    return jnp.mean(t, axis=-1, keepdims=True)


def column_sum(t):
    return jnp.sum(t, axis=0, keepdims=True)


def gelu_and_slope(pre):
    half = 0.5 * (1.0 + lax.erf(pre * (2.0**-0.5)))
    return (pre * half).astype(bf16), half + pre * jnp.exp(-0.5 * pre * pre) * (1.0 / math.sqrt(2.0 * math.pi))


ATTN, NORMED, FIRST = 0, 32, 128
FFN, OUT, LAST = 0, 96, 192


def first_kernel(
    w0, m1, m2, m3, u1, u2, u3, x, attn, b_out, g_one, s_one, w_out_far, state_far, pack0, pack1, pack2, pack3,
    w_out, state, heads, packs, sems,
):
    n, c = lax.axis_index("narrow"), lax.axis_index("dp")
    pairs = [(w0, w_out.at[0:E, :])]
    for s, (mine, other) in enumerate(((m1, u1), (m2, u2), (m3, u3)), 1):
        for source, core in ((mine, c), (other, 1 - c)):
            pairs.append((source, w_out.at[pl.ds(pl.multiple_of(s * E + core * (E // 2), E // 2), E // 2), :]))
    loads = copies(pairs, sems)
    for s in range(NN):
        for r in range(R):
            for h in range(NH):
                block = attn[(r * NH + h) * NN + (n + NN - s) % NN]
                at = s * E + h * HD
                heads[r * C : r * C + C // 2, at : at + HD] = block[:, 0:HD]
                heads[r * C + C // 2 : (r + 1) * C, at : at + HD] = block[:, HD:]
    mine = pl.ds(pl.multiple_of(n * C, C), C)
    tokens = jnp.concatenate([x[r, mine, :] for r in range(R)], axis=0).astype(f32)
    for load in loads:
        load.wait()
    stores = copies([(w_out, w_out_far)], sems.at[5:])
    residual = tokens + (dot(heads[...], w_out[...], NORMAL) + row_of(b_out))
    center = residual - row_mean(residual)
    rstd = lax.rsqrt(row_mean(center * center) + EPSILON)
    unit = center * rstd
    state[:, 0:D] = unit
    state[:, D:] = jnp.broadcast_to(rstd, (CH, T))
    stores += copies([(state, state_far)], sems.at[4:])
    low = (unit * row_of(g_one) + row_of(s_one)).astype(bf16)
    for s, pack in enumerate((pack0, pack1, pack2, pack3)):
        packs[s, NORMED:FIRST, :] = low
        for r in range(R):
            packs[s, ATTN:NORMED, 256 * r : 256 * r + E] = heads[r * C : (r + 1) * C, s * E : (s + 1) * E]
        stores.append(pltpu.make_async_copy(packs.at[s], pack, sems.at[s]))
        stores[-1].start()
    for store in stores:
        store.wait()


def middle_kernel(
    every_far, state_far, cot_far, w_out_far, g_one_far, s_one_far, b0_far, b_down_far, g_two_far, s_two_far, b1, b2, b3,
    slots_far, one_far, pack_far, layer_far, sums_far,
    state, cot, w_out, g_one, s_one, b0, b_down, g_two, s_two,
    weights, slope, grad_one, slots, pack, layer, totals, sems,
):
    n = lax.axis_index("narrow")
    pairs = [(state_far, state), (cot_far, cot), (w_out_far, w_out), (g_one_far, g_one), (s_one_far, s_one)]
    pairs += [(b0_far, b0), (b_down_far, b_down), (g_two_far, g_two), (s_two_far, s_two)]
    first = copies(pairs, sems.at[8:])
    pairs = [(every_far.at[which, :, s], weights.at[which, s]) for s in range(NN) for which in range(2)]
    loads = copies(pairs, sems)
    for load in first:
        load.wait()
    mine = pl.ds(pl.multiple_of(n * C, C), C)
    ct = jnp.concatenate([cot[r, mine, :] for r in range(R)], axis=0).astype(f32)
    unit, rstd = state[:, 0:D], state[:, D : D + 1]
    normed = unit * row_of(g_one) + row_of(s_one)
    low = normed.astype(bf16)

    def weight(which, s):
        return weights[which, s].reshape(D, F)

    total = None
    for s, b in enumerate((b0, b1, b2, b3)):
        loads[2 * s].wait()
        hidden, slope[s] = gelu_and_slope(dot(low, weight(0, s), NORMAL) + row_of(b))
        loads[2 * s + 1].wait()
        term = dot(hidden, weight(1, s), BOTH_LAST)
        total = term if s == 0 else total + term
    residual = normed + (total + row_of(b_down))
    center = residual - row_mean(residual)
    rstd_two = lax.rsqrt(row_mean(center * center) + EPSILON)
    unit_two = center * rstd_two
    layer[...] = (unit_two * row_of(g_two) + row_of(s_two)).astype(bf16)
    scaled = ct * row_of(g_two)
    grad_two = rstd_two * (scaled - row_mean(scaled) - unit_two * row_mean(scaled * unit_two))
    low_two = grad_two.astype(bf16)
    pack[FFN:OUT, :] = low_two
    total = None
    for s in range(NN):
        pre = (slope[s] * dot(low_two, weight(1, s), NORMAL)).astype(bf16)
        term = dot(pre, weight(0, s), BOTH_LAST)
        total = term if s == 0 else total + term
    grad = grad_two + total
    scaled = grad * row_of(g_one)
    one = rstd * (scaled - row_mean(scaled) - unit * row_mean(scaled * unit))
    grad_one[...] = one
    low_one = one.astype(bf16)
    every = dot(low_one, w_out[...], BOTH_LAST)
    for s in range(NN):
        for r in range(R):
            for h in range(NH):
                block = every[r * C : (r + 1) * C, s * E + h * HD : s * E + (h + 1) * HD]
                slot = jnp.concatenate([block[0 : C // 2], block[C // 2 :]], axis=1).astype(bf16)
                slots[(r * NH + h) * NN + (n + NN - s) % NN] = slot
    stores = copies([(slots, slots_far), (grad_one, one_far), (layer, layer_far)], sems)
    pack[OUT:LAST, :] = low_one
    stores += copies([(pack, pack_far)], sems.at[3:])
    sums = [ct * unit_two, ct, low_two.astype(f32), grad * unit, grad, low_one.astype(f32)]
    totals[...] = jnp.concatenate([column_sum(t) for t in sums] + [jnp.zeros((10, D), f32)], axis=0).astype(bf16)
    stores += copies([(totals, sums_far)], sems.at[4:])
    for store in stores:
        store.wait()


def hidden_kernel(a0, a1, a2, a3, every_far, b_up, hidden_far, slope_far, firsts, weights, hidden, slope, sems):
    pairs = [(p, firsts.at[s]) for s, p in enumerate((a0, a1, a2, a3))] + [(every_far.at[0, :, 0], weights)]
    for load in copies(pairs, sems):
        load.wait()
    normed = firsts[:, NORMED:FIRST, :].reshape(TOK, D)
    act, slant = gelu_and_slope(dot(normed, weights[...].reshape(D, F), NORMAL) + row_of(b_up))
    hidden[...] = act
    slope[...] = slant
    for store in copies([(hidden, hidden_far), (slope, slope_far)], sems):
        store.wait()


def weights_kernel(
    a0, a1, a2, a3, p0, p1, p2, p3, every_far, hidden_far, slope_far,
    send0_far, send1_far, send2_far, send3_far, keep_far, out_whole, bias,
    firsts, packs, weights, hidden, slope, whole, sems,
):
    c = lax.axis_index("dp")
    pairs = [(every_far.at[1, :, 0], weights), (slope_far, slope)]
    pairs += [(p, packs.at[s]) for s, p in enumerate((p0, p1, p2, p3))]
    pairs += [(p, firsts.at[s]) for s, p in enumerate((a0, a1, a2, a3))] + [(hidden_far, hidden)]
    loads = copies(pairs, sems)
    for load in loads[:6]:
        load.wait()
    grad_ffn = packs[:, FFN:OUT, :].reshape(TOK, D)
    pre = (slope[...] * dot(grad_ffn, weights[...].reshape(D, F), NORMAL)).astype(bf16)
    for load in loads[6:]:
        load.wait()
    whole[:, 0:F] = dot(firsts[:, NORMED:FIRST, :].reshape(TOK, D), pre, BOTH_FIRST).astype(bf16)
    whole[:, F : 2 * F] = dot(grad_ffn, hidden[...], BOTH_FIRST).astype(bf16)
    half = D // 2
    pairs = [(whole.at[pl.ds(pl.multiple_of(c * half, half), half), :], keep_far)]
    for k, far in enumerate((send0_far, send1_far, send2_far, send3_far)):
        pairs.append((whole.at[pl.ds(pl.multiple_of((1 - c) * half + 96 * k, 96), 96), :], far))
    stores = copies(pairs, sems)
    heads = [firsts[s, ATTN:NORMED, 256 * r : 256 * r + E] for s in range(NN) for r in range(R)]
    heads = jnp.concatenate(heads, axis=0)
    out_whole[...] = dot(packs[:, OUT:LAST, :].reshape(TOK, D), heads, BOTH_FIRST).astype(bf16)
    bias[...] = jnp.broadcast_to(column_sum(pre.astype(f32)), (8, F))
    for store in stores:
        store.wait()


def blocks_of(block):
    return jnp.concatenate([block[:, k : k + T] for k in range(0, block.shape[1], T)], axis=0).astype(bf16)


def input_weights_kernel(x_far, got, out_whole, grad, send_far, keep_far, sums, whole, bias, x, sems):
    c = lax.axis_index("dp")
    load = copies([(x_far, x)], sems)[0]
    grads = []
    for j in range(3):
        grad_t = jnp.concatenate(
            [
                jnp.concatenate([got[r * NH + h, j * HD : (j + 1) * HD, :] for h in range(NH)], axis=0)
                for r in range(R)
            ],
            axis=1,
        )
        grads.append(grad_t.astype(f32).T.astype(bf16))
    grads = jnp.concatenate(grads, axis=1)
    grad[...] = grads
    heads = []
    for h in range(NH):
        block = got[h, 3 * HD : SLOT, :].astype(f32)
        for r in range(1, R):
            block = block + got[r * NH + h, 3 * HD : SLOT, :].astype(f32)
        heads.append(block)
    first = jnp.concatenate([b[0:1, 0:HD] + b[2:3, 0:HD] for b in heads], axis=1)
    second = jnp.concatenate([b[0:1, HD:] + b[2:3, HD:] for b in heads], axis=1)
    third = jnp.concatenate([b[1:2, 0:HD] + b[3:4, 0:HD] for b in heads], axis=1)
    row = jnp.concatenate([first, second, third], axis=1)
    total = got[0, SLOT:, :].astype(f32)
    for w in range(1, NW):
        total = total + got[w, SLOT:, :].astype(f32)
    total = jnp.concatenate([total[k : k + 8, :] for k in range(0, VECTORS, 8)], axis=1)
    row = jnp.concatenate([row, jnp.zeros((1, E), f32)], axis=1)
    sums[...] = jnp.concatenate([total[0:6, :], row, row], axis=0)
    hi, mid, lo = split3(sums[...])
    bias[...] = jnp.concatenate([hi[0:7, :], mid[0:7, :], lo[6:7, :], lo[6:7, :]], axis=0).astype(bf16)
    whole[:, 3 * E :] = out_whole[...]
    load.wait()
    whole[:, 0 : 3 * E] = dot(x[...].reshape(TOK, D), grads, BOTH_FIRST).astype(bf16)
    half = D // 2
    pairs = [(bias, send_far.at[half:, :])]
    pairs.append((whole.at[pl.ds(pl.multiple_of((1 - c) * half, half), half), :], send_far.at[0:half, :]))
    pairs.append((whole.at[pl.ds(pl.multiple_of(c * half, half), half), :], keep_far))
    for store in copies(pairs, sems):
        store.wait()


def input_back_kernel(
    wq, wk, wv, grad, part0_far, part1_far, part2_far, part3_far, part0, part1, part2, part3, wide_part, near, sems
):
    n = lax.axis_index("narrow")
    for load in copies([(wq, near.at[0]), (wk, near.at[1]), (wv, near.at[2])], sems):
        load.wait()
    wide_part[...] = dot(grad[...], near[...].reshape(3 * E, D), NORMAL)
    for r in range(R):
        to = slice(r * C, (r + 1) * C)
        part0[to, :] = wide_part[chunk_rows(n, r), :]
        for s, part in ((1, part1), (2, part2), (3, part3)):
            part[to, :] = wide_part[chunk_rows((n + s) % NN, r), :].astype(bf16)
    pairs = [(part0, part0_far), (part1, part1_far), (part2, part2_far), (part3, part3_far)]
    for store in copies(pairs, sems):
        store.wait()


def first_add_kernel(keep_far, got0, got1, got2, got3, bias, bias_got, slots_far, keep, got, slots, more, sems):
    pairs = [(far, got.at[96 * k : 96 * (k + 1), :]) for k, far in enumerate((got0, got1, got2, got3))]
    loads = copies([*pairs, (keep_far, keep)], sems)
    row = bias[...] + bias_got[...]
    row = jnp.concatenate([row[0:1, k : k + T] for k in range(0, F, T)] + [jnp.zeros((10, T), f32)], axis=0)
    for w in range(NW):
        more[w] = row.astype(bf16)
    for load in loads:
        load.wait()
    stores = copies([(more, slots_far.at[:, FIRST_ROWS + LAST_ROWS :, :])], sems.at[NW:])
    for w in range(NW):
        at = slice(w * G, (w + 1) * G)
        slots[w] = blocks_of(keep[at, :].astype(f32) + got[at, :].astype(f32))
        stores += copies([(slots.at[w], slots_far.at[w, 0:FIRST_ROWS, :])], sems.at[w:])
    for store in stores:
        store.wait()


def last_add_kernel(
    keep_far, slots_in, got_far, sums, slots_far, b_q, b_k, b_v, g_two, s_two, b_down, g_one, s_one, b_out,
    keep, got, slots, sems,
):
    for load in copies([(keep_far, keep), (got_far, got)], sems):
        load.wait()
    stores = []
    for w in range(NW):
        at = slice(w * G, (w + 1) * G)
        slots[w] = blocks_of(keep[at, :].astype(f32) + got[at, :].astype(f32))
        stores += copies([(slots.at[w], slots_far.at[w, FIRST_ROWS : FIRST_ROWS + LAST_ROWS, :])], sems.at[w:])
    other = got[D // 2 :, :].astype(f32)
    hi, mid, lo = split3(sums[...])
    total = (hi[0:7, :] + other[0:7, :]) + (mid[0:7, :] + other[7:14, :])
    bias = total[6:7, :] + (lo[6:7, :] + other[14:15, :])
    for k, ref in enumerate((b_q, b_k, b_v)):
        ref[...] = bias[:, k * E : (k + 1) * E].reshape(E)
    for k, ref in enumerate((g_two, s_two, b_down, g_one, s_one, b_out)):
        ref[...] = total[k : k + 1, :].reshape(D)
    for store in stores:
        store.wait()


def last_sum_kernel(got, g_q, g_k, g_v, out, up, down, b_up):
    total = got[0].astype(f32)
    for w in range(1, NW):
        total = total + got[w].astype(f32)
    end = FIRST_ROWS + LAST_ROWS
    b_up[...] = jnp.concatenate([total[end + k : end + k + 1, :] for k in range(F // T)], axis=1).reshape(F)
    total = jnp.concatenate([total[k : k + G, :] for k in range(0, end, G)], axis=1)
    up[...] = total[:, 0:F]
    down[...] = total[:, F : 2 * F]
    for k, ref in enumerate((g_q, g_k, g_v, out)):
        ref[...] = total[:, 2 * F + k * E : 2 * F + (k + 1) * E]


def input_chunk_kernel(part_far, one_far, part1, part2, part3, low, part0, grad_one, sems):
    for load in copies([(part_far, part0), (one_far, grad_one)], sems):
        load.wait()
    total = part0[...] + part1[...].astype(f32) + part2[...].astype(f32) + part3[...].astype(f32)
    low[...] = (grad_one[...] + total).astype(bf16)


def spread_kernel(g0, g1, g2, g3, out):
    n = lax.axis_index("narrow")
    for s, part in enumerate((g0, g1, g2, g3)):
        at = pl.ds(pl.multiple_of((n + NN - s) % NN * C, C), C)
        for r in range(R):
            out[r, at, :] = part[r * C : (r + 1) * C, :].astype(f32)


def shifted(x, s):
    return lax.ppermute(x, "narrow", [(i, (i + s) % NN) for i in range(NN)])


def gather_narrow(x):
    return (x, shifted(x, 1), shifted(x, 2), shifted(x, 3))


def scatter_narrow(parts):
    return (parts[0], shifted(parts[1], 1), shifted(parts[2], 2), shifted(parts[3], 3))


def other_core(x):
    return lax.ppermute(x, "dp", [(0, 1), (1, 0)])


def exchange(slots):
    return lax.all_to_all(slots, "wide", 0, 0, tiled=True)


def exchange_all(slots):
    return lax.all_to_all(slots, ("wide", "narrow"), 0, 0, tiled=True)


def body(
    hidden_in, segments, weight_query, bias_query, weight_key, bias_key, weight_value, bias_value,
    weight_out, bias_out, gain_one, shift_one, weight_up, bias_up, weight_down, bias_down,
    gain_two, shift_two, cotangent,
):
    frequency = np.repeat(np.power(10000.0, -np.arange(0, HD, 2) / HD), 2).astype(np.float32)
    frequency = jnp.asarray(np.broadcast_to(frequency[:, None], (HD, T)))
    shard = jnp.where(lax.axis_index("dp") == 0, weight_up, weight_down.T)
    shards = gather_narrow(shard)
    mine = lax.dynamic_slice_in_dim(weight_out, lax.axis_index("dp") * (E // 2), E // 2, 0)
    weights_got = gather_narrow(mine)[1:]
    weights_out = (weight_out, *weights_got, *(other_core(w) for w in weights_got))
    biases_up = gather_narrow(bias_up)
    query_t, key_t, value_t = weight_query.T, weight_key.T, weight_value.T

    slots, token = call(
        "project",
        project_kernel,
        [((NW, SLOT, T), bf16)],
        (hidden_in, segments, query_t, bias_query, key_t, bias_key, value_t, bias_value),
        scratch=[
            pltpu.VMEM((R, T, D), bf16),
            pltpu.VMEM((3, E, D), bf16),
            pltpu.VMEM((E,), f32),
            pltpu.VMEM((E,), f32),
            pltpu.VMEM((E,), f32),
            pltpu.VMEM((R, T), jnp.int32),
            pltpu.SemaphoreType.DMA((8,)),
        ],
        far_in=range(8),
        token=True,
    )
    (shards,) = call(
        "stack",
        stack_kernel,
        [((NN, D // NW, F), bf16)],
        shards,
        scratch=[pltpu.SemaphoreType.DMA((NN,))],
        any_in=range(NN),
        far=(0,),
        after=(token,),
    )
    every = lax.all_gather(shards, ("dp", "wide")).reshape(2, NW, NN, D // NW, F)
    got = exchange(slots)
    out_slots, *saved = call(
        "attend",
        attend_kernel,
        [
            ((NW * NN, C // 2, 2 * HD), bf16),
            ((AUG, L), bf16),
            ((AUG, L), bf16),
            ((L, HD), bf16),
            ((L, AUG), bf16),
            ((L, AUG), bf16),
            ((HD, L), f32),
            ((HD, L), f32),
            ((HD, L), f32),
        ],
        (got, frequency),
        scratch=[
            pltpu.VMEM((NW * NN, C // 2, 2 * HD), bf16),
            pltpu.VMEM((AUG, L), bf16),
            pltpu.VMEM((AUG, L), bf16),
            pltpu.VMEM((AUG, L), bf16),
            pltpu.VMEM((L, HD), bf16),
            pltpu.VMEM((L, AUG), bf16),
            pltpu.VMEM((L, AUG), bf16),
            pltpu.VMEM((HD, L), f32),
            pltpu.VMEM((HD, L), f32),
            pltpu.VMEM((HD, L), f32),
            pltpu.VMEM((L, 256), f32),
            pltpu.VMEM((L, 256), f32),
            pltpu.VMEM((16, L), f32),
            pltpu.SemaphoreType.DMA((9,)),
        ],
        mib=24,
        after=weights_got,
        far=range(9),
    )
    attn = exchange_all(out_slots)
    chunk_f32, chunk_low = ((CH, D), f32), ((CH, D), bf16)
    parts4 = [chunk_f32, chunk_low, chunk_low, chunk_low]
    slot_shape = (NW * NN, C // 2, 2 * HD)
    w_out, state, *firsts, token = call(
        "first",
        first_kernel,
        [((D, D), bf16), ((CH, D + T), f32)] + [((FIRST, D), bf16)] * NN,
        (*weights_out, hidden_in, attn, bias_out, gain_one, shift_one),
        scratch=[
            pltpu.VMEM((D, D), bf16),
            pltpu.VMEM((CH, D + T), f32),
            pltpu.VMEM((CH, D), bf16),
            pltpu.VMEM((NN, FIRST, D), bf16),
            pltpu.SemaphoreType.DMA((7,)),
        ],
        far_in=range(7),
        far=range(6),
        token=True,
        after=biases_up[1:],
    )
    firsts = (firsts[0], *(shifted(firsts[s], NN - s) for s in range(1, NN)))
    every = later(every, token)
    slots, grad_one, pack, layer, totals = call(
        "middle",
        middle_kernel,
        [(slot_shape, bf16), chunk_f32, ((LAST, D), bf16), chunk_low, ((16, D), bf16)],
        (
            every, state, cotangent, w_out, gain_one, shift_one, biases_up[0], bias_down, gain_two, shift_two,
            *biases_up[1:],
        ),
        scratch=[
            pltpu.VMEM((CH, D + T), f32),
            pltpu.VMEM((R, T, D), bf16),
            pltpu.VMEM((D, D), bf16),
            *[pltpu.VMEM((D,), f32)] * 6,
            pltpu.VMEM((2, NN, NW, D // NW, F), bf16),
            pltpu.VMEM((NN, CH, F), f32),
            pltpu.VMEM((CH, D), f32),
            pltpu.VMEM(slot_shape, bf16),
            pltpu.VMEM((LAST, D), bf16),
            pltpu.VMEM((CH, D), bf16),
            pltpu.VMEM((16, D), bf16),
            pltpu.SemaphoreType.DMA((17,)),
        ],
        mib=32,
        far_in=range(10),
        far=range(5),
    )
    got = exchange_all(later(slots, *firsts[1:]))
    firsts = (firsts[0], firsts[3], firsts[2], firsts[1])
    hidden, slope = call(
        "hidden",
        hidden_kernel,
        [((TOK, F), bf16), ((TOK, F), f32)],
        (*firsts, every, bias_up),
        scratch=[
            pltpu.VMEM((NN, FIRST, D), bf16),
            pltpu.VMEM((NW, D // NW, F), bf16),
            pltpu.VMEM((TOK, F), bf16),
            pltpu.VMEM((TOK, F), f32),
            pltpu.SemaphoreType.DMA((5,)),
        ],
        far_in=range(5),
        far=(0, 1),
    )
    totals = gather_narrow(totals)
    packs = gather_narrow(later(pack, hidden, got, *totals[1:]))
    slots, token = call(
        "attend_back",
        attend_back_kernel,
        [((NW, SLOT + VECTORS, T), bf16)],
        (got, *saved, *totals),
        scratch=[
            pltpu.VMEM((NW, SLOT + VECTORS, T), bf16),
            pltpu.VMEM((NN, 16, D), bf16),
            pltpu.VMEM((NN, 16, D), f32),
            pltpu.VMEM((NW * NN, C // 2, 2 * HD), bf16),
            pltpu.VMEM((HD, L), f32),
            pltpu.VMEM((AUG, L), bf16),
            pltpu.VMEM((AUG, L), bf16),
            pltpu.VMEM((HD, L), f32),
            pltpu.VMEM((HD, L), f32),
            pltpu.VMEM((AUG, L), bf16),
            pltpu.VMEM((L, HD), bf16),
            pltpu.VMEM((L, HD), bf16),
            pltpu.VMEM((L, AUG), bf16),
            pltpu.VMEM((L, AUG), bf16),
            pltpu.VMEM((HD, L), f32),
            pltpu.SemaphoreType.DMA((NW + 2,)),
        ],
        far_in=range(13),
        far=(0,),
        token=True,
    )
    *sends, up_keep, out_whole, bias = call(
        "weights",
        weights_kernel,
        [((96, 2 * F), bf16)] * 4 + [((D // 2, 2 * F), bf16), ((D, E), bf16), ((8, D), f32)],
        (*firsts, *packs, every, hidden, slope),
        scratch=[
            pltpu.VMEM((NN, FIRST, D), bf16),
            pltpu.VMEM((NN, LAST, D), bf16),
            pltpu.VMEM((NW, D // NW, F), bf16),
            pltpu.VMEM((TOK, F), bf16),
            pltpu.VMEM((TOK, F), f32),
            pltpu.VMEM((D, 2 * F), bf16),
            pltpu.SemaphoreType.DMA((11,)),
        ],
        mib=32,
        far_in=range(11),
        far=range(5),
        cost=COST,
        after=(token,),
    )
    got = exchange(slots)
    last_shape = (NW, FIRST_ROWS + LAST_ROWS + BIAS_ROWS, T)
    slots, added = call(
        "first_add",
        first_add_kernel,
        [(last_shape, bf16)],
        (up_keep, *(other_core(send) for send in sends), bias, other_core(bias)),
        scratch=[
            pltpu.VMEM((D // 2, 2 * F), bf16),
            pltpu.VMEM((D // 2, 2 * F), bf16),
            pltpu.VMEM((NW, FIRST_ROWS, T), bf16),
            pltpu.VMEM((NW, BIAS_ROWS, T), bf16),
            pltpu.SemaphoreType.DMA((NW + 1,)),
        ],
        far_in=(0,),
        any_in=range(1, 5),
        far=(0,),
        token=True,
    )
    grad, send, keep, sums = call(
        "input_weights",
        input_weights_kernel,
        [((TOK, 3 * E), bf16), ((D // 2 + 16, D), bf16), ((D // 2, D), bf16), ((8, D), f32)],
        (hidden_in, got, out_whole),
        scratch=[
            pltpu.VMEM((D, D), bf16),
            pltpu.VMEM((16, D), bf16),
            pltpu.VMEM((R, T, D), bf16),
            pltpu.SemaphoreType.DMA((3,)),
        ],
        far_in=(0,),
        far=(1, 2),
        after=(added,),
    )
    *parts, done = call(
        "input_back",
        input_back_kernel,
        parts4,
        (query_t, key_t, value_t, grad),
        scratch=[
            pltpu.VMEM((CH, D), f32),
            pltpu.VMEM((CH, D), bf16),
            pltpu.VMEM((CH, D), bf16),
            pltpu.VMEM((CH, D), bf16),
            pltpu.VMEM((TOK, D), f32),
            pltpu.VMEM((3, E, D), bf16),
            pltpu.SemaphoreType.DMA((4,)),
        ],
        far_in=range(3),
        far=range(4),
        token=True,
    )
    slots, b_query, b_key, b_value, g_two, s_two, b_down, g_one, s_one, b_out = call(
        "last_add",
        last_add_kernel,
        [(last_shape, bf16)] + [((E,), f32)] * 3 + [((D,), f32)] * 6,
        (keep, slots, other_core(send), sums),
        scratch=[
            pltpu.VMEM((D // 2, D), bf16),
            pltpu.VMEM((D // 2 + 16, D), bf16),
            pltpu.VMEM((NW, LAST_ROWS, T), bf16),
            pltpu.SemaphoreType.DMA((NW,)),
        ],
        far_in=range(2),
        any_in=(2,),
        far=(0,),
        aliases={1: 0},
        after=(done,),
    )
    parts = scatter_narrow([parts[0], *(later(part, slots) for part in parts[1:])])
    (input_low,) = call("input_chunk", input_chunk_kernel, [chunk_low], (parts[0], grad_one, *parts[1:]),
        scratch=[pltpu.VMEM((CH, D), f32), pltpu.VMEM((CH, D), f32), pltpu.SemaphoreType.DMA((2,))],
        far_in=(0, 1),
    )
    layers = gather_narrow(later(layer, slots))
    whole_out = ((R, T, D), f32)
    (layer_out,) = call("layer_out", spread_kernel, [whole_out], layers)
    (grad_input,) = call("grad_input", spread_kernel, [whole_out], gather_narrow(input_low))
    g_query, g_key, g_value, g_out, grad_up, grad_down, b_up = call(
        "last_sum", last_sum_kernel, [((G, E), f32)] * 4 + [((G, F), f32)] * 2 + [((F,), f32)], (exchange(slots),)
    )
    return (
        layer_out, grad_input, g_query, b_query, g_key, b_key, g_value, b_value, g_out.T, b_out,
        g_one, s_one, grad_up, b_up, grad_down.T, b_down, g_two, s_two,
    )


def solution(mesh):
    tokens, whole = P("dp", "wide", None), P()
    column, vector = P(None, "narrow"), P("narrow")
    rows_split, columns_split = P(("dp", "wide"), "narrow"), P("narrow", ("dp", "wide"))
    in_specs = (
        tokens, P("dp", "wide"), column, vector, column, vector, column, vector, P("narrow", None), whole,
        whole, whole, P("wide", "narrow"), vector, P("narrow", "wide"), whole, whole, whole, tokens,
    )
    out_specs = (
        tokens, tokens, rows_split, vector, rows_split, vector, rows_split, vector, columns_split, whole,
        whole, whole, rows_split, vector, columns_split, whole, whole, whole,
    )
    return jax.shard_map(body, mesh=mesh, in_specs=in_specs, out_specs=out_specs, check_vma=False)
```

```python
import functools
import math

import jax
import jax.numpy as jnp
import numpy as np
from jax import lax
from jax.experimental import pallas as pl
from jax.experimental.pallas import tpu as pltpu
from jax.sharding import PartitionSpec as P

D = 768
HD = 64
R = 3
T = 128
NH = 3
E = NH * HD
F = 768
NW = 16
NN = 4
TOK = R * T
L = NW * T
C = T // NN
CH = R * C
PAIRS = R * NH
G = D // (2 * NW)
FIRST_ROWS, LAST_ROWS, BIAS_ROWS = 12 * G, 6 * G, 16
SLOT = 3 * HD + 16
VECTORS = 8 * D // T
AUG = HD + 16
EPSILON = 1e-12
BIG = 1e30
LOG2E = math.log2(math.e)
LN2 = math.log(2.0)
COST = 10**11
f32, bf16 = jnp.float32, jnp.bfloat16


def dot(a, b, dims):
    return lax.dot_general(a, b, (dims, ((), ())), preferred_element_type=f32)


NORMAL, BOTH_LAST, BOTH_FIRST = ((1,), (0,)), ((1,), (1,)), ((0,), (0,))


def in_far_memory(arrays):
    return [pltpu.with_memory_space_constraint(a, pltpu.HBM) if a.size > 1024 else a for a in arrays]


def call(
    name, kernel, outs, args, scratch=(), cost=1024, mib=16, after=(), far_in=(), any_in=(), near=(), far=(), aliases={},
    token=False,
):
    if token:
        outs = [*outs, ((8, 128), f32)]

    def run(*refs):
        end = len(args) + len(after)
        if token:
            at = end + len(outs) - 1
            refs[at][...] = jnp.zeros((8, 128), f32)
            refs = refs[:at] + refs[at + 1 :]
        kernel(*refs[: len(args)], *refs[end:])

    def shape(k, s, t):
        return pltpu.VMEM(s, t) if k in near else pltpu.HBM(s, t) if k in far else jax.ShapeDtypeStruct(s, t)

    args = [pltpu.with_memory_space_constraint(a, pltpu.HBM) if k in far_in else a for k, a in enumerate(args)]
    after = in_far_memory(after)
    return pl.pallas_call(
        run,
        out_shape=[shape(k, s, t) for k, (s, t) in enumerate(outs)],
        in_specs=[
            pl.BlockSpec(memory_space=pltpu.HBM if k in far_in else pl.ANY if k in any_in else pltpu.VMEM)
            for k in range(len(args))
        ]
        + [pl.BlockSpec(memory_space=pl.ANY) for _ in after],
        out_specs=[pl.BlockSpec(memory_space=pltpu.HBM if k in far else pltpu.VMEM) for k in range(len(outs))],
        scratch_shapes=list(scratch),
        input_output_aliases=aliases,
        compiler_params=pltpu.CompilerParams(vmem_limit_bytes=mib * 1024 * 1024),
        cost_estimate=pl.CostEstimate(flops=cost, bytes_accessed=1024, transcendentals=0),
        name=name,
    )(*args, *after)


def later(x, *after, anywhere=()):
    after = [*in_far_memory(after), *anywhere]
    return pl.pallas_call(
        lambda *refs: None,
        out_shape=jax.ShapeDtypeStruct(x.shape, x.dtype),
        in_specs=[pl.BlockSpec(memory_space=pltpu.HBM)] + [pl.BlockSpec(memory_space=pl.ANY) for _ in after],
        out_specs=pl.BlockSpec(memory_space=pltpu.HBM),
        input_output_aliases={0: 0},
        cost_estimate=pl.CostEstimate(flops=1024, bytes_accessed=1024, transcendentals=0),
        name="later",
    )(x, *after)


def copies(pairs, sems):
    made = [pltpu.make_async_copy(a, b, sems.at[k]) for k, (a, b) in enumerate(pairs)]
    for copy in made:
        copy.start()
    return made


def row_of(ref):
    return ref[...].reshape(1, ref.shape[-1])


def split3(v):
    hi = v.astype(bf16).astype(f32)
    rest = v - hi
    mid = rest.astype(bf16).astype(f32)
    return hi, mid, (rest - mid).astype(bf16).astype(f32)


def sine_cosine(angle):
    turns = jnp.floor(angle * (2.0 / math.pi) + 0.5)
    r = ((angle - turns * 1.5703125) - turns * 4.837512969970703125e-4) - turns * 7.54978995489188e-8
    z = r * r
    sine = r + r * z * (-1.6666654611e-1 + z * (8.3321608736e-3 + z * -1.9515295891e-4))
    cosine = 1.0 - 0.5 * z + z * z * (4.166664568298827e-2 + z * (-1.388731625493765e-3 + z * 2.443315711809948e-5))
    quarter = turns - 4.0 * jnp.floor(turns * 0.25)
    odd = (quarter == 1.0) | (quarter == 3.0)
    sin_abs = jnp.where(odd, cosine, sine)
    cos_abs = jnp.where(odd, sine, cosine)
    return jnp.where(quarter >= 2.0, -sin_abs, sin_abs), jnp.where((quarter == 1.0) | (quarter == 2.0), -cos_abs, cos_abs)


def swap_pairs(t):
    rows = lax.broadcasted_iota(jnp.int32, t.shape, 0)
    return jnp.where(rows % 2 == 0, pltpu.roll(t, HD - 1, 0), pltpu.roll(t, 1, 0))


def project_kernel(x_far, seg, wq, bq, wk, bk, wv, bv, slots, x, near, bias0, bias1, bias2, ids, sems):
    pairs = [(x_far, x), (wq, near.at[0]), (bq, bias0), (wk, near.at[1]), (bk, bias1)]
    pairs += [(wv, near.at[2]), (bv, bias2), (seg, ids)]
    loads = copies(pairs, sems)
    for load in loads:
        load.wait()
    flat = x[...].reshape(TOK, D)
    for j, b in enumerate((bias0, bias1, bias2)):
        w = near.at[j]
        bias = jnp.broadcast_to(row_of(b), (T, E)).T
        yt = (dot(w[...], flat, BOTH_LAST) + jnp.concatenate([bias] * R, axis=1)).astype(bf16)
        for r in range(R):
            for h in range(NH):
                slots[r * NH + h, j * HD : (j + 1) * HD, :] = yt[h * HD : (h + 1) * HD, r * T : (r + 1) * T]
    for r in range(R):
        block = jnp.broadcast_to(ids[r : r + 1, :].astype(f32), (16, T)).astype(bf16)
        for h in range(NH):
            slots[r * NH + h, 3 * HD :, :] = block


def stack_kernel(a, b, c, d, out, sems):
    for copy in copies([(part, out.at[s]) for s, part in enumerate((a, b, c, d))], sems):
        copy.wait()


def attend_kernel(
    got, freq, out_far, q_far, k_far, qn_far, kn_far, vn_far, o_far, cos_far, sin_far,
    out, q_t, k_t, v_t, q_nat, k_nat, v_nat, o_t, cos_t, sin_t, s_even, s_odd, lse_t, sems,
):
    @pl.when(lax.axis_index("wide") < PAIRS)
    def _():
        ids = [got[w, 3 * HD :, :].astype(f32)[0:1, :] for w in range(NW)]
        starts = []
        for d in range(1, 5):
            below = jnp.zeros((1, T), f32)
            for w in range(NW):
                below = below + jnp.where(ids[w] < d, 1.0, 0.0)
            starts.append(jnp.sum(below, axis=1, keepdims=True))
        odd = lax.broadcasted_iota(jnp.int32, (HD, T), 0) % 2 == 1
        ext = lax.broadcasted_iota(jnp.int32, (16, T), 0)
        lane = lax.broadcasted_iota(jnp.int32, (1, T), 1).astype(f32)
        for w in range(NW):
            at = slice(w * T, (w + 1) * T)
            start = jnp.zeros((1, T), f32)
            for d in range(1, 5):
                start = jnp.where(ids[w] == d, starts[d - 1], start)
            sine, cosine = sine_cosine(freq[...] * (lane + (w * T) - start))
            sine = jnp.where(odd, sine, -sine)
            cos_t[:, at] = cosine
            sin_t[:, at] = sine
            query = got[w, 0:HD, :].astype(f32)
            key = got[w, HD : 2 * HD, :].astype(f32)
            query = (query * cosine + swap_pairs(query) * sine) * (HD**-0.5 * LOG2E)
            key = key * cosine + swap_pairs(key) * sine
            same = ids[w] == ext.astype(f32)
            doc = ext < 5
            key_ext = jnp.where(doc, jnp.where(same, 1.0, 0.0), jnp.where(ext < 8, 1.0, 0.0))
            q_t[0:HD, at] = query.astype(bf16)
            q_t[HD:AUG, at] = jnp.where(doc, jnp.where(same, 0.0, -BIG), 0.0).astype(bf16)
            k_t[0:HD, at] = key.astype(bf16)
            k_t[HD:AUG, at] = key_ext.astype(bf16)
            k_nat[at, :] = jnp.concatenate([key, key_ext], axis=0).T.astype(bf16)
            value = got[w, 2 * HD : 3 * HD, :].astype(f32)
            value = jnp.concatenate([value, jnp.where(ext < 3, 1.0, 0.0)], axis=0)
            v_t[:, at] = value.astype(bf16)
            v_nat[at, :] = value.T.astype(bf16)
            q_nat[at, :] = query.T.astype(bf16)

        pairs = [(k_t, k_far), (cos_t, cos_far), (sin_t, sin_far), (q_nat, qn_far), (k_nat, kn_far), (v_nat, vn_far)]
        stores = copies(pairs, sems)

        def scores(i, s_ref):
            at = pl.ds(pl.multiple_of(i * 256, 256), 256)
            s_ref[...] = dot(k_nat[...], q_t[:, at], NORMAL)

        def tile(i, s_ref):
            at = pl.ds(pl.multiple_of(i * 256, 256), 256)
            s = s_ref[...]
            top = jnp.max(s, axis=0, keepdims=True)
            p = jnp.exp2(s - top).astype(bf16)
            o = dot(v_t[...], p, NORMAL)
            total = o[HD : HD + 1, :]
            o = o[0:HD, :] / total
            o_t[:, at] = o
            natural = o.T
            for j in range(2 * NN):
                block = natural[j * C : (j + 1) * C, :]
                out[2 * NN * i + j] = jnp.concatenate([block[0 : C // 2], block[C // 2 :]], axis=1).astype(bf16)
            hi, mid, lo = split3(-(top + jnp.log(total) * LOG2E))
            rows = lax.broadcasted_iota(jnp.int32, (16, 256), 0)
            more = jnp.where(rows == 5, hi, jnp.where(rows == 6, mid, jnp.where(rows == 7, lo, 0.0)))
            lse_t[:, at] = more

        def two_tiles(k, carry):
            scores(2 * k + 1, s_odd)
            tile(2 * k, s_even)
            scores(jnp.minimum(2 * k + 2, L // 256 - 1), s_even)
            tile(2 * k + 1, s_odd)
            return carry

        scores(0, s_even)
        lax.fori_loop(0, L // 512, two_tiles, 0)
        q_t[HD:AUG, :] = (q_t[HD:AUG, :].astype(f32) + lse_t[...]).astype(bf16)
        last = [(out, out_far, 6), (q_t, q_far, 7), (o_t, o_far, 8)]
        last = [pltpu.make_async_copy(a, b, sems.at[k]) for a, b, k in last]
        for store in last:
            store.start()
        for store in stores + last:
            store.wait()


def attend_back_kernel(
    got_far, q_far, k_far, qn_far, kn_far, vn_far, o_far, cos_far, sin_far, v0, v1, v2, v3, out_far,
    out, near, vectors, got, o_t, q_t, k_t, cos_t, sin_t, do_t, do_nat, q_nat, k_nat, v_nat, dq_t, sems,
):
    n, attends = lax.axis_index("narrow"), lax.axis_index("wide") < PAIRS
    pairs = [(got_far, got), (o_far, o_t), (qn_far, q_nat), (kn_far, k_nat), (vn_far, v_nat), (q_far, q_t)]
    pairs += [(k_far, k_t), (cos_far, cos_t), (sin_far, sin_t)]
    loads = [pltpu.make_async_copy(a, b, sems.at[k]) for k, (a, b) in enumerate(pairs)]

    @pl.when(attends)
    def _():
        for load in loads:
            load.start()

    for s, load in enumerate(copies([(v, near.at[s]) for s, v in enumerate((v0, v1, v2, v3))], sems.at[len(loads) :])):
        load.wait()
        vectors[(n + NN - s) % NN] = near[s].astype(f32)
    total = (vectors[0] + vectors[1] + vectors[2] + vectors[3])[0:8, :]
    block = jnp.concatenate([total[:, k : k + T] for k in range(0, D, T)], axis=0).astype(bf16)
    for w in range(NW):
        out[w, SLOT:, :] = block
    store = copies([(out.at[:, SLOT:, :], out_far.at[:, SLOT:, :])], sems.at[NW:])[0]

    @pl.when(attends)
    def _():
        ext = lax.broadcasted_iota(jnp.int32, (16, T), 0)
        for load in loads[:2]:
            load.wait()
        for w in range(NW):
            at = slice(w * T, (w + 1) * T)
            pieces = []
            for n in range(NN):
                piece = got[w * NN + n].astype(f32)
                pieces += [piece[:, 0:HD], piece[:, HD:]]
            natural = jnp.concatenate(pieces, axis=0)
            do_nat[at, :] = natural.astype(bf16)
            grad = natural.T
            delta = -jnp.sum(grad * o_t[:, at], axis=0, keepdims=True)
            hi, mid, lo = split3(delta)
            do_t[0:HD, at] = grad.astype(bf16)
            do_t[HD:AUG, at] = jnp.where(
                ext == 0, hi, jnp.where(ext == 1, mid, jnp.where(ext == 2, lo, 0.0))
            ).astype(bf16)
        dq_t[...] = jnp.zeros((HD, L), f32)
        for load in loads[2:]:
            load.wait()

        def folded(t):
            total = t[:, 0:T]
            for k in range(1, t.shape[1] // T):
                total = total + t[:, k * T : (k + 1) * T]
            return total

        def tile(j, carry):
            sum_key, sum_value = carry
            at = pl.ds(pl.multiple_of(j * 256, 256), 256)
            p = jnp.exp2(dot(k_nat[at, :], q_t[...], NORMAL))
            dp = dot(v_nat[at, :], do_t[...], NORMAL)
            ds = (p * dp).astype(bf16)
            dv = dot(p.astype(bf16), do_nat[...], NORMAL).T.astype(bf16)
            dk = dot(ds, q_nat[...], NORMAL).T * LN2
            dk = (dk * cos_t[:, at] - swap_pairs(dk) * sin_t[:, at]).astype(bf16)
            dq_t[...] += dot(k_t[0:HD, at], ds, NORMAL)
            for k in range(2):
                out[2 * j + k, HD : 2 * HD, :] = dk[:, k * T : (k + 1) * T]
                out[2 * j + k, 2 * HD : 3 * HD, :] = dv[:, k * T : (k + 1) * T]
            return sum_key + folded(dk.astype(f32)), sum_value + folded(dv.astype(f32))

        zero = jnp.zeros((HD, T), f32)
        sum_key, sum_value = lax.fori_loop(0, L // 256, tile, (zero, zero), unroll=2)
        sum_query = zero
        stores = []
        for w in range(NW):
            at = slice(w * T, (w + 1) * T)
            dq = dq_t[:, at] * (HD**-0.5)
            dq = (dq * cos_t[:, at] - swap_pairs(dq) * sin_t[:, at]).astype(bf16)
            out[w, 0:HD, :] = dq
            stores += copies([(out.at[w, 0 : 3 * HD, :], out_far.at[w, 0 : 3 * HD, :])], sems.at[w:])
            sum_query = sum_query + dq.astype(f32)
        rows = [jnp.sum(t.T, axis=0, keepdims=True) for t in (sum_query, sum_key, sum_value)]
        first = jnp.concatenate([rows[0], rows[1]], axis=1)
        second = jnp.concatenate([rows[2], rows[2]], axis=1)
        first_hi, second_hi = first.astype(bf16).astype(f32), second.astype(bf16).astype(f32)
        block = jnp.where(
            ext == 0,
            first_hi,
            jnp.where(ext == 1, second_hi, jnp.where(ext == 2, first - first_hi, second - second_hi)),
        )
        block = jnp.where(ext < 4, block, 0.0).astype(bf16)
        for w in range(NW):
            out[w, 3 * HD : SLOT, :] = block
        stores += copies([(out.at[:, 3 * HD : SLOT, :], out_far.at[:, 3 * HD : SLOT, :])], sems.at[NW + 1 :])
        for store in stores:
            store.wait()

    store.wait()


def chunk_rows(c, r):
    return pl.ds(pl.multiple_of(r * T + c * C, C), C)


def row_mean(t):
    return jnp.mean(t, axis=-1, keepdims=True)


def column_sum(t):
    return jnp.sum(t, axis=0, keepdims=True)


def gelu_and_slope(pre):
    half = 0.5 * (1.0 + lax.erf(pre * (2.0**-0.5)))
    return (pre * half).astype(bf16), half + pre * jnp.exp(-0.5 * pre * pre) * (1.0 / math.sqrt(2.0 * math.pi))


ATTN, NORMED, FIRST = 0, 32, 128
FFN, OUT, LAST = 0, 96, 192


def first_kernel(
    w0, m1, m2, m3, u1, u2, u3, x, attn, b_out, g_one, s_one, w_out_far, state_far, pack0, pack1, pack2, pack3,
    w_out, state, heads, packs, sems,
):
    n, c = lax.axis_index("narrow"), lax.axis_index("dp")
    pairs = [(w0, w_out.at[0:E, :])]
    for s, (mine, other) in enumerate(((m1, u1), (m2, u2), (m3, u3)), 1):
        for source, core in ((mine, c), (other, 1 - c)):
            pairs.append((source, w_out.at[pl.ds(pl.multiple_of(s * E + core * (E // 2), E // 2), E // 2), :]))
    loads = copies(pairs, sems)
    for s in range(NN):
        for r in range(R):
            for h in range(NH):
                block = attn[(r * NH + h) * NN + (n + NN - s) % NN]
                at = s * E + h * HD
                heads[r * C : r * C + C // 2, at : at + HD] = block[:, 0:HD]
                heads[r * C + C // 2 : (r + 1) * C, at : at + HD] = block[:, HD:]
    mine = pl.ds(pl.multiple_of(n * C, C), C)
    tokens = jnp.concatenate([x[r, mine, :] for r in range(R)], axis=0).astype(f32)
    for load in loads:
        load.wait()
    stores = copies([(w_out, w_out_far)], sems.at[5:])
    residual = tokens + (dot(heads[...], w_out[...], NORMAL) + row_of(b_out))
    center = residual - row_mean(residual)
    rstd = lax.rsqrt(row_mean(center * center) + EPSILON)
    unit = center * rstd
    state[:, 0:D] = unit
    state[:, D:] = jnp.broadcast_to(rstd, (CH, T))
    stores += copies([(state, state_far)], sems.at[4:])
    low = (unit * row_of(g_one) + row_of(s_one)).astype(bf16)
    for s, pack in enumerate((pack0, pack1, pack2, pack3)):
        packs[s, NORMED:FIRST, :] = low
        for r in range(R):
            packs[s, ATTN:NORMED, 256 * r : 256 * r + E] = heads[r * C : (r + 1) * C, s * E : (s + 1) * E]
        stores.append(pltpu.make_async_copy(packs.at[s], pack, sems.at[s]))
        stores[-1].start()
    for store in stores:
        store.wait()


def middle_kernel(
    every_far, state_far, cot_far, w_out_far, g_one_far, s_one_far, b0_far, b_down_far, g_two_far, s_two_far, b1, b2, b3,
    slots_far, one_far, pack_far, layer_far, sums_far,
    state, cot, w_out, g_one, s_one, b0, b_down, g_two, s_two,
    weights, slope, grad_one, slots, pack, layer, totals, sems,
):
    n = lax.axis_index("narrow")
    pairs = [(state_far, state), (cot_far, cot), (w_out_far, w_out), (g_one_far, g_one), (s_one_far, s_one)]
    pairs += [(b0_far, b0), (b_down_far, b_down), (g_two_far, g_two), (s_two_far, s_two)]
    first = copies(pairs, sems.at[8:])
    pairs = [(every_far.at[which, :, s], weights.at[which, s]) for s in range(NN) for which in range(2)]
    loads = copies(pairs, sems)
    for load in first:
        load.wait()
    mine = pl.ds(pl.multiple_of(n * C, C), C)
    ct = jnp.concatenate([cot[r, mine, :] for r in range(R)], axis=0).astype(f32)
    unit, rstd = state[:, 0:D], state[:, D : D + 1]
    normed = unit * row_of(g_one) + row_of(s_one)
    low = normed.astype(bf16)

    def weight(which, s):
        return weights[which, s].reshape(D, F)

    total = None
    for s, b in enumerate((b0, b1, b2, b3)):
        loads[2 * s].wait()
        hidden, slope[s] = gelu_and_slope(dot(low, weight(0, s), NORMAL) + row_of(b))
        loads[2 * s + 1].wait()
        term = dot(hidden, weight(1, s), BOTH_LAST)
        total = term if s == 0 else total + term
    residual = normed + (total + row_of(b_down))
    center = residual - row_mean(residual)
    rstd_two = lax.rsqrt(row_mean(center * center) + EPSILON)
    unit_two = center * rstd_two
    layer[...] = (unit_two * row_of(g_two) + row_of(s_two)).astype(bf16)
    scaled = ct * row_of(g_two)
    grad_two = rstd_two * (scaled - row_mean(scaled) - unit_two * row_mean(scaled * unit_two))
    low_two = grad_two.astype(bf16)
    pack[FFN:OUT, :] = low_two
    total = None
    for s in range(NN):
        pre = (slope[s] * dot(low_two, weight(1, s), NORMAL)).astype(bf16)
        term = dot(pre, weight(0, s), BOTH_LAST)
        total = term if s == 0 else total + term
    grad = grad_two + total
    scaled = grad * row_of(g_one)
    one = rstd * (scaled - row_mean(scaled) - unit * row_mean(scaled * unit))
    grad_one[...] = one
    low_one = one.astype(bf16)
    every = dot(low_one, w_out[...], BOTH_LAST)
    for s in range(NN):
        for r in range(R):
            for h in range(NH):
                block = every[r * C : (r + 1) * C, s * E + h * HD : s * E + (h + 1) * HD]
                slot = jnp.concatenate([block[0 : C // 2], block[C // 2 :]], axis=1).astype(bf16)
                slots[(r * NH + h) * NN + (n + NN - s) % NN] = slot
    stores = copies([(slots, slots_far), (grad_one, one_far), (layer, layer_far)], sems)
    pack[OUT:LAST, :] = low_one
    stores += copies([(pack, pack_far)], sems.at[3:])
    sums = [ct * unit_two, ct, low_two.astype(f32), grad * unit, grad, low_one.astype(f32)]
    totals[...] = jnp.concatenate([column_sum(t) for t in sums] + [jnp.zeros((10, D), f32)], axis=0).astype(bf16)
    stores += copies([(totals, sums_far)], sems.at[4:])
    for store in stores:
        store.wait()


def hidden_kernel(a0, a1, a2, a3, every_far, b_up, hidden_far, slope_far, firsts, weights, hidden, slope, sems):
    pairs = [(p, firsts.at[s]) for s, p in enumerate((a0, a1, a2, a3))] + [(every_far.at[0, :, 0], weights)]
    for load in copies(pairs, sems):
        load.wait()
    normed = firsts[:, NORMED:FIRST, :].reshape(TOK, D)
    act, slant = gelu_and_slope(dot(normed, weights[...].reshape(D, F), NORMAL) + row_of(b_up))
    hidden[...] = act
    slope[...] = slant
    for store in copies([(hidden, hidden_far), (slope, slope_far)], sems):
        store.wait()


def weights_kernel(
    a0, a1, a2, a3, p0, p1, p2, p3, every_far, hidden_far, slope_far,
    send0_far, send1_far, send2_far, send3_far, keep_far, out_whole, bias,
    firsts, packs, weights, hidden, slope, whole, sems,
):
    c = lax.axis_index("dp")
    pairs = [(every_far.at[1, :, 0], weights), (slope_far, slope)]
    pairs += [(p, packs.at[s]) for s, p in enumerate((p0, p1, p2, p3))]
    pairs += [(p, firsts.at[s]) for s, p in enumerate((a0, a1, a2, a3))] + [(hidden_far, hidden)]
    loads = copies(pairs, sems)
    for load in loads[:6]:
        load.wait()
    grad_ffn = packs[:, FFN:OUT, :].reshape(TOK, D)
    pre = (slope[...] * dot(grad_ffn, weights[...].reshape(D, F), NORMAL)).astype(bf16)
    for load in loads[6:]:
        load.wait()
    whole[:, 0:F] = dot(firsts[:, NORMED:FIRST, :].reshape(TOK, D), pre, BOTH_FIRST).astype(bf16)
    whole[:, F : 2 * F] = dot(grad_ffn, hidden[...], BOTH_FIRST).astype(bf16)
    half = D // 2
    pairs = [(whole.at[pl.ds(pl.multiple_of(c * half, half), half), :], keep_far)]
    for k, far in enumerate((send0_far, send1_far, send2_far, send3_far)):
        pairs.append((whole.at[pl.ds(pl.multiple_of((1 - c) * half + 96 * k, 96), 96), :], far))
    stores = copies(pairs, sems)
    heads = [firsts[s, ATTN:NORMED, 256 * r : 256 * r + E] for s in range(NN) for r in range(R)]
    heads = jnp.concatenate(heads, axis=0)
    out_whole[...] = dot(packs[:, OUT:LAST, :].reshape(TOK, D), heads, BOTH_FIRST).astype(bf16)
    bias[...] = jnp.broadcast_to(column_sum(pre.astype(f32)), (8, F))
    for store in stores:
        store.wait()


def blocks_of(block):
    return jnp.concatenate([block[:, k : k + T] for k in range(0, block.shape[1], T)], axis=0).astype(bf16)


def input_weights_kernel(x_far, got, out_whole, grad, send_far, keep, sums, whole, bias, x, sems):
    c = lax.axis_index("dp")
    load = copies([(x_far, x)], sems)[0]
    grads = []
    for j in range(3):
        grad_t = jnp.concatenate(
            [
                jnp.concatenate([got[r * NH + h, j * HD : (j + 1) * HD, :] for h in range(NH)], axis=0)
                for r in range(R)
            ],
            axis=1,
        )
        grads.append(grad_t.astype(f32).T.astype(bf16))
    grads = jnp.concatenate(grads, axis=1)
    grad[...] = grads
    heads = []
    for h in range(NH):
        block = got[h, 3 * HD : SLOT, :].astype(f32)
        for r in range(1, R):
            block = block + got[r * NH + h, 3 * HD : SLOT, :].astype(f32)
        heads.append(block)
    first = jnp.concatenate([b[0:1, 0:HD] + b[2:3, 0:HD] for b in heads], axis=1)
    second = jnp.concatenate([b[0:1, HD:] + b[2:3, HD:] for b in heads], axis=1)
    third = jnp.concatenate([b[1:2, 0:HD] + b[3:4, 0:HD] for b in heads], axis=1)
    row = jnp.concatenate([first, second, third], axis=1)
    total = got[0, SLOT:, :].astype(f32)
    for w in range(1, NW):
        total = total + got[w, SLOT:, :].astype(f32)
    total = jnp.concatenate([total[k : k + 8, :] for k in range(0, VECTORS, 8)], axis=1)
    row = jnp.concatenate([row, jnp.zeros((1, E), f32)], axis=1)
    sums[...] = jnp.concatenate([total[0:6, :], row, row], axis=0)
    hi, mid, lo = split3(sums[...])
    bias[...] = jnp.concatenate([hi[0:7, :], mid[0:7, :], lo[6:7, :], lo[6:7, :]], axis=0).astype(bf16)
    whole[:, 3 * E :] = out_whole[...]
    load.wait()
    whole[:, 0 : 3 * E] = dot(x[...].reshape(TOK, D), grads, BOTH_FIRST).astype(bf16)
    half = D // 2
    pairs = [(bias, send_far.at[half:, :])]
    pairs.append((whole.at[pl.ds(pl.multiple_of((1 - c) * half, half), half), :], send_far.at[0:half, :]))
    stores = copies(pairs, sems)
    keep[...] = whole[pl.ds(pl.multiple_of(c * half, half), half), :]
    for store in stores:
        store.wait()


def input_back_kernel(
    wq, wk, wv, grad, part0_far, part1_far, part2_far, part3_far, part0, part1, part2, part3, wide_part, near, sems
):
    n = lax.axis_index("narrow")
    for load in copies([(wq, near.at[0]), (wk, near.at[1]), (wv, near.at[2])], sems):
        load.wait()
    wide_part[...] = dot(grad[...], near[...].reshape(3 * E, D), NORMAL)
    for r in range(R):
        to = slice(r * C, (r + 1) * C)
        part0[to, :] = wide_part[chunk_rows(n, r), :]
        for s, part in ((1, part1), (2, part2), (3, part3)):
            part[to, :] = wide_part[chunk_rows((n + s) % NN, r), :].astype(bf16)
    pairs = [(part0, part0_far), (part1, part1_far), (part2, part2_far), (part3, part3_far)]
    for store in copies(pairs, sems):
        store.wait()


def first_add_kernel(keep_far, got0, got1, got2, got3, bias, bias_got, slots_far, keep, got, slots, more, sems):
    pairs = [(far, got.at[96 * k : 96 * (k + 1), :]) for k, far in enumerate((got0, got1, got2, got3))]
    loads = copies([*pairs, (keep_far, keep)], sems)
    row = bias[...] + bias_got[...]
    row = jnp.concatenate([row[0:1, k : k + T] for k in range(0, F, T)] + [jnp.zeros((10, T), f32)], axis=0)
    for w in range(NW):
        more[w] = row.astype(bf16)
    for load in loads:
        load.wait()
    stores = copies([(more, slots_far.at[:, FIRST_ROWS + LAST_ROWS :, :])], sems.at[NW:])
    for w in range(NW):
        at = slice(w * G, (w + 1) * G)
        slots[w] = blocks_of(keep[at, :].astype(f32) + got[at, :].astype(f32))
        stores += copies([(slots.at[w], slots_far.at[w, 0:FIRST_ROWS, :])], sems.at[w:])
    for store in stores:
        store.wait()


def last_add_kernel(
    keep, slots_in, got_far, sums, slots_far, b_q, b_k, b_v, g_two, s_two, b_down, g_one, s_one, b_out,
    got, slots, sems,
):
    for load in copies([(got_far, got)], sems):
        load.wait()
    stores = []
    for w in range(NW):
        at = slice(w * G, (w + 1) * G)
        slots[w] = blocks_of(keep[at, :].astype(f32) + got[at, :].astype(f32))
        stores += copies([(slots.at[w], slots_far.at[w, FIRST_ROWS : FIRST_ROWS + LAST_ROWS, :])], sems.at[w:])
    other = got[D // 2 :, :].astype(f32)
    hi, mid, lo = split3(sums[...])
    total = (hi[0:7, :] + other[0:7, :]) + (mid[0:7, :] + other[7:14, :])
    bias = total[6:7, :] + (lo[6:7, :] + other[14:15, :])
    for k, ref in enumerate((b_q, b_k, b_v)):
        ref[...] = bias[:, k * E : (k + 1) * E].reshape(E)
    for k, ref in enumerate((g_two, s_two, b_down, g_one, s_one, b_out)):
        ref[...] = total[k : k + 1, :].reshape(D)
    for store in stores:
        store.wait()


def last_sum_kernel(got, g_q, g_k, g_v, out, up, down, b_up):
    total = got[0].astype(f32)
    for w in range(1, NW):
        total = total + got[w].astype(f32)
    end = FIRST_ROWS + LAST_ROWS
    b_up[...] = jnp.concatenate([total[end + k : end + k + 1, :] for k in range(F // T)], axis=1).reshape(F)
    total = jnp.concatenate([total[k : k + G, :] for k in range(0, end, G)], axis=1)
    up[...] = total[:, 0:F]
    down[...] = total[:, F : 2 * F]
    for k, ref in enumerate((g_q, g_k, g_v, out)):
        ref[...] = total[:, 2 * F + k * E : 2 * F + (k + 1) * E]


def input_chunk_kernel(part_far, one_far, part1, part2, part3, low, part0, grad_one, sems):
    for load in copies([(part_far, part0), (one_far, grad_one)], sems):
        load.wait()
    total = part0[...] + part1[...].astype(f32) + part2[...].astype(f32) + part3[...].astype(f32)
    low[...] = (grad_one[...] + total).astype(bf16)


def spread_kernel(g0, g1, g2, g3, out):
    n = lax.axis_index("narrow")
    for s, part in enumerate((g0, g1, g2, g3)):
        at = pl.ds(pl.multiple_of((n + NN - s) % NN * C, C), C)
        for r in range(R):
            out[r, at, :] = part[r * C : (r + 1) * C, :].astype(f32)


def shifted(x, s):
    return lax.ppermute(x, "narrow", [(i, (i + s) % NN) for i in range(NN)])


def gather_narrow(x):
    return (x, shifted(x, 1), shifted(x, 2), shifted(x, 3))


def scatter_narrow(parts):
    return (parts[0], shifted(parts[1], 1), shifted(parts[2], 2), shifted(parts[3], 3))


def other_core(x):
    return lax.ppermute(x, "dp", [(0, 1), (1, 0)])


def exchange(slots):
    return lax.all_to_all(slots, "wide", 0, 0, tiled=True)


def exchange_all(slots):
    return lax.all_to_all(slots, ("wide", "narrow"), 0, 0, tiled=True)


def body(
    hidden_in, segments, weight_query, bias_query, weight_key, bias_key, weight_value, bias_value,
    weight_out, bias_out, gain_one, shift_one, weight_up, bias_up, weight_down, bias_down,
    gain_two, shift_two, cotangent,
):
    frequency = np.repeat(np.power(10000.0, -np.arange(0, HD, 2) / HD), 2).astype(np.float32)
    frequency = jnp.asarray(np.broadcast_to(frequency[:, None], (HD, T)))
    shard = jnp.where(lax.axis_index("dp") == 0, weight_up, weight_down.T)
    shards = gather_narrow(shard)
    mine = lax.dynamic_slice_in_dim(weight_out, lax.axis_index("dp") * (E // 2), E // 2, 0)
    weights_got = gather_narrow(mine)[1:]
    weights_out = (weight_out, *weights_got, *(other_core(w) for w in weights_got))
    biases_up = gather_narrow(bias_up)
    query_t, key_t, value_t = weight_query.T, weight_key.T, weight_value.T

    slots, token = call(
        "project",
        project_kernel,
        [((NW, SLOT, T), bf16)],
        (hidden_in, segments, query_t, bias_query, key_t, bias_key, value_t, bias_value),
        scratch=[
            pltpu.VMEM((R, T, D), bf16),
            pltpu.VMEM((3, E, D), bf16),
            pltpu.VMEM((E,), f32),
            pltpu.VMEM((E,), f32),
            pltpu.VMEM((E,), f32),
            pltpu.VMEM((R, T), jnp.int32),
            pltpu.SemaphoreType.DMA((8,)),
        ],
        far_in=range(8),
        token=True,
    )
    (shards,) = call(
        "stack",
        stack_kernel,
        [((NN, D // NW, F), bf16)],
        shards,
        scratch=[pltpu.SemaphoreType.DMA((NN,))],
        any_in=range(NN),
        far=(0,),
        after=(token,),
    )
    every = lax.all_gather(shards, ("dp", "wide")).reshape(2, NW, NN, D // NW, F)
    got = exchange(slots)
    out_slots, *saved = call(
        "attend",
        attend_kernel,
        [
            ((NW * NN, C // 2, 2 * HD), bf16),
            ((AUG, L), bf16),
            ((AUG, L), bf16),
            ((L, HD), bf16),
            ((L, AUG), bf16),
            ((L, AUG), bf16),
            ((HD, L), f32),
            ((HD, L), f32),
            ((HD, L), f32),
        ],
        (got, frequency),
        scratch=[
            pltpu.VMEM((NW * NN, C // 2, 2 * HD), bf16),
            pltpu.VMEM((AUG, L), bf16),
            pltpu.VMEM((AUG, L), bf16),
            pltpu.VMEM((AUG, L), bf16),
            pltpu.VMEM((L, HD), bf16),
            pltpu.VMEM((L, AUG), bf16),
            pltpu.VMEM((L, AUG), bf16),
            pltpu.VMEM((HD, L), f32),
            pltpu.VMEM((HD, L), f32),
            pltpu.VMEM((HD, L), f32),
            pltpu.VMEM((L, 256), f32),
            pltpu.VMEM((L, 256), f32),
            pltpu.VMEM((16, L), f32),
            pltpu.SemaphoreType.DMA((9,)),
        ],
        mib=24,
        after=weights_got,
        far=range(9),
    )
    attn = exchange_all(out_slots)
    chunk_f32, chunk_low = ((CH, D), f32), ((CH, D), bf16)
    parts4 = [chunk_f32, chunk_low, chunk_low, chunk_low]
    slot_shape = (NW * NN, C // 2, 2 * HD)
    w_out, state, *firsts, token = call(
        "first",
        first_kernel,
        [((D, D), bf16), ((CH, D + T), f32)] + [((FIRST, D), bf16)] * NN,
        (*weights_out, hidden_in, attn, bias_out, gain_one, shift_one),
        scratch=[
            pltpu.VMEM((D, D), bf16),
            pltpu.VMEM((CH, D + T), f32),
            pltpu.VMEM((CH, D), bf16),
            pltpu.VMEM((NN, FIRST, D), bf16),
            pltpu.SemaphoreType.DMA((7,)),
        ],
        far_in=range(7),
        far=range(6),
        token=True,
        after=biases_up[1:],
    )
    firsts = (firsts[0], *(shifted(firsts[s], NN - s) for s in range(1, NN)))
    every = later(every, token)
    slots, grad_one, pack, layer, totals = call(
        "middle",
        middle_kernel,
        [(slot_shape, bf16), chunk_f32, ((LAST, D), bf16), chunk_low, ((16, D), bf16)],
        (
            every, state, cotangent, w_out, gain_one, shift_one, biases_up[0], bias_down, gain_two, shift_two,
            *biases_up[1:],
        ),
        scratch=[
            pltpu.VMEM((CH, D + T), f32),
            pltpu.VMEM((R, T, D), bf16),
            pltpu.VMEM((D, D), bf16),
            *[pltpu.VMEM((D,), f32)] * 6,
            pltpu.VMEM((2, NN, NW, D // NW, F), bf16),
            pltpu.VMEM((NN, CH, F), f32),
            pltpu.VMEM((CH, D), f32),
            pltpu.VMEM(slot_shape, bf16),
            pltpu.VMEM((LAST, D), bf16),
            pltpu.VMEM((CH, D), bf16),
            pltpu.VMEM((16, D), bf16),
            pltpu.SemaphoreType.DMA((17,)),
        ],
        mib=32,
        far_in=range(10),
        far=range(5),
    )
    got = exchange_all(later(slots, *firsts[1:]))
    firsts = (firsts[0], firsts[3], firsts[2], firsts[1])
    hidden, slope = call(
        "hidden",
        hidden_kernel,
        [((TOK, F), bf16), ((TOK, F), f32)],
        (*firsts, every, bias_up),
        scratch=[
            pltpu.VMEM((NN, FIRST, D), bf16),
            pltpu.VMEM((NW, D // NW, F), bf16),
            pltpu.VMEM((TOK, F), bf16),
            pltpu.VMEM((TOK, F), f32),
            pltpu.SemaphoreType.DMA((5,)),
        ],
        far_in=range(5),
        far=(0, 1),
    )
    totals = gather_narrow(totals)
    packs = gather_narrow(later(pack, hidden, got, *totals[1:]))
    slots, token = call(
        "attend_back",
        attend_back_kernel,
        [((NW, SLOT + VECTORS, T), bf16)],
        (got, *saved, *totals),
        scratch=[
            pltpu.VMEM((NW, SLOT + VECTORS, T), bf16),
            pltpu.VMEM((NN, 16, D), bf16),
            pltpu.VMEM((NN, 16, D), f32),
            pltpu.VMEM((NW * NN, C // 2, 2 * HD), bf16),
            pltpu.VMEM((HD, L), f32),
            pltpu.VMEM((AUG, L), bf16),
            pltpu.VMEM((AUG, L), bf16),
            pltpu.VMEM((HD, L), f32),
            pltpu.VMEM((HD, L), f32),
            pltpu.VMEM((AUG, L), bf16),
            pltpu.VMEM((L, HD), bf16),
            pltpu.VMEM((L, HD), bf16),
            pltpu.VMEM((L, AUG), bf16),
            pltpu.VMEM((L, AUG), bf16),
            pltpu.VMEM((HD, L), f32),
            pltpu.SemaphoreType.DMA((NW + 2,)),
        ],
        far_in=range(13),
        far=(0,),
        token=True,
    )
    *sends, up_keep, out_whole, bias = call(
        "weights",
        weights_kernel,
        [((96, 2 * F), bf16)] * 4 + [((D // 2, 2 * F), bf16), ((D, E), bf16), ((8, D), f32)],
        (*firsts, *packs, every, hidden, slope),
        scratch=[
            pltpu.VMEM((NN, FIRST, D), bf16),
            pltpu.VMEM((NN, LAST, D), bf16),
            pltpu.VMEM((NW, D // NW, F), bf16),
            pltpu.VMEM((TOK, F), bf16),
            pltpu.VMEM((TOK, F), f32),
            pltpu.VMEM((D, 2 * F), bf16),
            pltpu.SemaphoreType.DMA((11,)),
        ],
        mib=32,
        far_in=range(11),
        far=range(5),
        cost=COST,
        after=(token,),
    )
    got = exchange(slots)
    last_shape = (NW, FIRST_ROWS + LAST_ROWS + BIAS_ROWS, T)
    slots, added = call(
        "first_add",
        first_add_kernel,
        [(last_shape, bf16)],
        (up_keep, *(other_core(send) for send in sends), bias, other_core(bias)),
        scratch=[
            pltpu.VMEM((D // 2, 2 * F), bf16),
            pltpu.VMEM((D // 2, 2 * F), bf16),
            pltpu.VMEM((NW, FIRST_ROWS, T), bf16),
            pltpu.VMEM((NW, BIAS_ROWS, T), bf16),
            pltpu.SemaphoreType.DMA((NW + 1,)),
        ],
        far_in=(0,),
        any_in=range(1, 5),
        far=(0,),
        token=True,
    )
    grad, send, keep, sums = call(
        "input_weights",
        input_weights_kernel,
        [((TOK, 3 * E), bf16), ((D // 2 + 16, D), bf16), ((D // 2, D), bf16), ((8, D), f32)],
        (hidden_in, got, out_whole),
        scratch=[
            pltpu.VMEM((D, D), bf16),
            pltpu.VMEM((16, D), bf16),
            pltpu.VMEM((R, T, D), bf16),
            pltpu.SemaphoreType.DMA((3,)),
        ],
        far_in=(0,),
        far=(1,),
        after=(added,),
    )
    *parts, done = call(
        "input_back",
        input_back_kernel,
        parts4,
        (query_t, key_t, value_t, grad),
        scratch=[
            pltpu.VMEM((CH, D), f32),
            pltpu.VMEM((CH, D), bf16),
            pltpu.VMEM((CH, D), bf16),
            pltpu.VMEM((CH, D), bf16),
            pltpu.VMEM((TOK, D), f32),
            pltpu.VMEM((3, E, D), bf16),
            pltpu.SemaphoreType.DMA((4,)),
        ],
        far_in=range(3),
        far=range(4),
        token=True,
    )
    slots, b_query, b_key, b_value, g_two, s_two, b_down, g_one, s_one, b_out = call(
        "last_add",
        last_add_kernel,
        [(last_shape, bf16)] + [((E,), f32)] * 3 + [((D,), f32)] * 6,
        (keep, slots, other_core(send), sums),
        scratch=[
            pltpu.VMEM((D // 2 + 16, D), bf16),
            pltpu.VMEM((NW, LAST_ROWS, T), bf16),
            pltpu.SemaphoreType.DMA((NW,)),
        ],
        far_in=(1,),
        any_in=(2,),
        far=(0,),
        aliases={1: 0},
        after=(done,),
    )
    parts = scatter_narrow([parts[0], *(later(part, slots) for part in parts[1:])])
    (input_low,) = call("input_chunk", input_chunk_kernel, [chunk_low], (parts[0], grad_one, *parts[1:]),
        scratch=[pltpu.VMEM((CH, D), f32), pltpu.VMEM((CH, D), f32), pltpu.SemaphoreType.DMA((2,))],
        far_in=(0, 1),
    )
    layers = gather_narrow(later(layer, slots))
    whole_out = ((R, T, D), f32)
    (layer_out,) = call("layer_out", spread_kernel, [whole_out], layers)
    (grad_input,) = call("grad_input", spread_kernel, [whole_out], gather_narrow(input_low))
    g_query, g_key, g_value, g_out, grad_up, grad_down, b_up = call(
        "last_sum", last_sum_kernel, [((G, E), f32)] * 4 + [((G, F), f32)] * 2 + [((F,), f32)], (exchange(slots),)
    )
    return (
        layer_out, grad_input, g_query, b_query, g_key, b_key, g_value, b_value, g_out.T, b_out,
        g_one, s_one, grad_up, b_up, grad_down.T, b_down, g_two, s_two,
    )


def solution(mesh):
    tokens, whole = P("dp", "wide", None), P()
    column, vector = P(None, "narrow"), P("narrow")
    rows_split, columns_split = P(("dp", "wide"), "narrow"), P("narrow", ("dp", "wide"))
    in_specs = (
        tokens, P("dp", "wide"), column, vector, column, vector, column, vector, P("narrow", None), whole,
        whole, whole, P("wide", "narrow"), vector, P("narrow", "wide"), whole, whole, whole, tokens,
    )
    out_specs = (
        tokens, tokens, rows_split, vector, rows_split, vector, rows_split, vector, columns_split, whole,
        whole, whole, rows_split, vector, columns_split, whole, whole, whole,
    )
    return jax.shard_map(body, mesh=mesh, in_specs=in_specs, out_specs=out_specs, check_vma=False)
```
